128 devices in a mesh: expert: 32 (over y, x, core), tensor: 4 (over z).
Axes of the slice: x: 4, y: 4, z: 4, core: 2. Of those that a mesh axis runs over, the one named last changes fastest.
Arguments:
- block_input: bfloat16 [4096, 2880], P('expert'), may hold values from -6 to 6
- out_cotangent: bfloat16 [4096, 2880], P('expert'), may hold values from -6 to 6
- seq_lengths: int32 [32, 4], P('expert'), may hold values from 1 to 64, 128 in all within a row
- route_ids: int32 [4096, 4], P('expert'), may hold values from 0 to 31, all different within a row; in each aligned block of 128 rows (0 to 127, 128 to 255, ...) at most 32 rows name the same one
- attn_gain: float32 [2880], replicated, may hold values from 0.5 to 1.5
- w_query: bfloat16 [2880, 4096], P('expert', 'tensor'), may hold values from -0.109375 to 0.109375
- w_key: bfloat16 [2880, 512], P('expert', 'tensor'), may hold values from -0.109375 to 0.109375
- w_value: bfloat16 [2880, 512], P('expert', 'tensor'), may hold values from -0.109375 to 0.109375
- b_query: float32 [4096], P('tensor'), may hold values from -1.2 to 1.2
- b_key: float32 [512], P('tensor'), may hold values from -1.2 to 1.2
- b_value: float32 [512], P('tensor'), may hold values from -1.2 to 1.2
- sink_logits: float32 [64], P('tensor'), may hold values from -4 to 4
- w_output: bfloat16 [4096, 2880], P('tensor', 'expert'), may hold values from -0.25 to 0.25
- b_output: float32 [2880], replicated, may hold values from -1.2 to 1.2
- ffn_gain: float32 [2880], replicated, may hold values from 0.5 to 1.5
- w_router: float32 [2880, 32], replicated, may hold values from -0.0546875 to 0.0546875
- b_router: float32 [32], replicated, may hold values from -3 to 3
- w_gate: bfloat16 [32, 2880, 2880], P('expert', None, 'tensor'), may hold values from -0.109375 to 0.109375
- w_up: bfloat16 [32, 2880, 2880], P('expert', None, 'tensor'), may hold values from -0.109375 to 0.109375
- b_gate: float32 [32, 2880], P('expert', 'tensor'), may hold values from -0.6 to 0.6
- b_up: float32 [32, 2880], P('expert', 'tensor'), may hold values from -0.6 to 0.6
- w_down: bfloat16 [32, 2880, 2880], P('expert', 'tensor'), may hold values from -0.109375 to 0.109375
- b_down: float32 [32, 2880], P('expert'), may hold values from -0.6 to 0.6
Outputs:
- block_output: bfloat16 [4096, 2880], P('expert')
- input_grad: float32 [4096, 2880], P('expert')
- attn_gain_grad: float32 [2880], replicated
- w_query_grad: float32 [2880, 4096], P('expert', 'tensor')
- w_key_grad: float32 [2880, 512], P('expert', 'tensor')
- w_value_grad: float32 [2880, 512], P('expert', 'tensor')
- b_query_grad: float32 [4096], P('tensor')
- b_key_grad: float32 [512], P('tensor')
- b_value_grad: float32 [512], P('tensor')
- sink_grad: float32 [64], P('tensor')
- w_output_grad: float32 [4096, 2880], P('tensor', 'expert')
- b_output_grad: float32 [2880], replicated
- ffn_gain_grad: float32 [2880], replicated
- w_router_grad: float32 [2880, 32], replicated
- b_router_grad: float32 [32], replicated
- w_gate_grad: float32 [32, 2880, 2880], P('expert', None, 'tensor')
- w_up_grad: float32 [32, 2880, 2880], P('expert', None, 'tensor')
- b_gate_grad: float32 [32, 2880], P('expert', 'tensor')
- b_up_grad: float32 [32, 2880], P('expert', 'tensor')
- w_down_grad: float32 [32, 2880, 2880], P('expert', 'tensor')
- b_down_grad: float32 [32, 2880], P('expert')
The draws below stay inside these ranges and needn't reach their ends.
Inputs may be any that keep to these rules, and one draw needn't show every extreme that they name: `seq_lengths`: each row lists in order the lengths of the 4 sequences packed into one device's 128 tokens; they sum to 128 and the longest is exactly 64. `route_ids`: each row names 4 different experts; within the rows of one device no expert is named more than 32 times, and in some device's rows an expert is named exactly 32 times.
All inputs are finite; a program needn't handle non-finite values.
Results may differ from the reference program's by a relative error of at most 0.034.
Values may be sent and summed in bfloat16 or wider, within the bound.
No kernel may reach another device: no remote copies, remote signals or barrier semaphores. Data moves between devices by JAX's collectives and lax.ppermute only.
A program may use at most 256 MiB of HBM per device.

```python
import math
import jax
import jax.numpy as jnp
import numpy as np
from jax import lax

D = 2880
HQ = 64
HK = 8
HD = 64
FF = 2880
TOP = 4
TOK_DEV = 128
SEQS = 4
LONGEST = 64
TOKENS = 4096
EXPERTS = 32
CAP = 32
N_EXPERT = 32


def block_scale(stream_key, shape, shards, smallest, top_value):
    def one(dim, parts):
        heights = jax.random.uniform(jax.random.fold_in(jax.random.fold_in(stream_key, 6), dim), (parts,), jnp.float32, smallest / len(shards), top_value / len(shards))
        return jnp.repeat(jnp.exp(heights), shape[dim] // parts).reshape((-1,) + (1,) * (len(shape) - dim - 1))

    factor_of = one(*shards[0])
    for cut in shards[1:]:
        factor_of = factor_of * one(*cut)
    return factor_of


def split_up(amount, total, reach, slope):
    loads = [(1 << 20) // math.isqrt(rank ** slope) + 1 for rank in range(2, amount + 1)]
    surplus, counts = total - reach - (amount - 1), [1] * (amount - 1)
    while surplus > 0:
        candidates = [i for i in range(amount - 1) if counts[i] < reach]
        pool, left = sum([loads[i] for i in candidates]), surplus
        for i in candidates:
            more = min(reach - counts[i], max(1, left * loads[i] // pool), surplus)
            counts[i] = counts[i] + more
            surplus = surplus - more
    return np.array([reach] + counts)


def ragged(own_key, amount, total, bound, skew):
    if amount == 2:
        one = jax.random.randint(own_key, (), max(1, total - bound), min(bound, total - 1) + 1)
        return jnp.stack([one, total - one])
    tallies = jnp.asarray(split_up(amount, total, bound, skew), jnp.int32)
    pairs = (amount - 1) // 2
    donor, receiver = tallies[1:1 + 2 * pairs:2], tallies[2:2 + 2 * pairs:2]
    room = jnp.minimum(donor - 1, bound - receiver)
    moved = jax.random.randint(jax.random.fold_in(own_key, 1), (pairs,), 0, 1 << 20) % (room + 1)
    tallies = tallies.at[1:1 + 2 * pairs:2].set(donor - moved).at[2:2 + 2 * pairs:2].set(receiver + moved)
    return tallies[jax.random.permutation(jax.random.fold_in(own_key, 2), amount)]


def routed_block(own_key, own, number, rows, amount, top, limit, lean):
    sequence = jax.random.permutation(own_key, amount)
    heavy_load, usual = load_shares(amount, rows * top, limit, lean, True), load_shares(amount, rows * top, limit, lean, False)
    places = jnp.arange(amount)

    def named(sizes, turn):
        used = int((sizes > 0).sum())
        fixed = max(1, used // 4)
        shifted = fixed + (places - fixed + turn * (used - fixed)) % max(1, amount - fixed)
        return jnp.zeros((amount,), jnp.int32).at[sequence[jnp.where(places < fixed, places, shifted)]].set(jnp.asarray(sizes, jnp.int32))

    sizes = jnp.where(number % 4 == 0, named(heavy_load, number // 4), named(usual, number - number // 4 - 1))
    mixed = jax.random.permutation(jax.random.fold_in(own, 3), amount)
    donor, receiver = mixed[0:amount // 2 * 2:2], mixed[1:amount // 2 * 2:2]
    room = jnp.minimum(sizes[donor] - 1, limit - sizes[receiver]) // 2
    room = jnp.where((donor == sequence[0]) | (receiver == sequence[0]) | (sizes[receiver] == 0), 0, jnp.maximum(room, 0))
    shifted = jax.random.randint(jax.random.fold_in(own, 4), (amount // 2,), 0, 1 << 20) % (room + 1)
    sizes = sizes.at[donor].add(-shifted).at[receiver].add(shifted)
    members = jnp.searchsorted(jnp.cumsum(sizes), jnp.arange(rows * top), side="right").astype(jnp.int32)
    table = members.reshape(top, rows).T
    table = table[jax.random.permutation(jax.random.fold_in(own, 1), rows)]
    turn = jax.random.randint(jax.random.fold_in(own, 2), (rows, 1), 0, top)
    return jnp.take_along_axis(table, (jnp.arange(top)[None, :] + turn) % top, axis=1)


def load_shares(amount, total, limit, slope, full):
    loads = [(1 << 20) // math.isqrt(grade ** slope) + 1 for grade in range(1, amount + 1)]
    largest = limit if full else min(limit, max(-(-total // amount), total * loads[0] // sum(loads)))
    least = 1 if total - largest >= amount - 1 else 0
    holding, spare = [largest] + [least] * (amount - 1), total - largest - least * (amount - 1)
    while spare > 0:
        candidates = [i for i in range(1, amount) if holding[i] < largest] or [i for i in range(1, amount) if holding[i] < limit]
        mass, left = sum([loads[i] for i in candidates]), spare
        for i in candidates:
            extra = min(limit - holding[i], max(1, left * loads[i] // mass), spare)
            holding[i] = holding[i] + extra
            spare = spare - extra
    return np.array(holding)


def normal_values(rng, extent, width, bound, cuts=(), kind=jnp.bfloat16):
    loudness = block_scale(rng, extent, cuts, -0.22, 0.18) if cuts else 1.0
    drawn = jax.random.normal(rng, extent, jnp.float32) * width * loudness
    return jnp.minimum(jnp.maximum(drawn, -bound), bound).astype(kind)


def setup_inputs(seed: int = 0) -> dict:
    seeds = jax.random.split(jax.random.key(seed), 24)
    block_input = normal_values(seeds[0], (TOKENS, D), 1.0, 6.0, ((0, 32),))
    out_cotangent = normal_values(seeds[1], (TOKENS, D), 1.0, 6.0, ((0, 32),))
    seq_lengths = jax.vmap(lambda own: ragged(own, SEQS, TOK_DEV, LONGEST, 2))(jax.random.split(seeds[2], N_EXPERT)).reshape((N_EXPERT, SEQS)).astype(jnp.int32)
    route_ids_keys = jax.random.split(jax.random.fold_in(seeds[3], 1), TOKENS // TOK_DEV)
    route_ids_turns = jax.random.permutation(jax.random.fold_in(seeds[3], 3), TOKENS // TOK_DEV)
    route_ids = jax.vmap(lambda own, number: routed_block(jax.random.fold_in(seeds[3], 2), own, number, TOK_DEV, EXPERTS, TOP, CAP, 2))(route_ids_keys, route_ids_turns).reshape((TOKENS, TOP))
    attn_gain = jnp.clip(1.0 + 0.1 * jax.random.normal(seeds[4], (D,), jnp.float32), 0.5, 1.5)
    w_query = normal_values(seeds[5], (D, HQ * HD), D ** -0.5, 0.109375, ((0, 32), (1, 4)))
    w_key = normal_values(seeds[6], (D, HK * HD), D ** -0.5, 0.109375, ((0, 32), (1, 4)))
    w_value = normal_values(seeds[7], (D, HK * HD), D ** -0.5, 0.109375, ((0, 32), (1, 4)))
    b_query = normal_values(seeds[8], (HQ * HD,), 0.2, 1.2, ((0, 4),), jnp.float32)
    b_key = normal_values(seeds[9], (HK * HD,), 0.2, 1.2, ((0, 4),), jnp.float32)
    b_value = normal_values(seeds[10], (HK * HD,), 0.2, 1.2, ((0, 4),), jnp.float32)
    sink_logits = normal_values(seeds[11], (HQ,), 1.0, 4.0, ((0, 4),), jnp.float32)
    w_output = normal_values(seeds[12], (HQ * HD, D), (HQ * HD // 8) ** -0.5, 0.25, ((0, 4), (1, 32)))
    b_output = normal_values(seeds[13], (D,), 0.2, 1.2, (), jnp.float32)
    ffn_gain = jnp.clip(1.0 + 0.1 * jax.random.normal(seeds[14], (D,), jnp.float32), 0.5, 1.5)
    w_router = normal_values(seeds[15], (D, EXPERTS), (4 * D) ** -0.5, 0.0546875, (), jnp.float32)
    b_router = normal_values(seeds[16], (EXPERTS,), 0.5, 3.0, (), jnp.float32)
    w_gate = normal_values(seeds[17], (EXPERTS, D, FF), D ** -0.5, 0.109375, ((0, 32), (2, 4)))
    w_up = normal_values(seeds[18], (EXPERTS, D, FF), D ** -0.5, 0.109375, ((0, 32), (2, 4)))
    b_gate = normal_values(seeds[19], (EXPERTS, FF), 0.1, 0.6, ((0, 32), (1, 4)), jnp.float32)
    b_up = normal_values(seeds[20], (EXPERTS, FF), 0.1, 0.6, ((0, 32), (1, 4)), jnp.float32)
    w_down = normal_values(seeds[21], (EXPERTS, FF, D), FF ** -0.5, 0.109375, ((0, 32), (1, 4)))
    b_down = normal_values(seeds[22], (EXPERTS, D), 0.1, 0.6, ((0, 32),), jnp.float32)
    return dict(block_input=block_input, out_cotangent=out_cotangent, seq_lengths=seq_lengths, route_ids=route_ids, attn_gain=attn_gain, w_query=w_query, w_key=w_key, w_value=w_value, b_query=b_query, b_key=b_key, b_value=b_value, sink_logits=sink_logits, w_output=w_output, b_output=b_output, ffn_gain=ffn_gain, w_router=w_router, b_router=b_router, w_gate=w_gate, w_up=w_up, b_gate=b_gate, b_up=b_up, w_down=w_down, b_down=b_down)


EPSILON = 1e-05
ROPE_BASE = 150000.0
CLAMP_LIMIT = 7.0
GLU_SLOPE = 1.702
MASKED = -1e+30
PRECISE = lax.Precision.HIGHEST

@jax.custom_vjp
def low(v):
    return lax.optimization_barrier(v.astype(jnp.bfloat16)).astype(jnp.float32)

@jax.custom_vjp
def low_back(v):
    return v

def low_keep(v):
    return (low(v), None)

def low_pass(kept, grad):
    return (grad,)

def back_keep(v):
    return (v, None)

def back_low(kept, grad):
    return (low(grad),)
low.defvjp(low_keep, low_pass)
low_back.defvjp(back_keep, back_low)

def rms_norm(values, gain_vec):
    return values * lax.rsqrt(lax.optimization_barrier(jnp.mean(values * values, axis=-1, keepdims=True)) + EPSILON) * gain_vec

def matmul(left_mat, right_mat):
    return jnp.dot(left_mat, right_mat, precision=PRECISE)

def layout(lengths, tok_count):
    seq_ends = jnp.cumsum(lengths).astype(jnp.int32)
    tok_index = jnp.arange(tok_count, dtype=jnp.int32)
    is_past = tok_index[:, None] >= seq_ends[None, :]
    segment = lax.optimization_barrier(jnp.sum(is_past.astype(jnp.int32), axis=1)).astype(jnp.int32)
    offset = lax.optimization_barrier(jnp.sum(jnp.where(is_past, lengths[None, :], 0), axis=1)).astype(jnp.int32)
    return (segment, (tok_index - offset).astype(jnp.int32))

def rotation(position, head_size):
    half_size = head_size // 2
    frequency = ROPE_BASE ** (-(jnp.arange(half_size).astype(jnp.float32) * 2.0 / head_size))
    angles = position.astype(jnp.float32)[:, None] * frequency[None, :]
    return (jnp.cos(angles), jnp.sin(angles))

def rotate(values, cosine, sine_table):
    half_size = values.shape[-1] // 2
    first = values[..., :half_size]
    second = values[..., half_size:]
    cos_cols = cosine[:, None, :]
    sin_cols = sine_table[:, None, :]
    return jnp.concatenate([first * cos_cols - second * sin_cols, second * cos_cols + first * sin_cols], axis=-1)

def activate(gate_lin, up_lin):
    gate_soft = CLAMP_LIMIT * jnp.tanh(gate_lin / CLAMP_LIMIT)
    up_soft = CLAMP_LIMIT * jnp.tanh(up_lin / CLAMP_LIMIT)
    return (up_soft + 1.0) * gate_soft * jax.nn.sigmoid(GLU_SLOPE * gate_soft)

def attend(queries, key_rows, value_rows, sink_table, segment, position):
    score_scale = queries.shape[-1] ** (-0.5)
    scores = low_back(jnp.einsum('qhgd,khd->hgqk', queries, key_rows, precision=PRECISE) * score_scale)
    allowed = (segment[:, None] == segment[None, :]) & (position[None, :] <= position[:, None])
    scores = jnp.where(allowed, scores, MASKED)
    sink_col = sink_table[:, :, None]
    row_max = jnp.maximum(lax.optimization_barrier(jnp.max(scores, axis=-1)), sink_col)
    weights = jnp.exp(scores - row_max[..., None])
    denom_sum = lax.optimization_barrier(jnp.sum(weights, axis=-1)) + jnp.exp(sink_col - row_max)
    probability = low(weights / denom_sum[..., None])
    return jnp.einsum('hgqk,khd->qhgd', probability, value_rows, precision=PRECISE)

def reference(block_input, out_cotangent, seq_lengths, route_ids, attn_gain, w_query, w_key, w_value, b_query, b_key, b_value, sink_logits, w_output, b_output, ffn_gain, w_router, b_router, w_gate, w_up, b_gate, b_up, w_down, b_down):
    group_size = HQ // HK
    segment, position = jax.vmap(lambda len_row: layout(len_row, TOK_DEV))(seq_lengths)
    cosine, sine_table = rotation(position.reshape(-1), HD)
    flat_ids = route_ids.reshape(-1)
    onehot = (route_ids[:, :, None] == jnp.arange(EXPERTS, dtype=jnp.int32)[None, None, :]).astype(jnp.float32)
    slot_count = N_EXPERT * CAP

    def pick_rows(expert):
        chosen_mask = flat_ids == expert
        picked = jnp.nonzero(chosen_mask, size=slot_count, fill_value=0)[0].astype(jnp.int32)
        live_mask = (jnp.arange(slot_count) < jnp.sum(chosen_mask.astype(jnp.int32))).astype(jnp.float32)
        return (picked, live_mask)
    picked_rows, live_rows = lax.map(pick_rows, jnp.arange(EXPERTS, dtype=jnp.int32))

    def forward(inputs, gain_one, wq_full, wk_full, wv_full, bq_vec, bk_vec, bv_vec, sinks, wo_full, bo_vec, gain_two, wr_full, br_vec, wg_all, wu_all, bg_all, bu_all, wd_all, bd_all):
        normed_low = low(rms_norm(inputs, gain_one))
        query_lin = low_back(matmul(normed_low, wq_full) + bq_vec)
        key_lin = low_back(matmul(normed_low, wk_full) + bk_vec)
        value_rows = low(low_back(matmul(normed_low, wv_full) + bv_vec)).reshape(N_EXPERT, TOK_DEV, HK, HD)
        queries = low(rotate(query_lin.reshape(TOKENS, HQ, HD), cosine, sine_table)).reshape(N_EXPERT, TOK_DEV, HK, group_size, HD)
        key_rows = low(rotate(key_lin.reshape(TOKENS, HK, HD), cosine, sine_table)).reshape(N_EXPERT, TOK_DEV, HK, HD)
        sink_table = sinks.reshape(HK, group_size)

        def one_device(item_tuple):
            return attend(item_tuple[0], item_tuple[1], item_tuple[2], sink_table, item_tuple[3], item_tuple[4])
        attended = lax.map(jax.checkpoint(one_device), (queries, key_rows, value_rows, segment, position))
        attn_low = low(low_back(attended.reshape(TOKENS, HQ * HD)))
        residual = inputs + low_back(matmul(attn_low, wo_full)) + bo_vec
        normed_two = rms_norm(residual, gain_two)
        ffn_low = low(normed_two)
        logits = matmul(normed_two, wr_full) + br_vec
        chosen = lax.optimization_barrier(jnp.sum(logits[:, None, :] * onehot, axis=-1))
        gate_probs = jax.nn.softmax(chosen, axis=-1)

        def expert_step(mixed_out, item_tuple):
            picked, live_mask, wg_one, wu_one, bg_one, bu_one, wd_one, bd_one = item_tuple
            token_idx = picked // TOP
            route_idx = picked % TOP
            row_vals = low_back(ffn_low[token_idx])
            gate_lin = low_back(matmul(row_vals, wg_one) + bg_one)
            up_lin = low_back(matmul(row_vals, wu_one) + bu_one)
            hidden = low(activate(gate_lin, up_lin))
            result = low(low_back(matmul(hidden, wd_one) + bd_one))
            weight = gate_probs[token_idx, route_idx] * live_mask
            return (mixed_out.at[token_idx].add(weight[:, None] * result), None)
        mixed_out, unused = lax.scan(jax.checkpoint(expert_step), jnp.zeros((TOKENS, D), jnp.float32), (picked_rows, live_rows, wg_all, wu_all, bg_all, bu_all, wd_all, bd_all))
        return residual + mixed_out
    floats = tuple((item.astype(jnp.float32) for item in (block_input, attn_gain, w_query, w_key, w_value, b_query, b_key, b_value, sink_logits, w_output, b_output, ffn_gain, w_router, b_router, w_gate, w_up, b_gate, b_up, w_down, b_down)))
    output, pullback = jax.vjp(forward, *floats)
    gradients = pullback(out_cotangent.astype(jnp.float32))
    return (output.astype(jnp.bfloat16), gradients[0], gradients[1], gradients[2], gradients[3], gradients[4], gradients[5], gradients[6], gradients[7], gradients[8], gradients[9], gradients[10], gradients[11], gradients[12], gradients[13], gradients[14], gradients[15], gradients[16], gradients[17], gradients[18], gradients[19])
```

```python
import functools

import jax
import jax.numpy as jnp
from jax import lax
from jax.experimental import pallas as pl
from jax.experimental.pallas import tpu as pltpu
from jax.sharding import PartitionSpec as P

HD = 64
PAIR = 2 * HD
EPSILON = 1e-05
ROPE_BASE = 150000.0
CLAMP_LIMIT = 7.0
GLU_SLOPE = 1.702
MASKED = -1e30
PRECISE = lax.Precision.HIGHEST
LOW = jnp.bfloat16
F32 = jnp.float32
VMEM_BYTES = 56 * 1024 * 1024
NN = (((1,), (0,)), ((), ()))
NT = (((1,), (1,)), ((), ()))
TN = (((0,), (0,)), ((), ()))


def round_up(value, unit):
    return -(-value // unit) * unit


def dot(left, right, dims=NN):
    return lax.dot_general(left, right, dims, preferred_element_type=F32)


def split_low(values):
    high = values.astype(LOW)
    return high, (values - high.astype(F32)).astype(LOW)


def layout(lengths, tok_count):
    seq_ends = jnp.cumsum(lengths)
    tok_index = jnp.arange(tok_count, dtype=jnp.int32)
    is_past = tok_index[:, None] >= seq_ends[None, :]
    segment = jnp.sum(is_past.astype(jnp.int32), axis=1)
    offset = jnp.sum(jnp.where(is_past, lengths[None, :], 0), axis=1)
    return (segment, tok_index - offset)


def rope_tables(position):
    half = HD // 2
    frequency = ROPE_BASE ** (-(jnp.arange(half).astype(F32) * 2.0 / HD))
    angles = position.astype(F32)[:, None] * frequency[None, :]
    cosine, sine = jnp.cos(angles), jnp.sin(angles)
    return (
        jnp.concatenate([cosine] * 4, axis=1),
        jnp.concatenate([-sine, sine, -sine, sine], axis=1),
    )


def lane_index(shape):
    return lax.broadcasted_iota(jnp.int32, shape, len(shape) - 1)


def swap_halves(values):
    first = (lane_index(values.shape) % HD) < HD // 2
    return jnp.where(
        first, pltpu.roll(values, PAIR - HD // 2, 1), pltpu.roll(values, HD // 2, 1)
    )


def twin(values, which):
    turned = pltpu.roll(values, HD, 1)
    left = lane_index(values.shape) < HD
    return jnp.where(left, values, turned) if which == 0 else jnp.where(left, turned, values)


def attend_forward_kernel(
    sink_ref, qkv_ref, cos_ref, sin_ref, allowed_ref, out_ref, rot_ref, lse_ref
):
    tokens = qkv_ref.shape[0]
    heads = sink_ref.shape[0]
    key_at = heads * HD
    value_at = key_at + PAIR
    per_group = heads // 2
    cos, sin = cos_ref[...], sin_ref[...]
    allowed = allowed_ref[...] > 0.5
    left = lane_index((tokens, PAIR)) < HD
    lanes = lane_index((tokens, PAIR))

    def rope(values):
        return values * cos + swap_halves(values) * sin

    key = rope(qkv_ref[:, key_at:value_at])
    value = qkv_ref[:, value_at : value_at + PAIR]
    rot_ref[:, key_at:value_at] = key.astype(LOW)
    rot_ref[:, value_at : value_at + PAIR] = value.astype(LOW)
    keys = [twin(key, g).astype(LOW) for g in range(2)]
    values = [twin(value, g).astype(LOW) for g in range(2)]
    lse_all = jnp.zeros((tokens, PAIR), F32)
    for pair in range(heads // 2):
        cols = slice(pair * PAIR, (pair + 1) * PAIR)
        group = (2 * pair) // per_group
        query = rope(qkv_ref[:, cols])
        rot_ref[:, cols] = query.astype(LOW)
        outs = []
        for side in range(2):
            head = 2 * pair + side
            mine = left if side == 0 else jnp.logical_not(left)
            one = jnp.where(mine, query, 0.0).astype(LOW)
            scores = dot(one, keys[group], NT) * HD ** (-0.5)
            scores = jnp.where(allowed, scores, MASKED)
            sink = sink_ref[head]
            top = jnp.maximum(jnp.max(scores, axis=1, keepdims=True), sink)
            weights = jnp.exp(scores - top)
            denom = jnp.sum(weights, axis=1, keepdims=True) + jnp.exp(sink - top)
            lse = top + jnp.log(denom)
            lse_all = jnp.where(lanes == head, lse, lse_all)
            prob = (weights / denom).astype(LOW)
            outs.append(dot(prob, values[group]))
        out_ref[:, cols] = jnp.where(left, outs[0], outs[1]).astype(LOW)
    lse_ref[...] = lse_all


def attend_backward_kernel(
    sink_ref, rot_ref, grad_ref, lse_ref, cos_ref, sin_ref, allowed_ref, out_ref, sink_out_ref
):
    tokens = rot_ref.shape[0]
    heads = sink_ref.shape[0]
    key_at = heads * HD
    value_at = key_at + PAIR
    per_group = heads // 2
    scale = HD ** (-0.5)
    cos, sin = cos_ref[...], sin_ref[...]
    allowed = allowed_ref[...] > 0.5
    lanes = lane_index((tokens, PAIR))
    left = lanes < HD

    def turn_back(values):
        return values * cos - swap_halves(values) * sin

    key = rot_ref[:, key_at:value_at].astype(F32)
    value = rot_ref[:, value_at : value_at + PAIR].astype(F32)
    keys = [twin(key, g).astype(LOW) for g in range(2)]
    values = [twin(value, g).astype(LOW) for g in range(2)]
    key_sums = [jnp.zeros((tokens, PAIR), F32) for _ in range(2)]
    value_sums = [jnp.zeros((tokens, PAIR), F32) for _ in range(2)]
    sink_all = jnp.zeros((tokens, PAIR), F32)
    lse_all = lse_ref[...]
    for pair in range(heads // 2):
        cols = slice(pair * PAIR, (pair + 1) * PAIR)
        group = (2 * pair) // per_group
        query = rot_ref[:, cols].astype(F32)
        grad = grad_ref[:, cols].astype(F32)
        outs = []
        for side in range(2):
            head = 2 * pair + side
            mine = left if side == 0 else jnp.logical_not(left)
            one = jnp.where(mine, query, 0.0).astype(LOW)
            grad_one = jnp.where(mine, grad, 0.0).astype(LOW)
            lse = jnp.sum(jnp.where(lanes == head, lse_all, 0.0), axis=1, keepdims=True)
            scores = dot(one, keys[group], NT) * scale
            prob = jnp.where(allowed, jnp.exp(jnp.where(allowed, scores - lse, 0.0)), 0.0)
            grad_prob = dot(grad_one, values[group], NT)
            delta = jnp.sum(prob * grad_prob, axis=1, keepdims=True)
            grad_score = (prob * (grad_prob - delta)).astype(LOW)
            outs.append(dot(grad_score, keys[group]))
            key_sums[group] += dot(grad_score, one, TN)
            value_sums[group] += dot(prob.astype(LOW), grad_one, TN)
            sink_all = jnp.where(lanes == head, jnp.exp(sink_ref[head] - lse) * delta, sink_all)
        out_ref[:, cols] = turn_back(jnp.where(left, outs[0], outs[1]) * scale).astype(LOW)

    def fold(sums):
        both = [one + pltpu.roll(one, HD, 1) for one in sums]
        return jnp.where(left, both[0], both[1])

    out_ref[:, key_at:value_at] = turn_back(fold(key_sums) * scale).astype(LOW)
    out_ref[:, value_at : value_at + PAIR] = fold(value_sums).astype(LOW)
    sink_out_ref[...] = -jnp.sum(sink_all, axis=0, keepdims=True)


def kernel_params():
    return pltpu.CompilerParams(vmem_limit_bytes=VMEM_BYTES)


IN_VMEM = pl.BlockSpec(memory_space=pltpu.VMEM)
IN_SMEM = pl.BlockSpec(memory_space=pltpu.SMEM)


def attend_forward(sinks, qkv, cos, sin, allowed):
    tokens, width = qkv.shape
    heads = sinks.shape[0]
    return pl.pallas_call(
        attend_forward_kernel,
        out_shape=(
            jax.ShapeDtypeStruct((tokens, heads * HD), LOW),
            jax.ShapeDtypeStruct((tokens, width), LOW),
            jax.ShapeDtypeStruct((tokens, PAIR), F32),
        ),
        in_specs=[IN_SMEM] + [IN_VMEM] * 4,
        out_specs=(IN_VMEM,) * 3,
        compiler_params=kernel_params(),
        name="attend_forward",
    )(sinks, qkv, cos, sin, allowed)


def attend_backward(sinks, rotated, grad, lse, cos, sin, allowed):
    tokens, width = rotated.shape
    return pl.pallas_call(
        attend_backward_kernel,
        out_shape=(
            jax.ShapeDtypeStruct((tokens, width), LOW),
            jax.ShapeDtypeStruct((1, PAIR), F32),
        ),
        in_specs=[IN_SMEM] + [IN_VMEM] * 6,
        out_specs=(IN_VMEM,) * 2,
        compiler_params=kernel_params(),
        name="attend_backward",
    )(sinks, rotated, grad, lse, cos, sin, allowed)


def grad_hidden_kernel(rows_ref, down_ref, bias_ref, out_ref):
    rows = rows_ref[...]
    hidden = down_ref.shape[0]
    spare = out_ref.shape[1] - hidden
    out_ref[:, :hidden] = dot(rows, down_ref[...], NT)
    with_bias = jnp.sum(rows.astype(F32) * bias_ref[...], axis=1, keepdims=True)
    out_ref[:, hidden:] = jnp.broadcast_to(with_bias, (rows.shape[0], spare))


def grad_hidden_product(rows, down, bias):
    count, features = rows.shape
    hidden = down.shape[0]
    width = round_up(hidden + 1, 128)
    block = count // 4
    return pl.pallas_call(
        grad_hidden_kernel,
        grid=(count // block,),
        out_shape=jax.ShapeDtypeStruct((count, width), F32),
        in_specs=[
            pl.BlockSpec((block, features), lambda i: (i, 0)),
            pl.BlockSpec((hidden, features), lambda i: (0, 0)),
            pl.BlockSpec((1, features), lambda i: (0, 0)),
        ],
        out_specs=pl.BlockSpec((block, width), lambda i: (i, 0)),
        compiler_params=kernel_params(),
        cost_estimate=pl.CostEstimate(
            flops=2 * count * features * hidden,
            bytes_accessed=2 * count * features + 2 * features * hidden + 4 * count * width,
            transcendentals=0,
        ),
        name="grad_hidden",
    )(rows, down, bias)


def expert_kernel(
    features,
    experts,
    rows_ref,
    first_ref,
    gate_ref,
    up_ref,
    gate_bias_ref,
    up_bias_ref,
    mine_ref,
    grad_rows_ref,
    act_ref,
    act_gated_ref,
    grad_gate_ref,
    grad_up_ref,
    bias_sums_ref,
):
    hidden = gate_ref.shape[0]
    rows = rows_ref[:, :features]
    mine = mine_ref[...]
    gate = jnp.sum(rows_ref[:, features:].astype(F32) * mine, axis=1, keepdims=True)
    gate_lin = dot(rows, gate_ref[...], NT) + gate_bias_ref[...]
    up_lin = dot(rows, up_ref[...], NT) + up_bias_ref[...]
    gate_tanh = jnp.tanh(gate_lin * (1.0 / CLAMP_LIMIT))
    up_tanh = jnp.tanh(up_lin * (1.0 / CLAMP_LIMIT))
    gate_soft = CLAMP_LIMIT * gate_tanh
    up_one = CLAMP_LIMIT * up_tanh + 1.0
    sigmoid = 1.0 / (1.0 + jnp.exp(-GLU_SLOPE * gate_soft))
    swish = gate_soft * sigmoid
    act = (up_one * swish).astype(LOW)
    act_ref[...] = act
    act_gated_ref[...] = (act.astype(F32) * gate).astype(LOW)
    first = first_ref[:, :hidden]
    with_bias = jnp.max(first_ref[:, hidden:], axis=1, keepdims=True)
    grad_weight = jnp.sum(act.astype(F32) * first, axis=1, keepdims=True) + with_bias
    grad_act = first * gate
    swish_slope = sigmoid + GLU_SLOPE * swish * (1.0 - sigmoid)
    grad_gate = (grad_act * up_one * swish_slope * (1.0 - gate_tanh * gate_tanh)).astype(LOW)
    grad_up = (grad_act * swish * (1.0 - up_tanh * up_tanh)).astype(LOW)
    grad_gate_ref[...] = grad_gate
    grad_up_ref[...] = grad_up
    grad_rows = dot(grad_gate, gate_ref[...]) + dot(grad_up, up_ref[...])
    grad_rows_ref[:, :features] = grad_rows.astype(LOW)
    high = grad_weight.astype(LOW).astype(F32)
    lanes = lane_index(mine.shape)
    spread = jnp.where(lanes < experts, high, grad_weight - high) * mine
    grad_rows_ref[:, features:] = spread.astype(LOW)
    sums = jnp.concatenate(
        [
            jnp.sum(grad_gate.astype(F32), axis=0, keepdims=True),
            jnp.sum(grad_up.astype(F32), axis=0, keepdims=True),
        ],
        axis=0,
    )
    is_first = pl.program_id(0) == 0
    bias_sums_ref[...] = jnp.where(is_first, 0.0, bias_sums_ref[...]) + sums


def expert_step(rows, first, gate, up, gate_bias, up_bias, mine, features, experts):
    count, width = rows.shape
    hidden = gate.shape[0]
    first_width = first.shape[1]
    block = count // 4

    def by_row(columns):
        return pl.BlockSpec((block, columns), lambda i: (i, 0))

    def whole(shape):
        return pl.BlockSpec(shape, lambda i: (0, 0))

    return pl.pallas_call(
        functools.partial(expert_kernel, features, experts),
        grid=(count // block,),
        out_shape=(
            jax.ShapeDtypeStruct((count, width), LOW),
            jax.ShapeDtypeStruct((count, hidden), LOW),
            jax.ShapeDtypeStruct((count, hidden), LOW),
            jax.ShapeDtypeStruct((count, hidden), LOW),
            jax.ShapeDtypeStruct((count, hidden), LOW),
            jax.ShapeDtypeStruct((2, hidden), F32),
        ),
        in_specs=[
            by_row(width),
            by_row(first_width),
            whole((hidden, features)),
            whole((hidden, features)),
            whole((1, hidden)),
            whole((1, hidden)),
            whole((1, width - features)),
        ],
        out_specs=(
            by_row(width),
            by_row(hidden),
            by_row(hidden),
            by_row(hidden),
            by_row(hidden),
            whole((2, hidden)),
        ),
        compiler_params=kernel_params(),
        cost_estimate=pl.CostEstimate(
            flops=8 * count * features * hidden,
            bytes_accessed=4 * count * width + 4 * features * hidden + 12 * count * hidden,
            transcendentals=3 * count * hidden,
        ),
        name="expert_step",
    )(rows, first, gate, up, gate_bias, up_bias, mine)


def exchange(rows, parts):
    count, width = rows.shape
    moved = lax.all_to_all(
        rows.reshape(parts, count // parts, width),
        "expert",
        split_axis=0,
        concat_axis=0,
        tiled=True,
    )
    return moved.reshape(count, width)


def tensor_sum(values, ring, to_low=lambda v: v.astype(LOW)):
    near = [(i, i ^ 1) for i in range(ring)]
    far = [(i, ring - 1 - i) for i in range(ring)]
    half = values.shape[0] // 2
    upper, lower = to_low(values[:half]), to_low(values[half:])
    upper_in = lax.ppermute(upper, "tensor", near)
    lower_in = lax.ppermute(lower, "tensor", far)
    upper = to_low(upper.astype(F32) + upper_in.astype(F32))
    lower = to_low(lower.astype(F32) + lower_in.astype(F32))
    upper_in = lax.ppermute(upper, "tensor", far)
    lower_in = lax.ppermute(lower, "tensor", near)
    return jnp.concatenate(
        [upper.astype(F32) + upper_in.astype(F32), lower.astype(F32) + lower_in.astype(F32)],
        axis=0,
    )


def on_device(
    expert_axis,
    tensor_axis,
    block_input,
    out_cotangent,
    seq_lengths,
    route_ids,
    attn_gain,
    w_query,
    w_key,
    w_value,
    b_query,
    b_key,
    b_value,
    sink_logits,
    w_output,
    b_output,
    ffn_gain,
    w_router,
    b_router,
    w_gate,
    w_up,
    b_gate,
    b_up,
    w_down,
    b_down,
):
    tokens, features = block_input.shape
    heads = sink_logits.shape[0]
    experts = w_router.shape[1]
    capacity = 2 * tokens * route_ids.shape[1] // experts
    slots = experts * capacity
    shard = w_query.shape[0]
    shard_pad = round_up(shard + 1, 16)
    qkv_width = w_query.shape[1] + w_key.shape[1] + w_value.shape[1]
    width = round_up(features + 2 * experts, 128)
    mine_expert = lax.axis_index("expert")
    mine_tensor = lax.axis_index("tensor")

    packed = jnp.concatenate([w_query, w_key, w_value, w_output.T], axis=1)
    packed = jnp.pad(packed, ((0, shard_pad - shard), (0, 0)))
    weights = lax.all_gather(packed, "expert", axis=0, tiled=True)

    expert_ids = jnp.arange(experts, dtype=jnp.int32)
    named = jnp.any(route_ids[:, :, None] == expert_ids[None, None, :], axis=1)
    named_t = jnp.any(route_ids.T[:, None, :] == expert_ids[None, :, None], axis=0)
    token_ids = jnp.arange(tokens, dtype=jnp.int32)
    earlier = (token_ids[:, None] < token_ids[None, :]).astype(LOW)
    rank_t = dot(named_t.astype(LOW), earlier).astype(jnp.int32)
    place = (rank_t[:, None, :] == jnp.arange(capacity, dtype=jnp.int32)[None, :, None]) & named_t[
        :, None, :
    ]
    place = place.astype(LOW).reshape(slots, tokens)

    grad_rows_in = exchange(dot(place, out_cotangent).astype(LOW), experts)

    segment, position = layout(seq_lengths[0], tokens)
    cos, sin = rope_tables(position)
    allowed = (segment[:, None] == segment[None, :]) & (token_ids[None, :] <= token_ids[:, None])
    allowed = allowed.astype(F32)

    inputs = block_input.astype(F32)
    scale_one = lax.rsqrt(jnp.mean(inputs * inputs, axis=-1, keepdims=True) + EPSILON)
    unit_one = inputs * scale_one
    normed_low = (unit_one * attn_gain).astype(LOW)
    spread_low = jnp.pad(
        normed_low.reshape(tokens, expert_axis, shard), ((0, 0), (0, 0), (0, shard_pad - shard))
    )
    one_column = (jnp.arange(shard_pad) == shard).astype(LOW)
    sent_low = jnp.transpose(spread_low + one_column, (1, 0, 2))
    normed_all = exchange(sent_low.reshape(expert_axis * tokens, shard_pad), expert_axis)

    bias = jnp.concatenate([b_query, b_key, b_value])
    qkv = dot(spread_low.reshape(tokens, expert_axis * shard_pad), weights[:, :qkv_width]) + bias
    attn_low, rotated, lse = attend_forward(sink_logits, qkv, cos, sin, allowed)
    attn_all = lax.all_gather(attn_low, "expert", axis=0, tiled=True)

    def compact(padded):
        return padded.reshape(padded.shape[0], expert_axis, shard_pad)[:, :, :shard].reshape(
            padded.shape[0], features
        )

    attn_part = compact(dot(attn_low, weights[:, qkv_width:], NT))
    residual = inputs + tensor_sum(attn_part, tensor_axis) + b_output
    scale_two = lax.rsqrt(jnp.mean(residual * residual, axis=-1, keepdims=True) + EPSILON)
    unit_two = residual * scale_two
    normed_two = unit_two * ffn_gain
    logits = jnp.dot(normed_two, w_router, precision=PRECISE) + b_router
    gates = jax.nn.softmax(jnp.where(named, logits, MASKED), axis=-1)
    gates = jnp.where(named, gates, 0.0)

    gates_high, gates_low = split_low(gates)
    spare = width - features - 2 * experts
    sent = jnp.concatenate(
        [normed_two.astype(LOW), gates_high, gates_low, jnp.zeros((tokens, spare), LOW)], axis=1
    )
    rows_in = exchange(dot(place, sent).astype(LOW), experts)

    gate_t, up_t, down = w_gate[0].T, w_up[0].T, w_down[0]
    bias_once = jnp.where(mine_tensor == 0, b_down, 0.0)
    first = grad_hidden_product(grad_rows_in, down, bias_once)
    lane = jnp.arange(width - features)
    mine = ((lane % experts == mine_expert) & (lane < 2 * experts)).astype(F32)[None, :]
    grad_rows, act, act_gated, grad_gate, grad_up, bias_sums = expert_step(
        rows_in, first, gate_t, up_t, b_gate, b_up, mine, features, experts
    )
    grad_back = exchange(grad_rows, experts)

    result = (dot(act, down) + bias_once).astype(LOW)
    returned = exchange(result, experts)

    gate_column = jnp.sum(rows_in[:, features:].astype(F32) * mine, axis=1)
    w_down_grad = dot(act_gated, grad_rows_in, TN)[None]
    b_down_grad = dot(gate_column.astype(LOW)[None, :], grad_rows_in)
    w_gate_grad = dot(grad_gate, rows_in[:, :features], TN).T[None]
    w_up_grad = dot(grad_up, rows_in[:, :features], TN).T[None]
    b_gate_grad = bias_sums[0:1]
    b_up_grad = bias_sums[1:2]

    def resplit(values):
        main, spread = values[:, :features], values[:, features:]
        weight = spread[:, :experts] + spread[:, experts : 2 * experts]
        high, low = split_low(weight)
        return jnp.concatenate([main.astype(LOW), high, low], axis=1)

    back = tensor_sum(dot(place, grad_back, TN)[:, : features + 2 * experts], tensor_axis, resplit)
    grad_gates = back[:, features : features + experts] + back[:, features + experts :]
    grad_logits = gates * (grad_gates - jnp.sum(gates * grad_gates, axis=-1, keepdims=True))
    grad_two = back[:, :features] + jnp.dot(grad_logits, w_router.T, precision=PRECISE)
    cotangent = out_cotangent.astype(F32)
    scaled_two = grad_two * ffn_gain
    grad_resid = cotangent + scale_two * (
        scaled_two - unit_two * jnp.mean(unit_two * scaled_two, axis=-1, keepdims=True)
    )
    ffn_gain_part = jnp.sum(grad_two * unit_two, axis=0)
    router_part = jnp.dot(grad_logits.T, normed_two, precision=PRECISE)
    router_bias_part = jnp.sum(grad_logits, axis=0)
    output_bias_part = jnp.sum(grad_resid, axis=0)
    resid_low = grad_resid.astype(LOW)

    whole = weights.reshape(expert_axis, shard_pad, weights.shape[1])[:, :shard].reshape(
        features, weights.shape[1]
    )
    grad_attn = dot(resid_low, whole[:, qkv_width:]).astype(LOW)
    grad_qkv, sink_part = attend_backward(
        sink_logits, rotated, grad_attn, lse, cos, sin, allowed
    )
    grad_qkv_all = lax.all_gather(grad_qkv, "expert", axis=0, tiled=True)

    sent_resid = jnp.pad(
        resid_low.reshape(tokens, expert_axis, shard), ((0, 0), (0, 0), (0, shard_pad - shard))
    )
    sent_resid = jnp.transpose(sent_resid, (1, 0, 2)).reshape(expert_axis * tokens, shard_pad)
    resid_all = exchange(sent_resid, expert_axis)
    w_output_grad = dot(resid_all, attn_all, TN)[:shard].T

    grad_normed_part = dot(grad_qkv, whole[:, :qkv_width], NT)
    attn_gain_part = jnp.sum(grad_normed_part * unit_one, axis=0)

    last = jnp.concatenate([sink_part[0, :heads], router_bias_part])
    last = jnp.pad(last, (0, features - last.shape[0]))
    vectors = jnp.stack([attn_gain_part, ffn_gain_part, output_bias_part, last])
    vectors = jnp.transpose(vectors.reshape(4, expert_axis, shard), (1, 0, 2))
    vectors = vectors.reshape(expert_axis, 4 * shard)
    small = jnp.concatenate([router_part, vectors], axis=1).astype(LOW)
    small = lax.all_to_all(small, "expert", split_axis=0, concat_axis=0, tiled=True)
    small = jnp.sum(small.astype(F32), axis=0)
    gain_here = small[features : features + shard]
    near = [(i, i ^ 1) for i in range(tensor_axis)]
    far = [(i, tensor_axis - 1 - i) for i in range(tensor_axis)]
    gain_here = gain_here + lax.ppermute(gain_here, "tensor", near)
    gain_here = gain_here + lax.ppermute(gain_here, "tensor", far)
    small = jnp.concatenate([small[:features], gain_here, small[features + shard :]])
    small = lax.all_gather(small.astype(LOW), "expert", axis=0).astype(F32)
    w_router_grad = small[:, :features].T
    vectors = jnp.transpose(small[:, features:].reshape(expert_axis, 4, shard), (1, 0, 2))
    vectors = vectors.reshape(4, features)

    grad_normed = tensor_sum(grad_normed_part, tensor_axis) * attn_gain
    input_grad = grad_resid + scale_one * (
        grad_normed - unit_one * jnp.mean(unit_one * grad_normed, axis=-1, keepdims=True)
    )

    weighted = place.reshape(experts, capacity, tokens).astype(F32) * gates.T[:, None, :]
    weighted = weighted.astype(LOW).reshape(slots, tokens)
    mixed = tensor_sum(dot(weighted, returned, TN), tensor_axis)
    block_output = (residual + mixed).astype(LOW)

    qkv_grad = dot(normed_all, grad_qkv_all, TN)
    query_end = w_query.shape[1]
    key_end = query_end + w_key.shape[1]
    return (
        block_output,
        input_grad,
        vectors[0],
        qkv_grad[:shard, :query_end],
        qkv_grad[:shard, query_end:key_end],
        qkv_grad[:shard, key_end:],
        qkv_grad[shard, :query_end],
        qkv_grad[shard, query_end:key_end],
        qkv_grad[shard, key_end:],
        vectors[3, :heads],
        w_output_grad,
        vectors[2],
        vectors[1],
        w_router_grad,
        vectors[3, heads : heads + experts],
        w_gate_grad,
        w_up_grad,
        b_gate_grad,
        b_up_grad,
        w_down_grad,
        b_down_grad,
    )


def solution(mesh):
    in_specs = (
        P("expert", None),
        P("expert", None),
        P("expert", None),
        P("expert", None),
        P(),
        P("expert", "tensor"),
        P("expert", "tensor"),
        P("expert", "tensor"),
        P("tensor"),
        P("tensor"),
        P("tensor"),
        P("tensor"),
        P("tensor", "expert"),
        P(),
        P(),
        P(),
        P(),
        P("expert", None, "tensor"),
        P("expert", None, "tensor"),
        P("expert", "tensor"),
        P("expert", "tensor"),
        P("expert", "tensor", None),
        P("expert", None),
    )
    out_specs = (
        P("expert", None),
        P("expert", None),
        P(),
        P("expert", "tensor"),
        P("expert", "tensor"),
        P("expert", "tensor"),
        P("tensor"),
        P("tensor"),
        P("tensor"),
        P("tensor"),
        P("tensor", "expert"),
        P(),
        P(),
        P(),
        P(),
        P("expert", None, "tensor"),
        P("expert", None, "tensor"),
        P("expert", "tensor"),
        P("expert", "tensor"),
        P("expert", "tensor", None),
        P("expert", None),
    )
    body = functools.partial(on_device, mesh.shape["expert"], mesh.shape["tensor"])
    return jax.shard_map(body, mesh=mesh, in_specs=in_specs, out_specs=out_specs, check_vma=False)
```

```python
import functools

import jax
import jax.numpy as jnp
from jax import lax
from jax.experimental import pallas as pl
from jax.experimental.pallas import tpu as pltpu
from jax.sharding import PartitionSpec as P

HD = 64
PAIR = 2 * HD
EPSILON = 1e-05
ROPE_BASE = 150000.0
CLAMP_LIMIT = 7.0
GLU_SLOPE = 1.702
MASKED = -1e30
PRECISE = lax.Precision.HIGHEST
LOW = jnp.bfloat16
F32 = jnp.float32
VMEM_BYTES = 56 * 1024 * 1024
NN = (((1,), (0,)), ((), ()))
NT = (((1,), (1,)), ((), ()))
TN = (((0,), (0,)), ((), ()))


def round_up(value, unit):
    return -(-value // unit) * unit


def dot(left, right, dims=NN):
    return lax.dot_general(left, right, dims, preferred_element_type=F32)


def split_low(values):
    high = values.astype(LOW)
    return high, (values - high.astype(F32)).astype(LOW)


def layout(lengths, tok_count):
    seq_ends = jnp.cumsum(lengths)
    tok_index = jnp.arange(tok_count, dtype=jnp.int32)
    is_past = tok_index[:, None] >= seq_ends[None, :]
    segment = jnp.sum(is_past.astype(jnp.int32), axis=1)
    offset = jnp.sum(jnp.where(is_past, lengths[None, :], 0), axis=1)
    return (segment, tok_index - offset)


def rope_tables(position):
    half = HD // 2
    frequency = ROPE_BASE ** (-(jnp.arange(half).astype(F32) * 2.0 / HD))
    angles = position.astype(F32)[:, None] * frequency[None, :]
    cosine, sine = jnp.cos(angles), jnp.sin(angles)
    return (
        jnp.concatenate([cosine] * 4, axis=1),
        jnp.concatenate([-sine, sine, -sine, sine], axis=1),
    )


def lane_index(shape):
    return lax.broadcasted_iota(jnp.int32, shape, len(shape) - 1)


def swap_halves(values):
    first = (lane_index(values.shape) % HD) < HD // 2
    return jnp.where(
        first, pltpu.roll(values, PAIR - HD // 2, 1), pltpu.roll(values, HD // 2, 1)
    )


def twin(values, which):
    turned = pltpu.roll(values, HD, 1)
    left = lane_index(values.shape) < HD
    return jnp.where(left, values, turned) if which == 0 else jnp.where(left, turned, values)


def attend_forward_kernel(
    sink_ref,
    rows_ref,
    weights_ref,
    bias_ref,
    cos_ref,
    sin_ref,
    allowed_ref,
    out_ref,
    rot_ref,
    lse_ref,
    qkv_ref,
):
    step = pl.program_id(0)
    start = weights_ref.shape[1] - qkv_ref.shape[1]
    part = dot(rows_ref[...], weights_ref[:, start:])

    @pl.when(step == 0)
    def _():
        qkv_ref[...] = part + bias_ref[...]

    @pl.when(step > 0)
    def _():
        qkv_ref[...] += part

    @pl.when(step == pl.num_programs(0) - 1)
    def _():
        attend(
            sink_ref, qkv_ref, cos_ref, sin_ref, allowed_ref, out_ref, rot_ref, lse_ref
        )


def attend(sink_ref, qkv_ref, cos_ref, sin_ref, allowed_ref, out_ref, rot_ref, lse_ref):
    tokens = qkv_ref.shape[0]
    heads = sink_ref.shape[0]
    key_at = heads * HD
    value_at = key_at + PAIR
    per_group = heads // 2
    cos, sin = cos_ref[...], sin_ref[...]
    allowed = allowed_ref[...] > 0.5
    left = lane_index((tokens, PAIR)) < HD
    lanes = lane_index((tokens, PAIR))

    def rope(values):
        return values * cos + swap_halves(values) * sin

    key = rope(qkv_ref[:, key_at:value_at])
    value = qkv_ref[:, value_at : value_at + PAIR]
    rot_ref[:, key_at:value_at] = key.astype(LOW)
    rot_ref[:, value_at : value_at + PAIR] = value.astype(LOW)
    keys = [twin(key, g).astype(LOW) for g in range(2)]
    values = [twin(value, g).astype(LOW) for g in range(2)]
    lse_all = jnp.zeros((tokens, PAIR), F32)
    for pair in range(heads // 2):
        cols = slice(pair * PAIR, (pair + 1) * PAIR)
        group = (2 * pair) // per_group
        query = rope(qkv_ref[:, cols])
        rot_ref[:, cols] = query.astype(LOW)
        outs = []
        for side in range(2):
            head = 2 * pair + side
            mine = left if side == 0 else jnp.logical_not(left)
            one = jnp.where(mine, query, 0.0).astype(LOW)
            scores = dot(one, keys[group], NT) * HD ** (-0.5)
            scores = jnp.where(allowed, scores, MASKED)
            sink = sink_ref[head]
            top = jnp.maximum(jnp.max(scores, axis=1, keepdims=True), sink)
            weights = jnp.exp(scores - top)
            denom = jnp.sum(weights, axis=1, keepdims=True) + jnp.exp(sink - top)
            lse = top + jnp.log(denom)
            lse_all = jnp.where(lanes == head, lse, lse_all)
            prob = (weights / denom).astype(LOW)
            outs.append(dot(prob, values[group]))
        out_ref[:, cols] = jnp.where(left, outs[0], outs[1]).astype(LOW)
    lse_ref[...] = lse_all


def attend_backward_kernel(
    sink_ref,
    rows_ref,
    weights_ref,
    rot_ref,
    lse_ref,
    cos_ref,
    sin_ref,
    allowed_ref,
    out_ref,
    sink_out_ref,
    sum_ref,
    grad_ref,
):
    step = pl.program_id(0)
    part = dot(rows_ref[...], weights_ref[...])

    @pl.when(step == 0)
    def _():
        sum_ref[...] = part

    @pl.when(step > 0)
    def _():
        sum_ref[...] += part

    @pl.when(step == pl.num_programs(0) - 1)
    def _():
        grad_ref[...] = sum_ref[...].astype(LOW)
        attend_back(
            sink_ref,
            rot_ref,
            grad_ref,
            lse_ref,
            cos_ref,
            sin_ref,
            allowed_ref,
            out_ref,
            sink_out_ref,
        )


def attend_back(
    sink_ref, rot_ref, grad_ref, lse_ref, cos_ref, sin_ref, allowed_ref, out_ref, sink_out_ref
):
    tokens = rot_ref.shape[0]
    heads = sink_ref.shape[0]
    key_at = heads * HD
    value_at = key_at + PAIR
    per_group = heads // 2
    scale = HD ** (-0.5)
    cos, sin = cos_ref[...], sin_ref[...]
    allowed = allowed_ref[...] > 0.5
    lanes = lane_index((tokens, PAIR))
    left = lanes < HD

    def turn_back(values):
        return values * cos - swap_halves(values) * sin

    key = rot_ref[:, key_at:value_at].astype(F32)
    value = rot_ref[:, value_at : value_at + PAIR].astype(F32)
    keys = [twin(key, g).astype(LOW) for g in range(2)]
    values = [twin(value, g).astype(LOW) for g in range(2)]
    key_sums = [jnp.zeros((tokens, PAIR), F32) for _ in range(2)]
    value_sums = [jnp.zeros((tokens, PAIR), F32) for _ in range(2)]
    sink_all = jnp.zeros((tokens, PAIR), F32)
    lse_all = lse_ref[...]
    for pair in range(heads // 2):
        cols = slice(pair * PAIR, (pair + 1) * PAIR)
        group = (2 * pair) // per_group
        query = rot_ref[:, cols].astype(F32)
        grad = grad_ref[:, cols].astype(F32)
        outs = []
        for side in range(2):
            head = 2 * pair + side
            mine = left if side == 0 else jnp.logical_not(left)
            one = jnp.where(mine, query, 0.0).astype(LOW)
            grad_one = jnp.where(mine, grad, 0.0).astype(LOW)
            lse = jnp.sum(jnp.where(lanes == head, lse_all, 0.0), axis=1, keepdims=True)
            scores = dot(one, keys[group], NT) * scale
            prob = jnp.where(allowed, jnp.exp(jnp.where(allowed, scores - lse, 0.0)), 0.0)
            grad_prob = dot(grad_one, values[group], NT)
            delta = jnp.sum(prob * grad_prob, axis=1, keepdims=True)
            grad_score = (prob * (grad_prob - delta)).astype(LOW)
            outs.append(dot(grad_score, keys[group]))
            key_sums[group] += dot(grad_score, one, TN)
            value_sums[group] += dot(prob.astype(LOW), grad_one, TN)
            sink_all = jnp.where(lanes == head, jnp.exp(sink_ref[head] - lse) * delta, sink_all)
        out_ref[:tokens, cols] = turn_back(jnp.where(left, outs[0], outs[1]) * scale).astype(LOW)

    def fold(sums):
        both = [one + pltpu.roll(one, HD, 1) for one in sums]
        return jnp.where(left, both[0], both[1])

    out_ref[:tokens, key_at:value_at] = turn_back(fold(key_sums) * scale).astype(LOW)
    out_ref[:tokens, value_at : value_at + PAIR] = fold(value_sums).astype(LOW)
    sink_out_ref[...] = -jnp.sum(sink_all, axis=0, keepdims=True)


def kernel_params():
    return pltpu.CompilerParams(vmem_limit_bytes=VMEM_BYTES)


SHORT = pl.CostEstimate(flops=1, bytes_accessed=1, transcendentals=0)
IN_VMEM = pl.BlockSpec(memory_space=pltpu.VMEM)
IN_SMEM = pl.BlockSpec(memory_space=pltpu.SMEM)


def by_row(block, columns):
    return pl.BlockSpec((block, columns), lambda i: (i, 0))


def by_column(rows, block):
    return pl.BlockSpec((rows, block), lambda i: (0, i))


def whole_block(*shape):
    return pl.BlockSpec(shape, lambda i: (0, 0))


STEPS = 4


def attend_forward(sinks, rows, weights, bias, cos, sin, allowed):
    tokens, inner = rows.shape
    width = bias.shape[1]
    heads = sinks.shape[0]
    block = inner // STEPS
    return pl.pallas_call(
        attend_forward_kernel,
        grid=(STEPS,),
        out_shape=(
            jax.ShapeDtypeStruct((tokens, heads * HD), LOW),
            jax.ShapeDtypeStruct((tokens, width), LOW),
            jax.ShapeDtypeStruct((tokens, PAIR), F32),
        ),
        in_specs=[
            IN_SMEM,
            by_column(tokens, block),
            by_row(block, weights.shape[1]),
            whole_block(1, width),
            whole_block(*cos.shape),
            whole_block(*sin.shape),
            whole_block(*allowed.shape),
        ],
        out_specs=(
            whole_block(tokens, heads * HD),
            whole_block(tokens, width),
            whole_block(tokens, PAIR),
        ),
        scratch_shapes=[pltpu.VMEM((tokens, width), F32)],
        compiler_params=kernel_params(),
        cost_estimate=SHORT,
        name="attend_forward",
    )(sinks, rows, weights, bias, cos, sin, allowed)


def attend_backward(sinks, rows, weights, rotated, lse, cos, sin, allowed):
    tokens, width = rotated.shape
    inner = rows.shape[1]
    out_width = sinks.shape[0] * HD
    block = inner // STEPS
    return pl.pallas_call(
        attend_backward_kernel,
        grid=(STEPS,),
        out_shape=(
            jax.ShapeDtypeStruct((tokens, width), LOW),
            jax.ShapeDtypeStruct((1, PAIR), F32),
        ),
        in_specs=[
            IN_SMEM,
            by_column(tokens, block),
            by_row(block, out_width),
            whole_block(tokens, width),
            whole_block(*lse.shape),
            whole_block(*cos.shape),
            whole_block(*sin.shape),
            whole_block(*allowed.shape),
        ],
        out_specs=(whole_block(tokens, width), whole_block(1, PAIR)),
        scratch_shapes=[pltpu.VMEM((tokens, out_width), F32), pltpu.VMEM((tokens, out_width), LOW)],
        compiler_params=kernel_params(),
        cost_estimate=SHORT,
        name="attend_backward",
    )(sinks, rows, weights, rotated, lse, cos, sin, allowed)


def compact_kernel(shard, shard_pad, left_ref, weights_ref, *refs):
    unit_ref, upper_ref, lower_ref, gain_ref = refs if len(refs) == 4 else (None, *refs, None)
    start = weights_ref.shape[1] - left_ref.shape[1]
    product = dot(left_ref[...], weights_ref[:, start:], NT)
    half = upper_ref.shape[0]
    shards = weights_ref.shape[0] // shard_pad
    if gain_ref is not None:
        gain = jnp.sum(product * unit_ref[...], axis=0, keepdims=True)
    for step in range(upper_ref.shape[1] // (shards * shard)):

        @pl.when(pl.program_id(0) == step)
        def _():
            for i in range(shards):
                piece = product[:, i * shard_pad : i * shard_pad + shard].astype(LOW)
                at = (step * shards + i) * shard
                upper_ref[:, at : at + shard] = piece[:half]
                lower_ref[:, at : at + shard] = piece[half:]
                if gain_ref is not None:
                    pad_at = i * shard_pad
                    gain_ref[:, at : at + shard] = gain[:, pad_at : pad_at + shard]


def compact_product(left, tokens, weights, block_width, shard, shard_pad, name, unit=None):
    inner = left.shape[1]
    rows = weights.shape[0]
    features = rows // shard_pad * shard
    half = jax.ShapeDtypeStruct((tokens // 2, features), LOW)
    operands = [left, weights]
    in_specs = [whole_block(tokens, inner), by_row(rows // STEPS, block_width)]
    out_shape = [half, half]
    if unit is not None:
        operands.append(unit)
        in_specs.append(by_column(tokens, rows // STEPS))
        out_shape.append(jax.ShapeDtypeStruct((1, features), F32))
    return pl.pallas_call(
        functools.partial(compact_kernel, shard, shard_pad),
        grid=(STEPS,),
        out_shape=out_shape,
        in_specs=in_specs,
        out_specs=[whole_block(*one.shape) for one in out_shape],
        compiler_params=kernel_params(),
        cost_estimate=SHORT,
        name=name,
    )(*operands)


def rms_scale(values):
    return lax.rsqrt(jnp.mean(values * values, axis=1, keepdims=True) + EPSILON)


def join_halves(halves, out_ref):
    upper, upper_in, lower, lower_in = halves
    half = upper.shape[0]
    out_ref[:half, :] = upper[...].astype(F32) + upper_in[...].astype(F32)
    out_ref[half:, :] = lower[...].astype(F32) + lower_in[...].astype(F32)


def token_forward_kernel(place_ref, input_ref, *refs):
    halves, refs = refs[:4], refs[4:]
    bias_ref, gain_ref, router_ref, router_bias_ref, named_ref, slots_ref = refs[:6]
    resid_ref, gates_ref, sent_ref, own_ref = refs[6:]
    features = input_ref.shape[1]
    experts = router_ref.shape[0]
    chunk = own_ref.shape[1]
    join_halves(halves, resid_ref)
    resid = input_ref[...].astype(F32) + resid_ref[...] + bias_ref[...]
    resid_ref[...] = resid
    normed = resid * rms_scale(resid) * gain_ref[...]
    logits = lax.dot_general(
        normed, router_ref[...], NT, precision=PRECISE, preferred_element_type=F32
    )
    named = named_ref[...] > 0.5
    logits = jnp.where(named, logits + router_bias_ref[...], MASKED)
    weights = jnp.exp(logits - jnp.max(logits, axis=1, keepdims=True))
    weights = jnp.where(named, weights, 0.0)
    gates = weights / jnp.sum(weights, axis=1, keepdims=True)
    gates_ref[...] = gates
    high, low = split_low(gates)
    sent_ref[:, :features] = normed.astype(LOW)
    sent_ref[:, features : features + experts] = high
    sent_ref[:, features + experts : features + 2 * experts] = low
    spare = sent_ref.shape[1] - features - 2 * experts
    if spare:
        sent_ref[:, features + 2 * experts :] = jnp.zeros((resid.shape[0], spare), LOW)
    own = sent_ref[:, pl.ds(pl.multiple_of(place_ref[0] * chunk, 128), chunk)]
    own_ref[...] = dot(slots_ref[...], own).astype(LOW)


def token_forward(place, inputs, halves, bias, gain, router, router_bias, named, slots, width, chunk):
    tokens, features = inputs.shape
    experts = router.shape[0]
    return pl.pallas_call(
        token_forward_kernel,
        out_shape=(
            jax.ShapeDtypeStruct((tokens, features), F32),
            jax.ShapeDtypeStruct((tokens, experts), F32),
            jax.ShapeDtypeStruct((tokens, width), LOW),
            jax.ShapeDtypeStruct((slots.shape[0], chunk), LOW),
        ),
        in_specs=[IN_SMEM] + [IN_VMEM] * 11,
        out_specs=(IN_VMEM,) * 4,
        compiler_params=kernel_params(),
        cost_estimate=SHORT,
        name="token_forward",
    )(place, inputs, *halves, bias, gain, router, router_bias, named, slots)


def token_backward_kernel(shard, shard_pad, place_ref, *refs):
    near_halves, halves, refs = refs[:4], refs[4:8], refs[8:]
    gates_ref, router_ref, resid_ref, cotangent_ref, gain_ref = refs[:5]
    out_ref, spread_ref, blocks_ref, router_out_ref, vectors_ref = refs[5:10]
    near_ref, far_ref, grad_ref, router_all_ref = refs[10:]
    tokens, features = resid_ref.shape
    experts = router_ref.shape[0]
    split = near_ref.shape[1]
    rest = features - split
    join_halves(near_halves, near_ref)
    join_halves(halves, far_ref)
    gates = gates_ref[...]
    grad_gates = far_ref[:, rest : rest + experts] + far_ref[:, rest + experts : rest + 2 * experts]
    grad_logits = gates * (grad_gates - jnp.sum(gates * grad_gates, axis=1, keepdims=True))
    through = lax.dot_general(
        grad_logits, router_ref[...], NN, precision=PRECISE, preferred_element_type=F32
    )
    grad_ref[:, :split] = through[:, :split] + near_ref[...]
    grad_ref[:, split:] = through[:, split:] + far_ref[:, :rest]
    grad_two = grad_ref[...]
    resid = resid_ref[...]
    scale = rms_scale(resid)
    unit = resid * scale
    gain = gain_ref[...]
    router_part = lax.dot_general(
        grad_logits, unit * gain, TN, precision=PRECISE, preferred_element_type=F32
    )
    scaled = grad_two * gain
    mean = jnp.mean(unit * scaled, axis=1, keepdims=True)
    grad_resid = cotangent_ref[...].astype(F32) + scale * (scaled - unit * mean)
    out_ref[...] = grad_resid
    vectors_ref[...] = jnp.zeros_like(vectors_ref)
    vectors_ref[0:1, :features] = jnp.sum(grad_two * unit, axis=0, keepdims=True)
    vectors_ref[1:2, :features] = jnp.sum(grad_resid, axis=0, keepdims=True)
    vectors_ref[2:3, :experts] = jnp.sum(grad_logits, axis=0, keepdims=True)
    low = grad_resid.astype(LOW)
    for i in range(features // shard):
        at = i * shard_pad
        spread_ref[:, at : at + shard] = low[:, i * shard : (i + 1) * shard]
        spread_ref[:, at + shard : at + shard_pad] = jnp.zeros((tokens, shard_pad - shard), LOW)
    turned = spread_ref[...].T
    for i in range(features // shard):
        blocks_ref[i] = turned[i * shard_pad : (i + 1) * shard_pad]
    router_all_ref[:, :features] = router_part.astype(LOW)
    spare = router_all_ref.shape[1] - features
    router_all_ref[:, features:] = jnp.zeros((router_part.shape[0], spare), LOW)
    block = router_out_ref.shape[1]
    start = pl.multiple_of(place_ref[0] * block, 128)
    router_out_ref[...] = router_all_ref[:, pl.ds(start, block)]


def pack_kernel(router_ref, vectors_ref, gain_ref, sinks_ref, out_ref):
    experts, width = router_ref.shape
    features = gain_ref.shape[1]
    out_ref[...] = jnp.zeros_like(out_ref)
    out_ref[:experts, :] = router_ref[...]
    row = experts
    for values in (gain_ref[...], vectors_ref[0:1, :features], vectors_ref[1:2, :features]):
        for at in range(0, features, width):
            piece = values[:, at : at + width].astype(LOW)
            out_ref[row : row + 1, : piece.shape[1]] = piece
            row += 1
    lanes = sinks_ref.shape[1]
    out_ref[row : row + 1, :lanes] = sinks_ref[...].astype(LOW)
    out_ref[row + 1 : row + 2, :lanes] = vectors_ref[2:3, :lanes].astype(LOW)


def pack_small(router, vectors, gain, sinks):
    experts, width = router.shape
    rows = round_up(experts + 3 * -(-gain.shape[1] // width) + 2, 16)
    return pl.pallas_call(
        pack_kernel,
        out_shape=jax.ShapeDtypeStruct((rows, width), LOW),
        in_specs=[IN_VMEM] * 4,
        out_specs=IN_VMEM,
        compiler_params=kernel_params(),
        cost_estimate=SHORT,
        name="pack_small",
    )(router, vectors, gain, sinks)


def unpack_kernel(place_ref, *refs):
    chunk_refs, (rest_ref, router_ref, gain_ref, first_ref, second_ref), refs = (
        refs[:4],
        refs[4:9],
        refs[9:],
    )
    sinks_ref, bias_ref, all_ref = refs
    experts, features = router_ref.shape
    width = chunk_refs[0].shape[1]
    assemble(place_ref, chunk_refs, all_ref)
    router_ref[...] = all_ref[:experts, :features].astype(F32)
    tiles = -(-features // width)
    for tile in range(tiles):
        at = tile * width
        size = min(width, features - at)
        row = experts + tile
        parts = all_ref[row : row + 1, :].astype(F32)
        total = sum(parts[:, i * width : (i + 1) * width] for i in range(4))
        gain_ref[:, at : at + size] = total[:, :size]
        for i, out_ref in enumerate((first_ref, second_ref)):
            row = i * tiles + tile
            out_ref[:, at : at + size] = rest_ref[row : row + 1, :size].astype(F32)
    lanes = sinks_ref.shape[1]
    row = 2 * tiles
    sinks_ref[...] = rest_ref[row : row + 1, :lanes].astype(F32)
    bias_ref[...] = rest_ref[row + 1 : row + 2, :lanes].astype(F32)


def unpack_small(place, chunks, rest, experts, features, lanes):
    rows, width = chunks[0].shape
    wide = jax.ShapeDtypeStruct((1, features), F32)
    short = jax.ShapeDtypeStruct((1, lanes), F32)
    return pl.pallas_call(
        unpack_kernel,
        out_shape=(
            jax.ShapeDtypeStruct((experts, features), F32),
            wide,
            wide,
            wide,
            short,
            short,
        ),
        in_specs=[IN_SMEM] + [IN_VMEM] * 5,
        out_specs=(IN_VMEM,) * 6,
        scratch_shapes=[pltpu.VMEM((rows, len(chunks) * width), LOW)],
        compiler_params=kernel_params(),
        cost_estimate=SHORT,
        name="unpack_small",
    )(place, *chunks, rest)


def gathered_kernel(shard, blocks_ref, rows_ref, *refs):
    *out_refs, sum_ref = refs
    blocks = blocks_ref.shape[0]
    tokens = blocks_ref.shape[2]
    total = None
    for i in range(blocks):
        rows = rows_ref[i * tokens : (i + 1) * tokens, :]
        part = dot(blocks_ref[i], rows)
        total = part if total is None else total + part
    first = pl.program_id(0) == 0

    @pl.when(first)
    def _():
        sum_ref[...] = total

    @pl.when(jnp.logical_not(first))
    def _():
        sum_ref[...] += total

    @pl.when(pl.program_id(0) == pl.num_programs(0) - 1)
    def _():
        at = 0
        for out_ref in out_refs[: len(out_refs) // 2 if len(out_refs) > 1 else 1]:
            out_ref[...] = sum_ref[:shard, at : at + out_ref.shape[1]]
            at += out_ref.shape[1]
        at = 0
        for out_ref in out_refs[len(out_refs) // 2 if len(out_refs) > 1 else 1 :]:
            out_ref[...] = sum_ref[shard : shard + 1, at : at + out_ref.shape[1]]
            at += out_ref.shape[1]


def gathered_products(blocks, which, rows, widths, shard, shard_pad, biases, name):
    parts, _, tokens = blocks.shape
    total, width = rows.shape
    block = parts // STEPS
    out_shape = [jax.ShapeDtypeStruct((shard, one), F32) for one in widths]
    if biases:
        out_shape += [jax.ShapeDtypeStruct((1, one), F32) for one in widths]
    return pl.pallas_call(
        functools.partial(gathered_kernel, shard),
        grid=(STEPS,),
        out_shape=out_shape,
        in_specs=[
            pl.BlockSpec((block, shard_pad, tokens), lambda i: (i, which, 0)),
            by_row(total // STEPS, width),
        ],
        out_specs=[whole_block(*one.shape) for one in out_shape],
        scratch_shapes=[pltpu.VMEM((shard_pad, width), F32)],
        compiler_params=kernel_params(),
        cost_estimate=SHORT,
        name=name,
    )(blocks, rows)


def token_backward(
    place, near, halves, gates, router, resid, cotangent, gain, shard, shard_pad, ring
):
    tokens, features = resid.shape
    experts = router.shape[0]
    router_block = round_up(-(-features // ring), 128)
    parts = features // shard
    return pl.pallas_call(
        functools.partial(token_backward_kernel, shard, shard_pad),
        out_shape=(
            jax.ShapeDtypeStruct((tokens, features), F32),
            jax.ShapeDtypeStruct((tokens, features // shard * shard_pad), LOW),
            jax.ShapeDtypeStruct((parts, shard_pad, tokens), LOW),
            jax.ShapeDtypeStruct((experts, router_block), LOW),
            jax.ShapeDtypeStruct((8, router_block * ring), F32),
        ),
        in_specs=[IN_SMEM] + [IN_VMEM] * 13,
        out_specs=(IN_VMEM,) * 5,
        scratch_shapes=[
            pltpu.VMEM((tokens, near[0].shape[1]), F32),
            pltpu.VMEM((tokens, halves[0].shape[1]), F32),
            pltpu.VMEM((tokens, features), F32),
            pltpu.VMEM((experts, router_block * ring), LOW),
        ],
        compiler_params=kernel_params(),
        cost_estimate=SHORT,
        name="token_backward",
    )(place, *near, *halves, gates, router, resid, cotangent, gain)


def output_kernel(place_ref, *refs):
    near_refs, (resid_ref, out_ref, near_ref) = refs[:4], refs[4:]
    assemble(place_ref, near_refs, near_ref)
    near = near_ref[:, : out_ref.shape[1]].astype(F32)
    out_ref[...] = (resid_ref[...] + near).astype(LOW)


def output_rows(place, near, resid):
    tokens, features = resid.shape
    return pl.pallas_call(
        output_kernel,
        out_shape=jax.ShapeDtypeStruct((tokens, features), LOW),
        in_specs=[IN_SMEM] + [IN_VMEM] * 5,
        out_specs=IN_VMEM,
        scratch_shapes=[pltpu.VMEM((tokens, sum(one.shape[1] for one in near)), LOW)],
        compiler_params=kernel_params(),
        cost_estimate=SHORT,
        name="output_rows",
    )(place, *near, resid)


def store_halves(values, rest, experts, upper_ref, lower_ref):
    half = upper_ref.shape[0]
    main = values[:, :rest].astype(LOW)
    upper_ref[:, :rest], lower_ref[:, :rest] = main[:half], main[half:]
    high, low = split_low(values[:, rest : rest + experts] + values[:, rest + experts : rest + 2 * experts])
    for out_ref, rows in ((upper_ref, slice(0, half)), (lower_ref, slice(half, 2 * half))):
        out_ref[:, rest : rest + experts] = high[rows]
        out_ref[:, rest + experts : rest + 2 * experts] = low[rows]
        spare = out_ref.shape[1] - rest - 2 * experts
        if spare:
            out_ref[:, rest + 2 * experts :] = jnp.zeros((half, spare), LOW)


def combine_kernel(rest, experts, place_ref, rows_ref, upper_ref, lower_ref):
    store_halves(dot(place_ref[...], rows_ref[...]), rest, experts, upper_ref, lower_ref)


def combine_far(place_t, rows, rest, experts):
    half = jax.ShapeDtypeStruct((place_t.shape[0] // 2, rows.shape[1]), LOW)
    return pl.pallas_call(
        functools.partial(combine_kernel, rest, experts),
        out_shape=(half, half),
        in_specs=[IN_VMEM] * 2,
        out_specs=(IN_VMEM,) * 2,
        compiler_params=kernel_params(),
        cost_estimate=SHORT,
        name="combine_far",
    )(place_t, rows)


def combine_near_kernel(place_ref, rows_ref, upper_ref, lower_ref):
    total = dot(place_ref[...], rows_ref[...]).astype(LOW)
    half = upper_ref.shape[0]
    upper_ref[...], lower_ref[...] = total[:half], total[half:]


def combine_near(place_t, rows):
    half = jax.ShapeDtypeStruct((place_t.shape[0] // 2, rows.shape[1]), LOW)
    return pl.pallas_call(
        combine_near_kernel,
        out_shape=(half, half),
        in_specs=[IN_VMEM] * 2,
        out_specs=(IN_VMEM,) * 2,
        compiler_params=kernel_params(),
        cost_estimate=SHORT,
        name="combine_near",
    )(place_t, rows)


def middle_kernel(rest, experts, *refs):
    halves, (upper_ref, lower_ref, sum_ref) = refs[:4], refs[4:]
    join_halves(halves, sum_ref)
    store_halves(sum_ref[...], rest, experts, upper_ref, lower_ref)


def middle_far(halves, rest, experts):
    half = jax.ShapeDtypeStruct(halves[0].shape, LOW)
    return pl.pallas_call(
        functools.partial(middle_kernel, rest, experts),
        out_shape=(half, half),
        in_specs=[IN_VMEM] * 4,
        out_specs=(IN_VMEM,) * 2,
        scratch_shapes=[pltpu.VMEM((2 * half.shape[0], half.shape[1]), F32)],
        compiler_params=kernel_params(),
        cost_estimate=SHORT,
        name="middle_far",
    )(*halves)


def assemble(place_ref, near_refs, out_ref):
    ring, width = len(near_refs), near_refs[0].shape[1]
    for ahead, near_ref in enumerate(near_refs):
        start = (place_ref[0] + ahead) % ring * width
        out_ref[:, pl.ds(pl.multiple_of(start, 128), width)] = near_ref[...]


def grad_hidden_kernel(place_ref, *refs):
    chunk_refs, (down_ref, bias_ref, out_ref, all_ref, rows_ref) = refs[:-5], refs[-5:]
    hidden, features = down_ref.shape
    assemble(place_ref, chunk_refs, rows_ref)
    rows = rows_ref[:, :features]
    all_ref[...] = rows
    spare = out_ref.shape[1] - hidden
    out_ref[:, :hidden] = dot(rows, down_ref[...], NT)
    with_bias = jnp.sum(rows.astype(F32) * bias_ref[...], axis=1, keepdims=True)
    out_ref[:, hidden:] = jnp.broadcast_to(with_bias, (rows.shape[0], spare))


def grad_hidden_product(place, chunks, down, bias):
    count, chunk = chunks[0].shape
    hidden, features = down.shape
    width = round_up(hidden + 1, 128)
    block = count // 4
    return pl.pallas_call(
        grad_hidden_kernel,
        grid=(count // block,),
        out_shape=(
            jax.ShapeDtypeStruct((count, width), F32),
            jax.ShapeDtypeStruct((count, features), LOW),
        ),
        in_specs=[IN_SMEM]
        + [by_row(block, chunk)] * len(chunks)
        + [whole_block(hidden, features), whole_block(1, features)],
        out_specs=(by_row(block, width), by_row(block, features)),
        scratch_shapes=[pltpu.VMEM((block, len(chunks) * chunk), LOW)],
        compiler_params=kernel_params(),
        cost_estimate=SHORT,
        name="grad_hidden",
    )(place, *chunks, down, bias)


def result_kernel(act_ref, down_ref, bias_ref, out_ref):
    parts, rows, width = out_ref.shape
    result = (dot(act_ref[...], down_ref[...]) + bias_ref[...]).astype(LOW)
    for part in range(parts):
        columns = result[:, part * width : (part + 1) * width]
        out_ref[part, :, : columns.shape[1]] = columns
        if columns.shape[1] < width:
            out_ref[part, :, columns.shape[1] :] = jnp.zeros((rows, width - columns.shape[1]), LOW)


def expert_result(act, down, bias, parts, width):
    count, hidden = act.shape
    features = down.shape[1]
    block = count // 4
    return pl.pallas_call(
        result_kernel,
        grid=(count // block,),
        out_shape=jax.ShapeDtypeStruct((parts, count, width), LOW),
        in_specs=[by_row(block, hidden), whole_block(hidden, features), whole_block(1, features)],
        out_specs=pl.BlockSpec((parts, block, width), lambda i: (0, i, 0)),
        compiler_params=kernel_params(),
        cost_estimate=SHORT,
        name="expert_result",
    )(act, down, bias)


def place_kernel(place_ref, rows_ref, out_ref):
    out_ref[...] = dot(place_ref[...], rows_ref[...]).astype(LOW)


def place_rows(place, rows):
    count, tokens = place.shape
    width = rows.shape[1]
    block = count // 4
    return pl.pallas_call(
        place_kernel,
        grid=(count // block,),
        out_shape=jax.ShapeDtypeStruct((count, width), LOW),
        in_specs=[
            pl.BlockSpec((block, tokens), lambda i: (i, 0)),
            pl.BlockSpec((tokens, width), lambda i: (0, 0)),
        ],
        out_specs=pl.BlockSpec((block, width), lambda i: (i, 0)),
        compiler_params=kernel_params(),
        cost_estimate=SHORT,
        name="place_rows",
    )(place, rows)


def expert_kernel(experts, ring, place_ref, *refs):
    near_refs, refs = refs[:ring], refs[ring:]
    far_ref, first_ref, gate_ref, up_ref, gate_bias_ref, up_bias_ref, mine_ref = refs[:7]
    grad_far_ref, act_ref, act_gated_ref, grad_gate_ref, grad_up_ref = refs[7:12]
    bias_sums_ref, rows_ref, near_ref = refs[12:]
    hidden, features = gate_ref.shape
    split = near_ref.shape[1]
    rest = features - split
    assemble(place_ref, near_refs, near_ref)
    near, far = near_ref[...], far_ref[:, :rest]
    rows_ref[:, :split], rows_ref[:, split:] = near, far
    mine = mine_ref[...]
    gate = jnp.sum(far_ref[:, rest:].astype(F32) * mine, axis=1, keepdims=True)

    def product(weights_ref):
        return dot(near, weights_ref[:, :split], NT) + dot(far, weights_ref[:, split:], NT)

    gate_lin = product(gate_ref) + gate_bias_ref[...]
    up_lin = product(up_ref) + up_bias_ref[...]
    gate_tanh = jnp.tanh(gate_lin * (1.0 / CLAMP_LIMIT))
    up_tanh = jnp.tanh(up_lin * (1.0 / CLAMP_LIMIT))
    gate_soft = CLAMP_LIMIT * gate_tanh
    up_one = CLAMP_LIMIT * up_tanh + 1.0
    sigmoid = 1.0 / (1.0 + jnp.exp(-GLU_SLOPE * gate_soft))
    swish = gate_soft * sigmoid
    act = (up_one * swish).astype(LOW)
    act_ref[...] = act
    act_gated_ref[:, :hidden] = (act.astype(F32) * gate).astype(LOW)
    spare = act_gated_ref.shape[1] - hidden
    act_gated_ref[:, hidden:] = jnp.broadcast_to(gate.astype(LOW), (act.shape[0], spare))
    first = first_ref[:, :hidden]
    with_bias = jnp.max(first_ref[:, hidden:], axis=1, keepdims=True)
    grad_weight = jnp.sum(act.astype(F32) * first, axis=1, keepdims=True) + with_bias
    grad_act = first * gate
    swish_slope = sigmoid + GLU_SLOPE * swish * (1.0 - sigmoid)
    grad_gate = (grad_act * up_one * swish_slope * (1.0 - gate_tanh * gate_tanh)).astype(LOW)
    grad_up = (grad_act * swish * (1.0 - up_tanh * up_tanh)).astype(LOW)
    grad_gate_ref[...] = grad_gate
    grad_up_ref[...] = grad_up
    grad_far = dot(grad_gate, gate_ref[:, split:]) + dot(grad_up, up_ref[:, split:])
    grad_far_ref[:, :rest] = grad_far.astype(LOW)
    high = grad_weight.astype(LOW).astype(F32)
    lanes = lane_index(mine.shape)
    spread = jnp.where(lanes < experts, high, grad_weight - high) * mine
    grad_far_ref[:, rest:] = spread.astype(LOW)
    sums = jnp.concatenate(
        [
            jnp.sum(grad_gate.astype(F32), axis=0, keepdims=True),
            jnp.sum(grad_up.astype(F32), axis=0, keepdims=True),
        ],
        axis=0,
    )
    is_first = pl.program_id(0) == 0
    bias_sums_ref[...] = jnp.where(is_first, 0.0, bias_sums_ref[...]) + sums


def expert_step(place, near, far, first, gate, up, gate_bias, up_bias, mine, experts):
    count = far.shape[0]
    hidden, features = gate.shape
    block = count // 4
    rest = features - sum(one.shape[1] for one in near)
    gated = round_up(hidden + 8, 128)
    hidden_rows = jax.ShapeDtypeStruct((count, hidden), LOW)
    return pl.pallas_call(
        functools.partial(expert_kernel, experts, len(near)),
        grid=(count // block,),
        out_shape=(
            jax.ShapeDtypeStruct(far.shape, LOW),
            hidden_rows,
            jax.ShapeDtypeStruct((count, gated), LOW),
            hidden_rows,
            hidden_rows,
            jax.ShapeDtypeStruct((2, hidden), F32),
            jax.ShapeDtypeStruct((count, features), LOW),
        ),
        in_specs=[IN_SMEM]
        + [by_row(block, one.shape[1]) for one in near]
        + [
            by_row(block, far.shape[1]),
            by_row(block, first.shape[1]),
            whole_block(hidden, features),
            whole_block(hidden, features),
            whole_block(1, hidden),
            whole_block(1, hidden),
            whole_block(1, mine.shape[1]),
        ],
        out_specs=(
            by_row(block, far.shape[1]),
            by_row(block, hidden),
            by_row(block, gated),
            by_row(block, hidden),
            by_row(block, hidden),
            whole_block(2, hidden),
            by_row(block, features),
        ),
        scratch_shapes=[pltpu.VMEM((block, features - rest), LOW)],
        compiler_params=kernel_params(),
        cost_estimate=pl.CostEstimate(
            flops=8 * count * features * hidden,
            bytes_accessed=8 * count * features + 4 * features * hidden + 12 * count * hidden,
            transcendentals=3 * count * hidden,
        ),
        name="expert_step",
    )(place, *near, far, first, gate, up, gate_bias, up_bias, mine)


def grad_rows_kernel(grad_gate_ref, grad_up_ref, gate_ref, up_ref, out_ref):
    out = dot(grad_gate_ref[...], gate_ref[...]) + dot(grad_up_ref[...], up_ref[...])
    out_ref[...] = out.astype(LOW)


def grad_rows_near(grad_gate, grad_up, gate, up, split):
    count, hidden = grad_gate.shape
    block = count // 4
    return pl.pallas_call(
        grad_rows_kernel,
        grid=(count // block,),
        out_shape=jax.ShapeDtypeStruct((count, split), LOW),
        in_specs=[
            by_row(block, hidden),
            by_row(block, hidden),
            whole_block(hidden, split),
            whole_block(hidden, split),
        ],
        out_specs=by_row(block, split),
        compiler_params=kernel_params(),
        cost_estimate=SHORT,
        name="grad_rows",
    )(grad_gate, grad_up, gate, up)


def weight_grad_kernel(left_ref, right_ref, out_ref, *refs):
    bias_ref, turned_ref = refs if len(refs) == 2 else (None, refs[0])

    @pl.when(pl.program_id(0) == 0)
    def _():
        turned_ref[...] = left_ref[...].T

    hidden = out_ref.shape[0]
    product = dot(turned_ref[...], right_ref[...])
    out_ref[...] = product[:hidden]
    if bias_ref is not None:
        bias_ref[...] = product[hidden : hidden + 8]


def weight_grad(left, right, hidden):
    count, width = left.shape
    features = right.shape[1]
    block = round_up(-(-features // STEPS), 128)
    out_shape = [jax.ShapeDtypeStruct((hidden, features), F32)]
    out_specs = [by_column(hidden, block)]
    if width > hidden:
        out_shape.append(jax.ShapeDtypeStruct((8, features), F32))
        out_specs.append(by_column(8, block))
    return pl.pallas_call(
        weight_grad_kernel,
        grid=(STEPS,),
        out_shape=out_shape,
        in_specs=[whole_block(count, width), by_column(count, block)],
        out_specs=out_specs,
        scratch_shapes=[pltpu.VMEM((width, count), LOW)],
        compiler_params=kernel_params(),
        cost_estimate=SHORT,
        name="weight_grad",
    )(left, right)


def exchange(rows, parts):
    count, width = rows.shape
    moved = lax.all_to_all(
        rows.reshape(parts, count // parts, width),
        "expert",
        split_axis=0,
        concat_axis=0,
        tiled=True,
    )
    return moved.reshape(count, width)


def low_sum(halves):
    upper, upper_in, lower, lower_in = halves
    return (
        (upper.astype(F32) + upper_in.astype(F32)).astype(LOW),
        (lower.astype(F32) + lower_in.astype(F32)).astype(LOW),
    )


def tensor_sum(upper, lower, ring, middle=low_sum):
    near = [(i, i ^ 1) for i in range(ring)]
    far = [(i, ring - 1 - i) for i in range(ring)]
    upper_in = lax.ppermute(upper, "tensor", near)
    lower_in = lax.ppermute(lower, "tensor", far)
    upper, lower = middle((upper, upper_in, lower, lower_in))
    upper_in = lax.ppermute(upper, "tensor", far)
    lower_in = lax.ppermute(lower, "tensor", near)
    return upper, upper_in, lower, lower_in


def together(*values):
    return lax.optimization_barrier(values)


def ring_steps(ring):
    return [(i, (i + 1) % ring) for i in range(ring)], [(i, (i - 1) % ring) for i in range(ring)]


def tensor_chunks(own, ring):
    up, down = ring_steps(ring)
    half = own.shape[0] // 2
    before = lax.ppermute(own, "tensor", up)
    behind = lax.ppermute(own, "tensor", down)
    far_top = lax.ppermute(before[:half], "tensor", up)
    far_bottom = lax.ppermute(behind[half:], "tensor", down)
    across = jnp.concatenate([far_top, far_bottom], axis=0)
    return own, behind, across, before


def tensor_chunks_short(own, ring):
    across = [(i, (i + 2) % ring) for i in range(ring)]
    up, down = ring_steps(ring)
    before = lax.ppermute(own, "tensor", up)
    behind = lax.ppermute(own, "tensor", down)
    return own, behind, lax.ppermute(own, "tensor", across), before


def expert_sum(values, count):
    masks = {32: (1, 2, 6, 8, 24)}.get(count) or [1 << i for i in range(count.bit_length() - 1)]
    for mask in masks:
        there = lax.ppermute(values, "expert", [(i, i ^ mask) for i in range(count)])
        values = (values.astype(F32) + there.astype(F32)).astype(values.dtype)
    return values


def on_device(
    expert_axis,
    tensor_axis,
    block_input,
    out_cotangent,
    seq_lengths,
    route_ids,
    attn_gain,
    w_query,
    w_key,
    w_value,
    b_query,
    b_key,
    b_value,
    sink_logits,
    w_output,
    b_output,
    ffn_gain,
    w_router,
    b_router,
    w_gate,
    w_up,
    b_gate,
    b_up,
    w_down,
    b_down,
):
    tokens, features = block_input.shape
    heads = sink_logits.shape[0]
    experts = w_router.shape[1]
    capacity = 2 * tokens * route_ids.shape[1] // experts
    slots = experts * capacity
    shard = w_query.shape[0]
    shard_pad = round_up(shard + 1, 16)
    width = round_up(features + 2 * experts, 128)
    chunk = max(1, round(width / 128 / (2 * tensor_axis))) * 128
    split = chunk * tensor_axis
    rest = features - split
    block_width = round_up(-(-features // tensor_axis), 128)
    mine_expert = lax.axis_index("expert")
    mine_tensor = lax.axis_index("tensor")

    out_width = w_output.shape[0]
    packed = jnp.concatenate([w_output.T, w_query, w_key, w_value], axis=1)
    packed = jnp.pad(packed, ((0, shard_pad - shard), (0, 0)))
    weights = lax.all_gather(packed, "expert", axis=0, tiled=True)

    expert_ids = jnp.arange(experts, dtype=jnp.int32)
    named = jnp.any(route_ids[:, :, None] == expert_ids[None, None, :], axis=1)
    named_t = jnp.any(route_ids.T[:, None, :] == expert_ids[None, :, None], axis=0)
    token_ids = jnp.arange(tokens, dtype=jnp.int32)
    earlier = (token_ids[:, None] < token_ids[None, :]).astype(LOW)
    rank_t = dot(named_t.astype(LOW), earlier).astype(jnp.int32)
    place = (rank_t[:, None, :] == jnp.arange(capacity, dtype=jnp.int32)[None, :, None]) & named_t[
        :, None, :
    ]
    place = place.astype(LOW).reshape(slots, tokens)
    place_t = place.T


    def own_block(rows, size, ahead=0):
        start = (mine_tensor + ahead) % tensor_axis * size
        return lax.dynamic_slice(rows, (0, start), (tokens, size))

    cotangent_wide = jnp.pad(
        out_cotangent, ((0, 0), (0, block_width * tensor_axis - features))
    )
    cotangent_own = exchange(place_rows(place, own_block(cotangent_wide, block_width)), experts)
    up, down_ring = ring_steps(tensor_axis)
    cotangent_before = lax.ppermute(cotangent_own, "tensor", up)
    cotangent_behind = lax.ppermute(cotangent_own, "tensor", down_ring)
    cotangent_across = place_rows(place, own_block(cotangent_wide, block_width, 2))

    segment, position = layout(seq_lengths[0], tokens)
    cos, sin = rope_tables(position)
    allowed = (segment[:, None] == segment[None, :]) & (token_ids[None, :] <= token_ids[:, None])
    allowed = allowed.astype(F32)

    inputs = block_input.astype(F32)
    scale_one = lax.rsqrt(jnp.mean(inputs * inputs, axis=-1, keepdims=True) + EPSILON)
    unit_one = inputs * scale_one
    unit_spread = jnp.pad(
        unit_one.reshape(tokens, expert_axis, shard), ((0, 0), (0, 0), (0, shard_pad - shard))
    ).reshape(tokens, expert_axis * shard_pad)
    normed_low = (unit_one * attn_gain).astype(LOW)
    spread_low = jnp.pad(
        normed_low.reshape(tokens, expert_axis, shard), ((0, 0), (0, 0), (0, shard_pad - shard))
    )
    one_column = (jnp.arange(shard_pad) == shard).astype(LOW)
    normed_blocks = jnp.transpose(spread_low + one_column, (1, 2, 0))
    normed_blocks = normed_blocks.reshape(expert_axis * shard_pad, tokens)

    weights, cotangent_across, cotangent_own, cotangent_before, cotangent_behind = together(
        weights, cotangent_across, cotangent_own, cotangent_before, cotangent_behind
    )
    cotangent_across = exchange(cotangent_across, experts)
    bias = jnp.concatenate([b_query, b_key, b_value])[None, :]
    spread_low = spread_low.reshape(tokens, expert_axis * shard_pad)
    attn_low, rotated, lse = attend_forward(
        sink_logits, spread_low, weights, bias, cos, sin, allowed
    )
    attn_all = lax.all_gather(attn_low, "expert", axis=0, tiled=True)
    attn_part = compact_product(attn_low, tokens, weights, out_width, shard, shard_pad, "attn_output")
    attn_sum = tensor_sum(*attn_part, tensor_axis)
    ring_place = mine_tensor.astype(jnp.int32).reshape(1)
    residual, gates, sent, rows_own = token_forward(
        ring_place,
        block_input,
        attn_sum,
        b_output[None, :],
        ffn_gain[None, :],
        w_router.T,
        b_router[None, :],
        named.astype(F32),
        place,
        width,
        chunk,
    )

    gate_t, up_t, down = w_gate[0].T, w_up[0].T, w_down[0]
    hidden = down.shape[0]
    bias_once = jnp.where(mine_tensor == 0, b_down, 0.0)
    rows_own, cotangent_across = together(rows_own, cotangent_across)
    cotangent_rows = (cotangent_own, cotangent_behind, cotangent_across, cotangent_before)
    first, cotangent_all = grad_hidden_product(ring_place, cotangent_rows, down, bias_once)
    rows_own = exchange(rows_own, experts)
    rows_far = place_rows(place, sent[:, split:])
    rows_own, rows_far, first = together(rows_own, rows_far, first)
    rows_near = tensor_chunks(rows_own, tensor_axis)
    rows_far = exchange(rows_far, experts)

    lane = jnp.arange(width - features)
    mine = ((lane % experts == mine_expert) & (lane < 2 * experts)).astype(F32)[None, :]
    rows_near, rows_far, attn_all = together(rows_near, rows_far, attn_all)
    grad_far, act, act_gated, grad_gate, grad_up, bias_sums, rows_all = expert_step(
        ring_place, rows_near, rows_far, first, gate_t, up_t, b_gate, b_up, mine, experts
    )
    back_far = exchange(grad_far, experts)
    grad_near = grad_rows_near(grad_gate, grad_up, gate_t, up_t, split)
    result = expert_result(act, down, bias_once, tensor_axis, block_width)
    result_own = lax.psum_scatter(result, "tensor", scatter_dimension=0, tiled=False)
    grad_near, back_far, grad_gate, grad_up, act_gated = together(
        grad_near, back_far, grad_gate, grad_up, act_gated
    )
    back_near = exchange(grad_near, experts)
    far_halves = combine_far(place_t, back_far, rest, experts)
    w_gate_grad = weight_grad(grad_gate, rows_all, hidden)[0]

    def middle(halves):
        nonlocal w_gate_grad, grad_up, act_gated
        *halves, w_gate_grad = together(*halves, w_gate_grad)
        upper, lower = middle_far(halves, rest, experts)
        upper, lower, grad_up, act_gated = together(upper, lower, grad_up, act_gated)
        return upper, lower

    far_sum = tensor_sum(*far_halves, tensor_axis, middle)
    w_up_grad = weight_grad(grad_up, rows_all, hidden)[0]
    w_down_grad, b_down_grad = weight_grad(act_gated, cotangent_all, hidden)
    back_near, w_up_grad, w_down_grad, b_down_grad, result_own, *far_sum = together(
        back_near, w_up_grad, w_down_grad, b_down_grad, result_own, *far_sum
    )
    w_gate_grad, w_up_grad = w_gate_grad.T[None], w_up_grad.T[None]
    w_down_grad, b_down_grad = w_down_grad[None], b_down_grad[0:1]
    returned = exchange(result_own, experts)
    b_gate_grad = bias_sums[0:1]
    b_up_grad = bias_sums[1:2]

    near_sum = tensor_sum(*combine_near(place_t, back_near), tensor_axis)
    grad_resid, resid_spread, resid_blocks, router_block, vectors = token_backward(
        ring_place,
        near_sum,
        far_sum,
        gates,
        w_router.T,
        residual,
        out_cotangent,
        ffn_gain[None, :],
        shard,
        shard_pad,
        tensor_axis,
    )
    resid_spread, returned = together(resid_spread, returned)
    grad_qkv, sink_part = attend_backward(
        sink_logits, resid_spread, weights, rotated, lse, cos, sin, allowed
    )
    grad_qkv_all = lax.all_gather(grad_qkv, "expert", axis=0, tiled=True)
    upper, lower, attn_gain_part = compact_product(
        grad_qkv, tokens, weights, weights.shape[1], shard, shard_pad, "grad_normed", unit_spread
    )
    grad_normed = tensor_sum(upper, lower, tensor_axis)
    upper, upper_in, lower, lower_in = (one.astype(F32) for one in grad_normed)
    grad_normed = jnp.concatenate([upper + upper_in, lower + lower_in], axis=0)

    normed_blocks = normed_blocks.reshape(expert_axis, shard_pad, tokens)
    blocks = jnp.concatenate([normed_blocks, resid_blocks], axis=1)
    blocks = exchange(blocks.reshape(expert_axis * 2 * shard_pad, tokens), expert_axis)
    blocks = blocks.reshape(expert_axis, 2 * shard_pad, tokens)

    sinks_row = jnp.pad(sink_part[:, :heads], ((0, 0), (0, tokens - heads)))
    small = expert_sum(pack_small(router_block, vectors, attn_gain_part, sinks_row), expert_axis)
    shared = experts + -(-features // block_width)
    widths = (w_query.shape[1], w_key.shape[1], w_value.shape[1])
    (w_output_grad,) = gathered_products(
        blocks, 1, attn_all, (out_width,), shard, shard_pad, False, "output_grad"
    )
    w_output_grad = w_output_grad.T
    qkv_grads = list(gathered_products(
        blocks, 0, grad_qkv_all, widths, shard, shard_pad, True, "qkv_grad"
    ))
    chunks = tensor_chunks_short(small[:shared], tensor_axis)
    *chunks, qkv_grads[0] = together(*chunks, qkv_grads[0])
    router_grad, gain_grad, ffn_gain_grad, output_bias_grad, sink_grad, router_bias_grad = (
        unpack_small(ring_place, chunks, small[shared:], experts, features, tokens)
    )

    grad_normed = grad_normed * attn_gain
    input_grad = grad_resid + scale_one * (
        grad_normed - unit_one * jnp.mean(unit_one * grad_normed, axis=-1, keepdims=True)
    )

    weighted = place.reshape(experts, capacity, tokens).astype(F32) * gates.T[:, None, :]
    weighted = weighted.astype(LOW).reshape(slots, tokens)
    mixed = tensor_chunks_short(dot(weighted, returned, TN).astype(LOW), tensor_axis)
    block_output = output_rows(ring_place, mixed, residual)

    return (
        block_output,
        input_grad,
        gain_grad[0],
        qkv_grads[0],
        qkv_grads[1],
        qkv_grads[2],
        qkv_grads[3][0],
        qkv_grads[4][0],
        qkv_grads[5][0],
        sink_grad[0, :heads],
        w_output_grad,
        output_bias_grad[0],
        ffn_gain_grad[0],
        router_grad.T,
        router_bias_grad[0, :experts],
        w_gate_grad,
        w_up_grad,
        b_gate_grad,
        b_up_grad,
        w_down_grad,
        b_down_grad,
    )


def solution(mesh):
    in_specs = (
        P("expert", None),
        P("expert", None),
        P("expert", None),
        P("expert", None),
        P(),
        P("expert", "tensor"),
        P("expert", "tensor"),
        P("expert", "tensor"),
        P("tensor"),
        P("tensor"),
        P("tensor"),
        P("tensor"),
        P("tensor", "expert"),
        P(),
        P(),
        P(),
        P(),
        P("expert", None, "tensor"),
        P("expert", None, "tensor"),
        P("expert", "tensor"),
        P("expert", "tensor"),
        P("expert", "tensor", None),
        P("expert", None),
    )
    out_specs = (
        P("expert", None),
        P("expert", None),
        P(),
        P("expert", "tensor"),
        P("expert", "tensor"),
        P("expert", "tensor"),
        P("tensor"),
        P("tensor"),
        P("tensor"),
        P("tensor"),
        P("tensor", "expert"),
        P(),
        P(),
        P(),
        P(),
        P("expert", None, "tensor"),
        P("expert", None, "tensor"),
        P("expert", "tensor"),
        P("expert", "tensor"),
        P("expert", "tensor", None),
        P("expert", None),
    )
    body = functools.partial(on_device, mesh.shape["expert"], mesh.shape["tensor"])
    return jax.shard_map(body, mesh=mesh, in_specs=in_specs, out_specs=out_specs, check_vma=False)
```

```python
import functools

import jax
import jax.numpy as jnp
from jax import lax
from jax.experimental import pallas as pl
from jax.experimental.pallas import tpu as pltpu
from jax.sharding import PartitionSpec as P

HD = 64
PAIR = 2 * HD
EPSILON = 1e-05
ROPE_BASE = 150000.0
CLAMP_LIMIT = 7.0
GLU_SLOPE = 1.702
MASKED = -1e30
PRECISE = lax.Precision.HIGHEST
LOW = jnp.bfloat16
F32 = jnp.float32
VMEM_BYTES = 56 * 1024 * 1024
NN = (((1,), (0,)), ((), ()))
NT = (((1,), (1,)), ((), ()))
TN = (((0,), (0,)), ((), ()))


def round_up(value, unit):
    return -(-value // unit) * unit


def dot(left, right, dims=NN):
    return lax.dot_general(left, right, dims, preferred_element_type=F32)


def split_low(values):
    high = values.astype(LOW)
    return high, (values - high.astype(F32)).astype(LOW)


def layout(lengths, tok_count):
    seq_ends = jnp.cumsum(lengths)
    tok_index = jnp.arange(tok_count, dtype=jnp.int32)
    is_past = tok_index[:, None] >= seq_ends[None, :]
    segment = jnp.sum(is_past.astype(jnp.int32), axis=1)
    offset = jnp.sum(jnp.where(is_past, lengths[None, :], 0), axis=1)
    return (segment, tok_index - offset)


def rope_tables(position):
    half = HD // 2
    frequency = ROPE_BASE ** (-(jnp.arange(half).astype(F32) * 2.0 / HD))
    angles = position.astype(F32)[:, None] * frequency[None, :]
    cosine, sine = jnp.cos(angles), jnp.sin(angles)
    return (
        jnp.concatenate([cosine] * 4, axis=1),
        jnp.concatenate([-sine, sine, -sine, sine], axis=1),
    )


def lane_index(shape):
    return lax.broadcasted_iota(jnp.int32, shape, len(shape) - 1)


def swap_halves(values):
    first = (lane_index(values.shape) % HD) < HD // 2
    return jnp.where(
        first, pltpu.roll(values, PAIR - HD // 2, 1), pltpu.roll(values, HD // 2, 1)
    )


def twin(values, which):
    turned = pltpu.roll(values, HD, 1)
    left = lane_index(values.shape) < HD
    return jnp.where(left, values, turned) if which == 0 else jnp.where(left, turned, values)


def attend_forward_kernel(
    sink_ref,
    rows_ref,
    weights_ref,
    bias_ref,
    cos_ref,
    sin_ref,
    allowed_ref,
    out_ref,
    rot_ref,
    lse_ref,
    qkv_ref,
):
    step = pl.program_id(0)
    start = weights_ref.shape[1] - qkv_ref.shape[1]
    part = dot(rows_ref[...], weights_ref[:, start:])

    @pl.when(step == 0)
    def _():
        qkv_ref[...] = part + bias_ref[...]

    @pl.when(step > 0)
    def _():
        qkv_ref[...] += part

    @pl.when(step == pl.num_programs(0) - 1)
    def _():
        attend(
            sink_ref, qkv_ref, cos_ref, sin_ref, allowed_ref, out_ref, rot_ref, lse_ref
        )


def attend(sink_ref, qkv_ref, cos_ref, sin_ref, allowed_ref, out_ref, rot_ref, lse_ref):
    tokens = qkv_ref.shape[0]
    heads = sink_ref.shape[0]
    key_at = heads * HD
    value_at = key_at + PAIR
    per_group = heads // 2
    cos, sin = cos_ref[...], sin_ref[...]
    allowed = allowed_ref[...] > 0.5
    left = lane_index((tokens, PAIR)) < HD
    lanes = lane_index((tokens, PAIR))

    def rope(values):
        return values * cos + swap_halves(values) * sin

    key = rope(qkv_ref[:, key_at:value_at])
    value = qkv_ref[:, value_at : value_at + PAIR]
    rot_ref[:, key_at:value_at] = key.astype(LOW)
    rot_ref[:, value_at : value_at + PAIR] = value.astype(LOW)
    keys = [twin(key, g).astype(LOW) for g in range(2)]
    values = [twin(value, g).astype(LOW) for g in range(2)]
    lse_all = jnp.zeros((tokens, PAIR), F32)
    for pair in range(heads // 2):
        cols = slice(pair * PAIR, (pair + 1) * PAIR)
        group = (2 * pair) // per_group
        query = rope(qkv_ref[:, cols])
        rot_ref[:, cols] = query.astype(LOW)
        outs = []
        for side in range(2):
            head = 2 * pair + side
            mine = left if side == 0 else jnp.logical_not(left)
            one = jnp.where(mine, query, 0.0).astype(LOW)
            scores = dot(one, keys[group], NT) * HD ** (-0.5)
            scores = jnp.where(allowed, scores, MASKED)
            sink = sink_ref[head]
            top = jnp.maximum(jnp.max(scores, axis=1, keepdims=True), sink)
            weights = jnp.exp(scores - top)
            denom = jnp.sum(weights, axis=1, keepdims=True) + jnp.exp(sink - top)
            lse = top + jnp.log(denom)
            lse_all = jnp.where(lanes == head, lse, lse_all)
            prob = (weights / denom).astype(LOW)
            outs.append(dot(prob, values[group]))
        out_ref[:, cols] = jnp.where(left, outs[0], outs[1]).astype(LOW)
    lse_ref[...] = lse_all


def attend_backward_kernel(
    sink_ref,
    rows_ref,
    weights_ref,
    rot_ref,
    lse_ref,
    cos_ref,
    sin_ref,
    allowed_ref,
    out_ref,
    sink_out_ref,
    sum_ref,
    grad_ref,
):
    step = pl.program_id(0)
    part = dot(rows_ref[...], weights_ref[...])

    @pl.when(step == 0)
    def _():
        sum_ref[...] = part

    @pl.when(step > 0)
    def _():
        sum_ref[...] += part

    @pl.when(step == pl.num_programs(0) - 1)
    def _():
        grad_ref[...] = sum_ref[...].astype(LOW)
        attend_back(
            sink_ref,
            rot_ref,
            grad_ref,
            lse_ref,
            cos_ref,
            sin_ref,
            allowed_ref,
            out_ref,
            sink_out_ref,
        )


def attend_back(
    sink_ref, rot_ref, grad_ref, lse_ref, cos_ref, sin_ref, allowed_ref, out_ref, sink_out_ref
):
    tokens = rot_ref.shape[0]
    heads = sink_ref.shape[0]
    key_at = heads * HD
    value_at = key_at + PAIR
    per_group = heads // 2
    scale = HD ** (-0.5)
    cos, sin = cos_ref[...], sin_ref[...]
    allowed = allowed_ref[...] > 0.5
    lanes = lane_index((tokens, PAIR))
    left = lanes < HD

    def turn_back(values):
        return values * cos - swap_halves(values) * sin

    key = rot_ref[:, key_at:value_at].astype(F32)
    value = rot_ref[:, value_at : value_at + PAIR].astype(F32)
    keys = [twin(key, g).astype(LOW) for g in range(2)]
    values = [twin(value, g).astype(LOW) for g in range(2)]
    key_sums = [jnp.zeros((tokens, PAIR), F32) for _ in range(2)]
    value_sums = [jnp.zeros((tokens, PAIR), F32) for _ in range(2)]
    sink_all = jnp.zeros((tokens, PAIR), F32)
    lse_all = lse_ref[...]
    for pair in range(heads // 2):
        cols = slice(pair * PAIR, (pair + 1) * PAIR)
        group = (2 * pair) // per_group
        query = rot_ref[:, cols].astype(F32)
        grad = grad_ref[:, cols].astype(F32)
        outs = []
        for side in range(2):
            head = 2 * pair + side
            mine = left if side == 0 else jnp.logical_not(left)
            one = jnp.where(mine, query, 0.0).astype(LOW)
            grad_one = jnp.where(mine, grad, 0.0).astype(LOW)
            lse = jnp.sum(jnp.where(lanes == head, lse_all, 0.0), axis=1, keepdims=True)
            scores = dot(one, keys[group], NT) * scale
            prob = jnp.where(allowed, jnp.exp(jnp.where(allowed, scores - lse, 0.0)), 0.0)
            grad_prob = dot(grad_one, values[group], NT)
            delta = jnp.sum(prob * grad_prob, axis=1, keepdims=True)
            grad_score = (prob * (grad_prob - delta)).astype(LOW)
            outs.append(dot(grad_score, keys[group]))
            key_sums[group] += dot(grad_score, one, TN)
            value_sums[group] += dot(prob.astype(LOW), grad_one, TN)
            sink_all = jnp.where(lanes == head, jnp.exp(sink_ref[head] - lse) * delta, sink_all)
        out_ref[:tokens, cols] = turn_back(jnp.where(left, outs[0], outs[1]) * scale).astype(LOW)

    def fold(sums):
        both = [one + pltpu.roll(one, HD, 1) for one in sums]
        return jnp.where(left, both[0], both[1])

    out_ref[:tokens, key_at:value_at] = turn_back(fold(key_sums) * scale).astype(LOW)
    out_ref[:tokens, value_at : value_at + PAIR] = fold(value_sums).astype(LOW)
    sink_out_ref[...] = -jnp.sum(sink_all, axis=0, keepdims=True)


def kernel_params():
    return pltpu.CompilerParams(vmem_limit_bytes=VMEM_BYTES)


SHORT = pl.CostEstimate(flops=1, bytes_accessed=1, transcendentals=0)
IN_VMEM = pl.BlockSpec(memory_space=pltpu.VMEM)
IN_SMEM = pl.BlockSpec(memory_space=pltpu.SMEM)


def by_row(block, columns):
    return pl.BlockSpec((block, columns), lambda i: (i, 0))


def by_column(rows, block):
    return pl.BlockSpec((rows, block), lambda i: (0, i))


def whole_block(*shape):
    return pl.BlockSpec(shape, lambda i: (0, 0))


def held_block(*shape):
    return pl.BlockSpec(shape, lambda i: (0, 0), pipeline_mode=pl.Buffered(1))


STEPS = 4


def attend_forward(sinks, rows, weights, bias, cos, sin, allowed):
    tokens, inner = rows.shape
    width = bias.shape[1]
    heads = sinks.shape[0]
    block = inner // STEPS
    return pl.pallas_call(
        attend_forward_kernel,
        grid=(STEPS,),
        out_shape=(
            jax.ShapeDtypeStruct((tokens, heads * HD), LOW),
            jax.ShapeDtypeStruct((tokens, width), LOW),
            jax.ShapeDtypeStruct((tokens, PAIR), F32),
        ),
        in_specs=[
            IN_SMEM,
            by_column(tokens, block),
            by_row(block, weights.shape[1]),
            whole_block(1, width),
            whole_block(*cos.shape),
            whole_block(*sin.shape),
            whole_block(*allowed.shape),
        ],
        out_specs=(
            whole_block(tokens, heads * HD),
            whole_block(tokens, width),
            whole_block(tokens, PAIR),
        ),
        scratch_shapes=[pltpu.VMEM((tokens, width), F32)],
        compiler_params=kernel_params(),
        cost_estimate=SHORT,
        name="attend_forward",
    )(sinks, rows, weights, bias, cos, sin, allowed)


def attend_backward(sinks, rows, weights, rotated, lse, cos, sin, allowed):
    tokens, width = rotated.shape
    inner = rows.shape[1]
    out_width = sinks.shape[0] * HD
    block = inner // STEPS
    return pl.pallas_call(
        attend_backward_kernel,
        grid=(STEPS,),
        out_shape=(
            jax.ShapeDtypeStruct((tokens, width), LOW),
            jax.ShapeDtypeStruct((1, PAIR), F32),
        ),
        in_specs=[
            IN_SMEM,
            by_column(tokens, block),
            by_row(block, out_width),
            whole_block(tokens, width),
            whole_block(*lse.shape),
            whole_block(*cos.shape),
            whole_block(*sin.shape),
            whole_block(*allowed.shape),
        ],
        out_specs=(whole_block(tokens, width), whole_block(1, PAIR)),
        scratch_shapes=[pltpu.VMEM((tokens, out_width), F32), pltpu.VMEM((tokens, out_width), LOW)],
        compiler_params=kernel_params(),
        cost_estimate=SHORT,
        name="attend_backward",
    )(sinks, rows, weights, rotated, lse, cos, sin, allowed)


def compact_kernel(shard, shard_pad, left_ref, weights_ref, *refs):
    unit_ref, upper_ref, lower_ref, gain_ref = refs if len(refs) == 4 else (None, *refs, None)
    start = weights_ref.shape[1] - left_ref.shape[1]
    product = dot(left_ref[...], weights_ref[:, start:], NT)
    half = upper_ref.shape[0]
    shards = weights_ref.shape[0] // shard_pad
    if gain_ref is not None:
        gain = jnp.sum(product * unit_ref[...].astype(F32), axis=0, keepdims=True)
    for step in range(upper_ref.shape[1] // (shards * shard)):

        @pl.when(pl.program_id(0) == step)
        def _():
            for i in range(shards):
                piece = product[:, i * shard_pad : i * shard_pad + shard].astype(LOW)
                at = (step * shards + i) * shard
                upper_ref[:, at : at + shard] = piece[:half]
                lower_ref[:, at : at + shard] = piece[half:]
                if gain_ref is not None:
                    pad_at = i * shard_pad
                    gain_ref[:, at : at + shard] = gain[:, pad_at : pad_at + shard]


def compact_product(left, tokens, weights, block_width, shard, shard_pad, name, unit=None):
    inner = left.shape[1]
    rows = weights.shape[0]
    features = rows // shard_pad * shard
    half = jax.ShapeDtypeStruct((tokens // 2, features), LOW)
    operands = [left, weights]
    in_specs = [whole_block(tokens, inner), by_row(rows // STEPS, block_width)]
    out_shape = [half, half]
    if unit is not None:
        operands.append(unit)
        in_specs.append(by_column(tokens, rows // STEPS))
        out_shape.append(jax.ShapeDtypeStruct((1, features), F32))
    return pl.pallas_call(
        functools.partial(compact_kernel, shard, shard_pad),
        grid=(STEPS,),
        out_shape=out_shape,
        in_specs=in_specs,
        out_specs=[whole_block(*one.shape) for one in out_shape],
        compiler_params=kernel_params(),
        cost_estimate=SHORT,
        name=name,
    )(*operands)


def rms_scale(values):
    return lax.rsqrt(jnp.mean(values * values, axis=1, keepdims=True) + EPSILON)


def join_halves(halves, out_ref):
    upper, upper_in, lower, lower_in = halves
    half = upper.shape[0]
    out_ref[:half, :] = upper[...].astype(F32) + upper_in[...].astype(F32)
    out_ref[half:, :] = lower[...].astype(F32) + lower_in[...].astype(F32)


def token_forward_kernel(place_ref, input_ref, *refs):
    halves, refs = refs[:4], refs[4:]
    bias_ref, gain_ref, router_ref, router_bias_ref, named_ref, slots_ref = refs[:6]
    resid_ref, gates_ref, sent_ref, own_ref = refs[6:]
    features = input_ref.shape[1]
    experts = router_ref.shape[0]
    chunk = own_ref.shape[1]
    join_halves(halves, resid_ref)
    resid = input_ref[...].astype(F32) + resid_ref[...] + bias_ref[...]
    resid_ref[...] = resid
    normed = resid * rms_scale(resid) * gain_ref[...]
    logits = lax.dot_general(
        normed, router_ref[...], NT, precision=PRECISE, preferred_element_type=F32
    )
    named = named_ref[...] > 0.5
    logits = jnp.where(named, logits + router_bias_ref[...], MASKED)
    weights = jnp.exp(logits - jnp.max(logits, axis=1, keepdims=True))
    weights = jnp.where(named, weights, 0.0)
    gates = weights / jnp.sum(weights, axis=1, keepdims=True)
    gates_ref[...] = gates
    high, low = split_low(gates)
    sent_ref[:, :features] = normed.astype(LOW)
    sent_ref[:, features : features + experts] = high
    sent_ref[:, features + experts : features + 2 * experts] = low
    spare = sent_ref.shape[1] - features - 2 * experts
    if spare:
        sent_ref[:, features + 2 * experts :] = jnp.zeros((resid.shape[0], spare), LOW)
    own = sent_ref[:, pl.ds(pl.multiple_of(place_ref[0] * chunk, 128), chunk)]
    own_ref[...] = dot(slots_ref[...], own).astype(LOW)


def token_forward(place, inputs, halves, bias, gain, router, router_bias, named, slots, width, chunk):
    tokens, features = inputs.shape
    experts = router.shape[0]
    return pl.pallas_call(
        token_forward_kernel,
        out_shape=(
            jax.ShapeDtypeStruct((tokens, features), F32),
            jax.ShapeDtypeStruct((tokens, experts), F32),
            jax.ShapeDtypeStruct((tokens, width), LOW),
            jax.ShapeDtypeStruct((slots.shape[0], chunk), LOW),
        ),
        in_specs=[IN_SMEM] + [IN_VMEM] * 11,
        out_specs=(IN_VMEM,) * 4,
        compiler_params=kernel_params(),
        cost_estimate=SHORT,
        name="token_forward",
    )(place, inputs, *halves, bias, gain, router, router_bias, named, slots)


def token_backward_kernel(shard, shard_pad, place_ref, *refs):
    near_halves, halves, refs = refs[:4], refs[4:8], refs[8:]
    gates_ref, router_ref, resid_ref, cotangent_ref, gain_ref = refs[:5]
    out_ref, spread_ref, blocks_ref, router_out_ref, vectors_ref = refs[5:10]
    near_ref, far_ref, grad_ref, router_all_ref = refs[10:]
    tokens, features = resid_ref.shape
    experts = router_ref.shape[0]
    split = near_ref.shape[1]
    rest = features - split
    join_halves(near_halves, near_ref)
    join_halves(halves, far_ref)
    gates = gates_ref[...]
    grad_gates = far_ref[:, rest : rest + experts] + far_ref[:, rest + experts : rest + 2 * experts]
    grad_logits = gates * (grad_gates - jnp.sum(gates * grad_gates, axis=1, keepdims=True))
    through = lax.dot_general(
        grad_logits, router_ref[...], NN, precision=PRECISE, preferred_element_type=F32
    )
    grad_ref[:, :split] = through[:, :split] + near_ref[...]
    grad_ref[:, split:] = through[:, split:] + far_ref[:, :rest]
    grad_two = grad_ref[...]
    resid = resid_ref[...]
    scale = rms_scale(resid)
    unit = resid * scale
    gain = gain_ref[...]
    router_part = lax.dot_general(
        grad_logits, unit * gain, TN, precision=PRECISE, preferred_element_type=F32
    )
    scaled = grad_two * gain
    mean = jnp.mean(unit * scaled, axis=1, keepdims=True)
    grad_resid = cotangent_ref[...].astype(F32) + scale * (scaled - unit * mean)
    out_ref[...] = grad_resid
    vectors_ref[...] = jnp.zeros_like(vectors_ref)
    vectors_ref[0:1, :features] = jnp.sum(grad_two * unit, axis=0, keepdims=True)
    vectors_ref[1:2, :features] = jnp.sum(grad_resid, axis=0, keepdims=True)
    vectors_ref[2:3, :experts] = jnp.sum(grad_logits, axis=0, keepdims=True)
    low = grad_resid.astype(LOW)
    for i in range(features // shard):
        at = i * shard_pad
        spread_ref[:, at : at + shard] = low[:, i * shard : (i + 1) * shard]
        spread_ref[:, at + shard : at + shard_pad] = jnp.zeros((tokens, shard_pad - shard), LOW)
    turned = spread_ref[...].T
    for i in range(features // shard):
        blocks_ref[i] = turned[i * shard_pad : (i + 1) * shard_pad]
    router_all_ref[:, :features] = router_part.astype(LOW)
    spare = router_all_ref.shape[1] - features
    router_all_ref[:, features:] = jnp.zeros((router_part.shape[0], spare), LOW)
    block = router_out_ref.shape[1]
    start = pl.multiple_of(place_ref[0] * block, 128)
    router_out_ref[...] = router_all_ref[:, pl.ds(start, block)]


def pack_kernel(router_ref, vectors_ref, gain_ref, sinks_ref, out_ref):
    experts, width = router_ref.shape
    features = gain_ref.shape[1]
    out_ref[...] = jnp.zeros_like(out_ref)
    out_ref[:experts, :] = router_ref[...]
    row = experts
    for values in (gain_ref[...], vectors_ref[0:1, :features], vectors_ref[1:2, :features]):
        for at in range(0, features, width):
            piece = values[:, at : at + width].astype(LOW)
            out_ref[row : row + 1, : piece.shape[1]] = piece
            row += 1
    lanes = sinks_ref.shape[1]
    out_ref[row : row + 1, :lanes] = sinks_ref[...].astype(LOW)
    out_ref[row + 1 : row + 2, :lanes] = vectors_ref[2:3, :lanes].astype(LOW)


def pack_small(router, vectors, gain, sinks):
    experts, width = router.shape
    rows = round_up(experts + 3 * -(-gain.shape[1] // width) + 2, 16)
    return pl.pallas_call(
        pack_kernel,
        out_shape=jax.ShapeDtypeStruct((rows, width), LOW),
        in_specs=[IN_VMEM] * 4,
        out_specs=IN_VMEM,
        compiler_params=kernel_params(),
        cost_estimate=SHORT,
        name="pack_small",
    )(router, vectors, gain, sinks)


def unpack_kernel(place_ref, *refs):
    chunk_refs, (scale_ref, rest_ref), refs = refs[:4], refs[4:6], refs[6:]
    router_ref, gain_ref, first_ref, second_ref, sinks_ref, bias_ref, all_ref, vector_ref = refs
    experts, features = router_ref.shape
    width = chunk_refs[0].shape[1]
    assemble(place_ref, chunk_refs, all_ref)
    router_ref[...] = all_ref[:experts, :features].astype(F32)
    tiles = -(-features // width)
    for tile in range(tiles):
        at = tile * width
        size = min(width, features - at)
        row = experts + tile
        parts = all_ref[row : row + 1, :].astype(F32)
        total = sum(parts[:, i * width : (i + 1) * width] for i in range(4))
        vector_ref[0:1, at : at + size] = total[:, :size]
        for i in range(2):
            row = i * tiles + tile
            vector_ref[i + 1 : i + 2, at : at + size] = rest_ref[row : row + 1, :size].astype(F32)
    gain_ref[...] = (vector_ref[0:1, :] / scale_ref[...]).reshape(features)
    first_ref[...] = vector_ref[1:2, :].reshape(features)
    second_ref[...] = vector_ref[2:3, :].reshape(features)
    row = 2 * tiles
    heads, biases = sinks_ref.shape[0], bias_ref.shape[0]
    sinks_ref[...] = rest_ref[row : row + 1, :heads].astype(F32).reshape(heads)
    bias_ref[...] = rest_ref[row + 1 : row + 2, :biases].astype(F32).reshape(biases)


def unpack_small(place, chunks, rest, gain, experts, heads):
    rows, width = chunks[0].shape
    features = gain.shape[1]
    wide = jax.ShapeDtypeStruct((features,), F32)
    return pl.pallas_call(
        unpack_kernel,
        out_shape=(
            jax.ShapeDtypeStruct((experts, features), F32),
            wide,
            wide,
            wide,
            jax.ShapeDtypeStruct((heads,), F32),
            jax.ShapeDtypeStruct((experts,), F32),
        ),
        in_specs=[IN_SMEM] + [IN_VMEM] * 6,
        out_specs=(IN_VMEM,) * 6,
        scratch_shapes=[
            pltpu.VMEM((rows, len(chunks) * width), LOW),
            pltpu.VMEM((8, features), F32),
        ],
        compiler_params=kernel_params(),
        cost_estimate=SHORT,
        name="unpack_small",
    )(place, *chunks, gain, rest)


def gathered_kernel(shard, blocks_ref, rows_ref, *refs):
    *out_refs, sum_ref = refs
    blocks = blocks_ref.shape[0]
    tokens = blocks_ref.shape[2]
    total = None
    for i in range(blocks):
        rows = rows_ref[i * tokens : (i + 1) * tokens, :]
        part = dot(blocks_ref[i], rows)
        total = part if total is None else total + part
    first = pl.program_id(0) == 0

    @pl.when(first)
    def _():
        sum_ref[...] = total

    @pl.when(jnp.logical_not(first))
    def _():
        sum_ref[...] += total

    @pl.when(pl.program_id(0) == pl.num_programs(0) - 1)
    def _():
        at = 0
        for out_ref in out_refs[: len(out_refs) // 2 if len(out_refs) > 1 else 1]:
            out_ref[...] = sum_ref[:shard, at : at + out_ref.shape[1]]
            at += out_ref.shape[1]
        at = 0
        for out_ref in out_refs[len(out_refs) // 2 if len(out_refs) > 1 else 1 :]:
            size = out_ref.shape[0]
            out_ref[...] = sum_ref[shard : shard + 1, at : at + size].reshape(size)
            at += size


def gathered_products(blocks, which, rows, widths, shard, shard_pad, biases, name):
    parts, _, tokens = blocks.shape
    total, width = rows.shape
    block = parts // STEPS
    out_shape = [jax.ShapeDtypeStruct((shard, one), F32) for one in widths]
    if biases:
        out_shape += [jax.ShapeDtypeStruct((one,), F32) for one in widths]
    return pl.pallas_call(
        functools.partial(gathered_kernel, shard),
        grid=(STEPS,),
        out_shape=out_shape,
        in_specs=[
            pl.BlockSpec((block, shard_pad, tokens), lambda i: (i, which, 0)),
            by_row(total // STEPS, width),
        ],
        out_specs=[
            pl.BlockSpec(one.shape, lambda i, rank=len(one.shape): (0,) * rank)
            for one in out_shape
        ],
        scratch_shapes=[pltpu.VMEM((shard_pad, width), F32)],
        compiler_params=kernel_params(),
        cost_estimate=SHORT,
        name=name,
    )(blocks, rows)


def token_backward(
    place, near, halves, gates, router, resid, cotangent, gain, shard, shard_pad, ring
):
    tokens, features = resid.shape
    experts = router.shape[0]
    router_block = round_up(-(-features // ring), 128)
    parts = features // shard
    return pl.pallas_call(
        functools.partial(token_backward_kernel, shard, shard_pad),
        out_shape=(
            jax.ShapeDtypeStruct((tokens, features), F32),
            jax.ShapeDtypeStruct((tokens, features // shard * shard_pad), LOW),
            jax.ShapeDtypeStruct((parts, shard_pad, tokens), LOW),
            jax.ShapeDtypeStruct((experts, router_block), LOW),
            jax.ShapeDtypeStruct((8, router_block * ring), F32),
        ),
        in_specs=[IN_SMEM] + [IN_VMEM] * 13,
        out_specs=(IN_VMEM,) * 5,
        scratch_shapes=[
            pltpu.VMEM((tokens, near[0].shape[1]), F32),
            pltpu.VMEM((tokens, halves[0].shape[1]), F32),
            pltpu.VMEM((tokens, features), F32),
            pltpu.VMEM((experts, router_block * ring), LOW),
        ],
        compiler_params=kernel_params(),
        cost_estimate=SHORT,
        name="token_backward",
    )(place, *near, *halves, gates, router, resid, cotangent, gain)


def output_kernel(place_ref, *refs):
    near_refs, (resid_ref, out_ref, near_ref) = refs[:4], refs[4:]
    assemble(place_ref, near_refs, near_ref)
    near = near_ref[:, : out_ref.shape[0]].astype(F32)
    out_ref[...] = (resid_ref[...] + near).astype(LOW).T


def output_rows(place, near, resid):
    tokens, features = resid.shape
    return pl.pallas_call(
        output_kernel,
        out_shape=jax.ShapeDtypeStruct((features, tokens), LOW),
        in_specs=[IN_SMEM] + [IN_VMEM] * 5,
        out_specs=IN_VMEM,
        scratch_shapes=[pltpu.VMEM((tokens, sum(one.shape[1] for one in near)), LOW)],
        compiler_params=kernel_params(),
        cost_estimate=SHORT,
        name="output_rows",
    )(place, *near, resid)


def mix_kernel(place_ref, gates_ref, rows_ref, out_ref):
    experts, slots = gates_ref.shape[1], place_ref.shape[1]
    own = lax.broadcasted_iota(jnp.int32, (experts, slots), 1) // (slots // experts)
    own = own == lax.broadcasted_iota(jnp.int32, (experts, slots), 0)
    spread = dot(gates_ref[...].astype(LOW), own.astype(F32).astype(LOW))
    weights = (place_ref[...].astype(F32) * spread).astype(LOW)
    out_ref[...] = dot(weights, rows_ref[...]).astype(LOW)


def mix_results(place_t, gates, rows):
    return pl.pallas_call(
        mix_kernel,
        out_shape=jax.ShapeDtypeStruct((place_t.shape[0], rows.shape[1]), LOW),
        in_specs=[IN_VMEM] * 3,
        out_specs=IN_VMEM,
        compiler_params=kernel_params(),
        cost_estimate=SHORT,
        name="mix_results",
    )(place_t, gates, rows)


def input_grad_kernel(*refs):
    halves, (resid_ref, input_ref, gain_ref, out_ref, sum_ref) = refs[:4], refs[4:]
    join_halves(halves, sum_ref)
    inputs = input_ref[...].astype(F32)
    scale = rms_scale(inputs)
    unit = inputs * scale
    scaled = sum_ref[...] * gain_ref[...]
    mean = jnp.mean(unit * scaled, axis=1, keepdims=True)
    out_ref[...] = (resid_ref[...] + scale * (scaled - unit * mean)).T


def input_grad_rows(halves, resid, inputs, gain):
    tokens, features = resid.shape
    return pl.pallas_call(
        input_grad_kernel,
        out_shape=jax.ShapeDtypeStruct((features, tokens), F32),
        in_specs=[IN_VMEM] * 7,
        out_specs=IN_VMEM,
        scratch_shapes=[pltpu.VMEM((tokens, features), F32)],
        compiler_params=kernel_params(),
        cost_estimate=SHORT,
        name="input_grad",
    )(*halves, resid, inputs, gain)


def store_halves(values, rest, experts, upper_ref, lower_ref):
    half = upper_ref.shape[0]
    main = values[:, :rest].astype(LOW)
    upper_ref[:, :rest], lower_ref[:, :rest] = main[:half], main[half:]
    high, low = split_low(values[:, rest : rest + experts] + values[:, rest + experts : rest + 2 * experts])
    for out_ref, rows in ((upper_ref, slice(0, half)), (lower_ref, slice(half, 2 * half))):
        out_ref[:, rest : rest + experts] = high[rows]
        out_ref[:, rest + experts : rest + 2 * experts] = low[rows]
        spare = out_ref.shape[1] - rest - 2 * experts
        if spare:
            out_ref[:, rest + 2 * experts :] = jnp.zeros((half, spare), LOW)


def combine_kernel(rest, experts, place_ref, rows_ref, upper_ref, lower_ref):
    store_halves(dot(place_ref[...], rows_ref[...]), rest, experts, upper_ref, lower_ref)


def combine_far(place_t, rows, rest, experts):
    half = jax.ShapeDtypeStruct((place_t.shape[0] // 2, rows.shape[1]), LOW)
    return pl.pallas_call(
        functools.partial(combine_kernel, rest, experts),
        out_shape=(half, half),
        in_specs=[IN_VMEM] * 2,
        out_specs=(IN_VMEM,) * 2,
        compiler_params=kernel_params(),
        cost_estimate=SHORT,
        name="combine_far",
    )(place_t, rows)


def combine_near_kernel(place_ref, rows_ref, upper_ref, lower_ref):
    total = dot(place_ref[...], rows_ref[...]).astype(LOW)
    half = upper_ref.shape[0]
    upper_ref[...], lower_ref[...] = total[:half], total[half:]


def combine_near(place_t, rows):
    half = jax.ShapeDtypeStruct((place_t.shape[0] // 2, rows.shape[1]), LOW)
    return pl.pallas_call(
        combine_near_kernel,
        out_shape=(half, half),
        in_specs=[IN_VMEM] * 2,
        out_specs=(IN_VMEM,) * 2,
        compiler_params=kernel_params(),
        cost_estimate=SHORT,
        name="combine_near",
    )(place_t, rows)


def middle_kernel(rest, experts, *refs):
    halves, (upper_ref, lower_ref, sum_ref) = refs[:4], refs[4:]
    join_halves(halves, sum_ref)
    store_halves(sum_ref[...], rest, experts, upper_ref, lower_ref)


def middle_far(halves, rest, experts):
    half = jax.ShapeDtypeStruct(halves[0].shape, LOW)
    return pl.pallas_call(
        functools.partial(middle_kernel, rest, experts),
        out_shape=(half, half),
        in_specs=[IN_VMEM] * 4,
        out_specs=(IN_VMEM,) * 2,
        scratch_shapes=[pltpu.VMEM((2 * half.shape[0], half.shape[1]), F32)],
        compiler_params=kernel_params(),
        cost_estimate=SHORT,
        name="middle_far",
    )(*halves)


def assemble(place_ref, near_refs, out_ref):
    ring, width = len(near_refs), near_refs[0].shape[1]
    for ahead, near_ref in enumerate(near_refs):
        start = (place_ref[0] + ahead) % ring * width
        out_ref[:, pl.ds(pl.multiple_of(start, 128), width)] = near_ref[...]


def grad_hidden_kernel(place_ref, *refs):
    chunk_refs, (down_ref, bias_ref, out_ref, all_ref, rows_ref) = refs[:-5], refs[-5:]
    hidden, features = down_ref.shape
    assemble(place_ref, chunk_refs, rows_ref)
    rows = rows_ref[:, :features]
    all_ref[...] = rows
    spare = out_ref.shape[1] - hidden
    out_ref[:, :hidden] = dot(rows, down_ref[...], NT)
    with_bias = jnp.sum(rows.astype(F32) * bias_ref[...], axis=1, keepdims=True)
    out_ref[:, hidden:] = jnp.broadcast_to(with_bias, (rows.shape[0], spare))


def grad_hidden_product(place, chunks, down, bias):
    count, chunk = chunks[0].shape
    hidden, features = down.shape
    width = round_up(hidden + 1, 128)
    block = count // 4
    return pl.pallas_call(
        grad_hidden_kernel,
        grid=(count // block,),
        out_shape=(
            jax.ShapeDtypeStruct((count, width), F32),
            jax.ShapeDtypeStruct((count, features), LOW),
        ),
        in_specs=[IN_SMEM]
        + [by_row(block, chunk)] * len(chunks)
        + [whole_block(hidden, features), whole_block(1, features)],
        out_specs=(by_row(block, width), by_row(block, features)),
        scratch_shapes=[pltpu.VMEM((block, len(chunks) * chunk), LOW)],
        compiler_params=kernel_params(),
        cost_estimate=SHORT,
        name="grad_hidden",
    )(place, *chunks, down, bias)


def result_kernel(act_ref, down_ref, bias_ref, out_ref):
    parts, rows, width = out_ref.shape
    result = (dot(act_ref[...], down_ref[...]) + bias_ref[...]).astype(LOW)
    for part in range(parts):
        columns = result[:, part * width : (part + 1) * width]
        out_ref[part, :, : columns.shape[1]] = columns
        if columns.shape[1] < width:
            out_ref[part, :, columns.shape[1] :] = jnp.zeros((rows, width - columns.shape[1]), LOW)


def expert_result(act, down, bias, parts, width):
    count, hidden = act.shape
    features = down.shape[1]
    block = count // 4
    return pl.pallas_call(
        result_kernel,
        grid=(count // block,),
        out_shape=jax.ShapeDtypeStruct((parts, count, width), LOW),
        in_specs=[by_row(block, hidden), held_block(hidden, features), whole_block(1, features)],
        out_specs=pl.BlockSpec((parts, block, width), lambda i: (0, i, 0)),
        compiler_params=kernel_params(),
        cost_estimate=SHORT,
        name="expert_result",
    )(act, down, bias)


def place_kernel(place_ref, rows_ref, out_ref):
    out_ref[...] = dot(place_ref[...], rows_ref[...]).astype(LOW)


def place_rows(place, rows):
    count, tokens = place.shape
    width = rows.shape[1]
    block = count // 4
    return pl.pallas_call(
        place_kernel,
        grid=(count // block,),
        out_shape=jax.ShapeDtypeStruct((count, width), LOW),
        in_specs=[
            pl.BlockSpec((block, tokens), lambda i: (i, 0)),
            pl.BlockSpec((tokens, width), lambda i: (0, 0)),
        ],
        out_specs=pl.BlockSpec((block, width), lambda i: (i, 0)),
        compiler_params=kernel_params(),
        cost_estimate=SHORT,
        name="place_rows",
    )(place, rows)


def expert_kernel(experts, ring, place_ref, *refs):
    near_refs, refs = refs[:ring], refs[ring:]
    far_ref, first_ref, gate_ref, up_ref, gate_bias_ref, up_bias_ref, mine_ref = refs[:7]
    grad_far_ref, act_ref, act_gated_ref, grad_gate_ref, grad_up_ref = refs[7:12]
    bias_sums_ref, rows_ref, near_ref = refs[12:]
    hidden, features = gate_ref.shape
    split = near_ref.shape[1]
    rest = features - split
    assemble(place_ref, near_refs, near_ref)
    near, far = near_ref[...], far_ref[:, :rest]
    rows_ref[:, :split], rows_ref[:, split:] = near, far
    mine = mine_ref[...]
    gate = jnp.sum(far_ref[:, rest:].astype(F32) * mine, axis=1, keepdims=True)

    def product(weights_ref):
        return dot(near, weights_ref[:, :split], NT) + dot(far, weights_ref[:, split:], NT)

    gate_lin = product(gate_ref) + gate_bias_ref[...]
    up_lin = product(up_ref) + up_bias_ref[...]
    gate_tanh = jnp.tanh(gate_lin * (1.0 / CLAMP_LIMIT))
    up_tanh = jnp.tanh(up_lin * (1.0 / CLAMP_LIMIT))
    gate_soft = CLAMP_LIMIT * gate_tanh
    up_one = CLAMP_LIMIT * up_tanh + 1.0
    sigmoid = 1.0 / (1.0 + jnp.exp(-GLU_SLOPE * gate_soft))
    swish = gate_soft * sigmoid
    act = (up_one * swish).astype(LOW)
    act_ref[...] = act
    act_gated_ref[:, :hidden] = (act.astype(F32) * gate).astype(LOW)
    spare = act_gated_ref.shape[1] - hidden
    act_gated_ref[:, hidden:] = jnp.broadcast_to(gate.astype(LOW), (act.shape[0], spare))
    first = first_ref[:, :hidden]
    with_bias = jnp.max(first_ref[:, hidden:], axis=1, keepdims=True)
    grad_weight = jnp.sum(act.astype(F32) * first, axis=1, keepdims=True) + with_bias
    grad_act = first * gate
    swish_slope = sigmoid + GLU_SLOPE * swish * (1.0 - sigmoid)
    grad_gate = (grad_act * up_one * swish_slope * (1.0 - gate_tanh * gate_tanh)).astype(LOW)
    grad_up = (grad_act * swish * (1.0 - up_tanh * up_tanh)).astype(LOW)
    grad_gate_ref[...] = grad_gate
    grad_up_ref[...] = grad_up
    grad_far = dot(grad_gate, gate_ref[:, split:]) + dot(grad_up, up_ref[:, split:])
    grad_far_ref[:, :rest] = grad_far.astype(LOW)
    high = grad_weight.astype(LOW).astype(F32)
    lanes = lane_index(mine.shape)
    spread = jnp.where(lanes < experts, high, grad_weight - high) * mine
    grad_far_ref[:, rest:] = spread.astype(LOW)
    sums = jnp.concatenate(
        [
            jnp.sum(grad_gate.astype(F32), axis=0, keepdims=True),
            jnp.sum(grad_up.astype(F32), axis=0, keepdims=True),
        ],
        axis=0,
    )
    is_first = pl.program_id(0) == 0
    bias_sums_ref[...] = jnp.where(is_first, 0.0, bias_sums_ref[...]) + sums


def expert_step(place, near, far, first, gate, up, gate_bias, up_bias, mine, experts):
    count = far.shape[0]
    hidden, features = gate.shape
    block = count // 4
    rest = features - sum(one.shape[1] for one in near)
    gated = round_up(hidden + 8, 128)
    hidden_rows = jax.ShapeDtypeStruct((count, hidden), LOW)
    return pl.pallas_call(
        functools.partial(expert_kernel, experts, len(near)),
        grid=(count // block,),
        out_shape=(
            jax.ShapeDtypeStruct(far.shape, LOW),
            hidden_rows,
            jax.ShapeDtypeStruct((count, gated), LOW),
            hidden_rows,
            hidden_rows,
            jax.ShapeDtypeStruct((2, hidden), F32),
            jax.ShapeDtypeStruct((count, features), LOW),
        ),
        in_specs=[IN_SMEM]
        + [by_row(block, one.shape[1]) for one in near]
        + [
            by_row(block, far.shape[1]),
            by_row(block, first.shape[1]),
            held_block(hidden, features),
            held_block(hidden, features),
            whole_block(1, hidden),
            whole_block(1, hidden),
            whole_block(1, mine.shape[1]),
        ],
        out_specs=(
            by_row(block, far.shape[1]),
            by_row(block, hidden),
            by_row(block, gated),
            by_row(block, hidden),
            by_row(block, hidden),
            whole_block(2, hidden),
            by_row(block, features),
        ),
        scratch_shapes=[pltpu.VMEM((block, features - rest), LOW)],
        compiler_params=kernel_params(),
        cost_estimate=pl.CostEstimate(
            flops=8 * count * features * hidden,
            bytes_accessed=8 * count * features + 4 * features * hidden + 12 * count * hidden,
            transcendentals=3 * count * hidden,
        ),
        name="expert_step",
    )(place, *near, far, first, gate, up, gate_bias, up_bias, mine)


def grad_rows_kernel(grad_gate_ref, grad_up_ref, gate_ref, up_ref, out_ref):
    out = dot(grad_gate_ref[...], gate_ref[...]) + dot(grad_up_ref[...], up_ref[...])
    out_ref[...] = out.astype(LOW)


def grad_rows_near(grad_gate, grad_up, gate, up, split):
    count, hidden = grad_gate.shape
    block = count // 4
    return pl.pallas_call(
        grad_rows_kernel,
        grid=(count // block,),
        out_shape=jax.ShapeDtypeStruct((count, split), LOW),
        in_specs=[
            by_row(block, hidden),
            by_row(block, hidden),
            held_block(hidden, split),
            held_block(hidden, split),
        ],
        out_specs=by_row(block, split),
        compiler_params=kernel_params(),
        cost_estimate=SHORT,
        name="grad_rows",
    )(grad_gate, grad_up, gate, up)


def weight_grad_kernel(left_ref, right_ref, out_ref, *refs):
    bias_ref, turned_ref = refs if len(refs) == 2 else (None, refs[0])

    @pl.when(pl.program_id(0) == 0)
    def _():
        turned_ref[...] = left_ref[...].T

    hidden = out_ref.shape[0]
    product = dot(turned_ref[...], right_ref[...])
    out_ref[...] = product[:hidden]
    if bias_ref is not None:
        bias_ref[...] = product[hidden : hidden + 8]


def weight_grad(left, right, hidden):
    count, width = left.shape
    features = right.shape[1]
    block = round_up(-(-features // STEPS), 128)
    out_shape = [jax.ShapeDtypeStruct((hidden, features), F32)]
    out_specs = [by_column(hidden, block)]
    if width > hidden:
        out_shape.append(jax.ShapeDtypeStruct((8, features), F32))
        out_specs.append(by_column(8, block))
    return pl.pallas_call(
        weight_grad_kernel,
        grid=(STEPS,),
        out_shape=out_shape,
        in_specs=[whole_block(count, width), by_column(count, block)],
        out_specs=out_specs,
        scratch_shapes=[pltpu.VMEM((width, count), LOW)],
        compiler_params=kernel_params(),
        cost_estimate=SHORT,
        name="weight_grad",
    )(left, right)


def exchange(rows, parts):
    count, width = rows.shape
    moved = lax.all_to_all(
        rows.reshape(parts, count // parts, width),
        "expert",
        split_axis=0,
        concat_axis=0,
        tiled=True,
    )
    return moved.reshape(count, width)


def low_sum(halves):
    upper, upper_in, lower, lower_in = halves
    return (
        (upper.astype(F32) + upper_in.astype(F32)).astype(LOW),
        (lower.astype(F32) + lower_in.astype(F32)).astype(LOW),
    )


def tensor_sum(upper, lower, ring, middle=low_sum):
    near = [(i, i ^ 1) for i in range(ring)]
    far = [(i, ring - 1 - i) for i in range(ring)]
    upper_in = lax.ppermute(upper, "tensor", near)
    lower_in = lax.ppermute(lower, "tensor", far)
    upper, lower = middle((upper, upper_in, lower, lower_in))
    upper_in = lax.ppermute(upper, "tensor", far)
    lower_in = lax.ppermute(lower, "tensor", near)
    return upper, upper_in, lower, lower_in


def together(*values):
    return lax.optimization_barrier(values)


def ring_steps(ring):
    return [(i, (i + 1) % ring) for i in range(ring)], [(i, (i - 1) % ring) for i in range(ring)]


def tensor_chunks(own, ring):
    up, down = ring_steps(ring)
    half = own.shape[0] // 2
    before = lax.ppermute(own, "tensor", up)
    behind = lax.ppermute(own, "tensor", down)
    far_top = lax.ppermute(before[:half], "tensor", up)
    far_bottom = lax.ppermute(behind[half:], "tensor", down)
    across = jnp.concatenate([far_top, far_bottom], axis=0)
    return own, behind, across, before


def tensor_chunks_short(own, ring):
    across = [(i, (i + 2) % ring) for i in range(ring)]
    up, down = ring_steps(ring)
    before = lax.ppermute(own, "tensor", up)
    behind = lax.ppermute(own, "tensor", down)
    return own, behind, lax.ppermute(own, "tensor", across), before


def expert_sum(values, count, beside, work):
    masks = {32: (1, 2, 6, 8, 24)}.get(count) or [1 << i for i in range(count.bit_length() - 1)]
    for step, mask in enumerate(masks):
        if step == len(masks) // 2:
            values, beside = together(values, beside)
            made = work(beside)
        if step == len(masks) - 1:
            values, made = together(values, made)
        there = lax.ppermute(values, "expert", [(i, i ^ mask) for i in range(count)])
        values = (values.astype(F32) + there.astype(F32)).astype(values.dtype)
    return values, beside, made


def on_device(
    expert_axis,
    tensor_axis,
    block_input,
    out_cotangent,
    seq_lengths,
    route_ids,
    attn_gain,
    w_query,
    w_key,
    w_value,
    b_query,
    b_key,
    b_value,
    sink_logits,
    w_output,
    b_output,
    ffn_gain,
    w_router,
    b_router,
    w_gate,
    w_up,
    b_gate,
    b_up,
    w_down,
    b_down,
):
    tokens, features = block_input.shape
    heads = sink_logits.shape[0]
    experts = w_router.shape[1]
    capacity = 2 * tokens * route_ids.shape[1] // experts
    slots = experts * capacity
    shard = w_query.shape[0]
    shard_pad = round_up(shard + 1, 16)
    width = round_up(features + 2 * experts, 128)
    chunk = max(1, round(width / 128 / (2 * tensor_axis))) * 128
    split = chunk * tensor_axis
    rest = features - split
    block_width = round_up(-(-features // tensor_axis), 128)
    mine_expert = lax.axis_index("expert")
    mine_tensor = lax.axis_index("tensor")

    out_width = w_output.shape[0]
    packed = jnp.concatenate([w_output.T, w_query, w_key, w_value], axis=1)
    packed = jnp.pad(packed, ((0, shard_pad - shard), (0, 0)))
    weights = lax.all_gather(packed, "expert", axis=0, tiled=True)

    expert_ids = jnp.arange(experts, dtype=jnp.int32)
    named = jnp.any(route_ids[:, :, None] == expert_ids[None, None, :], axis=1)
    named_t = jnp.any(route_ids.T[:, None, :] == expert_ids[None, :, None], axis=0)
    token_ids = jnp.arange(tokens, dtype=jnp.int32)
    earlier = (token_ids[:, None] < token_ids[None, :]).astype(LOW)
    rank_t = dot(named_t.astype(LOW), earlier).astype(jnp.int32)
    place = (rank_t[:, None, :] == jnp.arange(capacity, dtype=jnp.int32)[None, :, None]) & named_t[
        :, None, :
    ]
    place = place.astype(LOW).reshape(slots, tokens)
    place_t = place.T


    def own_block(rows, size, ahead=0):
        start = (mine_tensor + ahead) % tensor_axis * size
        return lax.dynamic_slice(rows, (0, start), (tokens, size))

    cotangent_wide = jnp.pad(
        out_cotangent, ((0, 0), (0, block_width * tensor_axis - features))
    )
    cotangent_own = exchange(place_rows(place, own_block(cotangent_wide, block_width)), experts)
    up, down_ring = ring_steps(tensor_axis)
    cotangent_before = lax.ppermute(cotangent_own, "tensor", up)
    cotangent_behind = lax.ppermute(cotangent_own, "tensor", down_ring)
    cotangent_across = place_rows(place, own_block(cotangent_wide, block_width, 2))

    segment, position = layout(seq_lengths[0], tokens)
    cos, sin = rope_tables(position)
    allowed = (segment[:, None] == segment[None, :]) & (token_ids[None, :] <= token_ids[:, None])
    allowed = allowed.astype(F32)

    inputs = block_input.astype(F32)
    scale_one = lax.rsqrt(jnp.mean(inputs * inputs, axis=-1, keepdims=True) + EPSILON)
    unit_one = inputs * scale_one
    normed_low = (unit_one * attn_gain).astype(LOW)
    spread_low = jnp.pad(
        normed_low.reshape(tokens, expert_axis, shard), ((0, 0), (0, 0), (0, shard_pad - shard))
    )
    one_column = (jnp.arange(shard_pad) == shard).astype(LOW)
    normed_blocks = jnp.transpose(spread_low + one_column, (1, 2, 0))
    normed_blocks = normed_blocks.reshape(expert_axis * shard_pad, tokens)

    (
        weights,
        cotangent_across,
        cotangent_own,
        cotangent_before,
        cotangent_behind,
        normed_blocks,
    ) = together(
        weights,
        cotangent_across,
        cotangent_own,
        cotangent_before,
        cotangent_behind,
        normed_blocks,
    )
    cotangent_across = exchange(cotangent_across, experts)
    bias = jnp.concatenate([b_query, b_key, b_value])[None, :]
    spread_low = spread_low.reshape(tokens, expert_axis * shard_pad)
    attn_low, rotated, lse = attend_forward(
        sink_logits, spread_low, weights, bias, cos, sin, allowed
    )
    attn_all = lax.all_gather(attn_low, "expert", axis=0, tiled=True)
    attn_part = compact_product(attn_low, tokens, weights, out_width, shard, shard_pad, "attn_output")
    attn_sum = tensor_sum(*attn_part, tensor_axis)
    ring_place = mine_tensor.astype(jnp.int32).reshape(1)
    residual, gates, sent, rows_own = token_forward(
        ring_place,
        block_input,
        attn_sum,
        b_output[None, :],
        ffn_gain[None, :],
        w_router.T,
        b_router[None, :],
        named.astype(F32),
        place,
        width,
        chunk,
    )

    gate_t, up_t, down = w_gate[0].T, w_up[0].T, w_down[0]
    hidden = down.shape[0]
    bias_once = jnp.where(mine_tensor == 0, b_down, 0.0)
    rows_own, cotangent_across = together(rows_own, cotangent_across)
    cotangent_rows = (cotangent_own, cotangent_behind, cotangent_across, cotangent_before)
    first, cotangent_all = grad_hidden_product(ring_place, cotangent_rows, down, bias_once)
    rows_own = exchange(rows_own, experts)
    rows_far = place_rows(place, sent[:, split:])
    rows_own, rows_far, first = together(rows_own, rows_far, first)
    rows_near = tensor_chunks(rows_own, tensor_axis)
    rows_far = exchange(rows_far, experts)

    lane = jnp.arange(width - features)
    mine = ((lane % experts == mine_expert) & (lane < 2 * experts)).astype(F32)[None, :]
    rows_near, rows_far, attn_all = together(rows_near, rows_far, attn_all)
    grad_far, act, act_gated, grad_gate, grad_up, bias_sums, rows_all = expert_step(
        ring_place, rows_near, rows_far, first, gate_t, up_t, b_gate, b_up, mine, experts
    )
    back_far = exchange(grad_far, experts)
    grad_near = grad_rows_near(grad_gate, grad_up, gate_t, up_t, split)
    result = expert_result(act, down, bias_once, tensor_axis, block_width)
    result_own = lax.psum_scatter(result, "tensor", scatter_dimension=0, tiled=False)
    grad_near, back_far, grad_gate, grad_up, act_gated = together(
        grad_near, back_far, grad_gate, grad_up, act_gated
    )
    back_near = exchange(grad_near, experts)
    far_halves = combine_far(place_t, back_far, rest, experts)
    w_gate_grad = weight_grad(grad_gate, rows_all, hidden)[0]

    def middle(halves):
        nonlocal w_gate_grad, grad_up, act_gated
        *halves, w_gate_grad = together(*halves, w_gate_grad)
        upper, lower = middle_far(halves, rest, experts)
        upper, lower, grad_up, act_gated = together(upper, lower, grad_up, act_gated)
        return upper, lower

    far_sum = tensor_sum(*far_halves, tensor_axis, middle)
    w_up_grad = weight_grad(grad_up, rows_all, hidden)[0]
    w_down_grad, b_down_grad = weight_grad(act_gated, cotangent_all, hidden)
    back_near, w_up_grad, w_down_grad, b_down_grad, result_own, *far_sum = together(
        back_near, w_up_grad, w_down_grad, b_down_grad, result_own, *far_sum
    )
    w_gate_grad, w_up_grad = w_gate_grad.T[None], w_up_grad.T[None]
    w_down_grad, b_down_grad = w_down_grad[None], b_down_grad[0:1]
    b_gate_grad = bias_sums[0:1]
    b_up_grad = bias_sums[1:2]

    upper, lower = combine_near(place_t, back_near)
    upper, lower, result_own = together(upper, lower, result_own)
    near_sum = tensor_sum(upper, lower, tensor_axis)
    returned = exchange(result_own, experts)
    grad_resid, resid_spread, resid_blocks, router_block, vectors = token_backward(
        ring_place,
        near_sum,
        far_sum,
        gates,
        w_router.T,
        residual,
        out_cotangent,
        ffn_gain[None, :],
        shard,
        shard_pad,
        tensor_axis,
    )
    grad_qkv, sink_part = attend_backward(
        sink_logits, resid_spread, weights, rotated, lse, cos, sin, allowed
    )
    grad_qkv, returned = together(grad_qkv, returned)
    grad_qkv_all = lax.all_gather(grad_qkv, "expert", axis=0, tiled=True)
    upper, lower, attn_gain_part = compact_product(
        grad_qkv, tokens, weights, weights.shape[1], shard, shard_pad, "grad_normed", spread_low
    )
    grad_normed = tensor_sum(upper, lower, tensor_axis)
    normed_blocks = normed_blocks.reshape(expert_axis, shard_pad, tokens)
    blocks = jnp.concatenate([normed_blocks, resid_blocks], axis=1)
    blocks = exchange(blocks.reshape(expert_axis * 2 * shard_pad, tokens), expert_axis)
    blocks = blocks.reshape(expert_axis, 2 * shard_pad, tokens)

    sinks_row = jnp.pad(sink_part[:, :heads], ((0, 0), (0, tokens - heads)))
    small = pack_small(router_block, vectors, attn_gain_part, sinks_row)

    def output_product(blocks):
        return gathered_products(
            blocks, 1, attn_all, (out_width,), shard, shard_pad, False, "output_grad"
        )[0]

    small, blocks, w_output_grad = expert_sum(small, expert_axis, blocks, output_product)
    small, returned = together(small, returned)
    shared = experts + -(-features // block_width)
    widths = (w_query.shape[1], w_key.shape[1], w_value.shape[1])
    w_output_grad = w_output_grad.T
    qkv_grads = gathered_products(
        blocks, 0, grad_qkv_all, widths, shard, shard_pad, True, "qkv_grad"
    )
    query_grad, *qkv_grads = qkv_grads
    chunks = tensor_chunks_short(small[:shared], tensor_axis)
    router_grad, gain_grad, ffn_gain_grad, output_bias_grad, sink_grad, router_bias_grad = (
        unpack_small(ring_place, chunks, small[shared:], attn_gain[None, :], experts, heads)
    )

    input_grad = input_grad_rows(grad_normed, grad_resid, block_input, attn_gain[None, :]).T
    mixed = tensor_chunks_short(mix_results(place_t, gates, returned), tensor_axis)
    block_output = output_rows(ring_place, mixed, residual).T

    return (
        block_output,
        input_grad,
        gain_grad,
        query_grad,
        qkv_grads[0],
        qkv_grads[1],
        qkv_grads[2],
        qkv_grads[3],
        qkv_grads[4],
        sink_grad,
        w_output_grad,
        output_bias_grad,
        ffn_gain_grad,
        router_grad.T,
        router_bias_grad,
        w_gate_grad,
        w_up_grad,
        b_gate_grad,
        b_up_grad,
        w_down_grad,
        b_down_grad,
    )


def solution(mesh):
    in_specs = (
        P("expert", None),
        P("expert", None),
        P("expert", None),
        P("expert", None),
        P(),
        P("expert", "tensor"),
        P("expert", "tensor"),
        P("expert", "tensor"),
        P("tensor"),
        P("tensor"),
        P("tensor"),
        P("tensor"),
        P("tensor", "expert"),
        P(),
        P(),
        P(),
        P(),
        P("expert", None, "tensor"),
        P("expert", None, "tensor"),
        P("expert", "tensor"),
        P("expert", "tensor"),
        P("expert", "tensor", None),
        P("expert", None),
    )
    out_specs = (
        P("expert", None),
        P("expert", None),
        P(),
        P("expert", "tensor"),
        P("expert", "tensor"),
        P("expert", "tensor"),
        P("tensor"),
        P("tensor"),
        P("tensor"),
        P("tensor"),
        P("tensor", "expert"),
        P(),
        P(),
        P(),
        P(),
        P("expert", None, "tensor"),
        P("expert", None, "tensor"),
        P("expert", "tensor"),
        P("expert", "tensor"),
        P("expert", "tensor", None),
        P("expert", None),
    )
    body = functools.partial(on_device, mesh.shape["expert"], mesh.shape["tensor"])
    return jax.shard_map(body, mesh=mesh, in_specs=in_specs, out_specs=out_specs, check_vma=False)
```

```python
import functools

import jax
import jax.numpy as jnp
from jax import lax
from jax.experimental import pallas as pl
from jax.experimental.pallas import tpu as pltpu
from jax.sharding import PartitionSpec as P

HD = 64
PAIR = 2 * HD
EPSILON = 1e-05
ROPE_BASE = 150000.0
CLAMP_LIMIT = 7.0
GLU_SLOPE = 1.702
MASKED = -1e30
PRECISE = lax.Precision.HIGHEST
LOW = jnp.bfloat16
F32 = jnp.float32
VMEM_BYTES = 56 * 1024 * 1024
NN = (((1,), (0,)), ((), ()))
NT = (((1,), (1,)), ((), ()))
TN = (((0,), (0,)), ((), ()))


def round_up(value, unit):
    return -(-value // unit) * unit


def dot(left, right, dims=NN):
    return lax.dot_general(left, right, dims, preferred_element_type=F32)


def split_low(values):
    high = values.astype(LOW)
    return high, (values - high.astype(F32)).astype(LOW)


def layout(lengths, tok_count):
    seq_ends = jnp.cumsum(lengths)
    tok_index = jnp.arange(tok_count, dtype=jnp.int32)
    is_past = tok_index[:, None] >= seq_ends[None, :]
    segment = jnp.sum(is_past.astype(jnp.int32), axis=1)
    offset = jnp.sum(jnp.where(is_past, lengths[None, :], 0), axis=1)
    return (segment, tok_index - offset)


def rope_tables(position):
    half = HD // 2
    frequency = ROPE_BASE ** (-(jnp.arange(half).astype(F32) * 2.0 / HD))
    angles = position.astype(F32)[:, None] * frequency[None, :]
    cosine, sine = jnp.cos(angles), jnp.sin(angles)
    return (
        jnp.concatenate([cosine] * 4, axis=1),
        jnp.concatenate([-sine, sine, -sine, sine], axis=1),
    )


def lane_index(shape):
    return lax.broadcasted_iota(jnp.int32, shape, len(shape) - 1)


def swap_halves(values):
    first = (lane_index(values.shape) % HD) < HD // 2
    return jnp.where(
        first, pltpu.roll(values, PAIR - HD // 2, 1), pltpu.roll(values, HD // 2, 1)
    )


def twin(values, which):
    turned = pltpu.roll(values, HD, 1)
    left = lane_index(values.shape) < HD
    return jnp.where(left, values, turned) if which == 0 else jnp.where(left, turned, values)


def attend_forward_kernel(
    sink_ref,
    rows_ref,
    weights_ref,
    bias_ref,
    cos_ref,
    sin_ref,
    allowed_ref,
    out_ref,
    rot_ref,
    lse_ref,
    qkv_ref,
):
    step = pl.program_id(0)
    start = weights_ref.shape[1] - qkv_ref.shape[1]
    part = dot(rows_ref[...], weights_ref[:, start:])

    @pl.when(step == 0)
    def _():
        qkv_ref[...] = part + bias_ref[...]

    @pl.when(step > 0)
    def _():
        qkv_ref[...] += part

    @pl.when(step == pl.num_programs(0) - 1)
    def _():
        attend(
            sink_ref, qkv_ref, cos_ref, sin_ref, allowed_ref, out_ref, rot_ref, lse_ref
        )


def attend(sink_ref, qkv_ref, cos_ref, sin_ref, allowed_ref, out_ref, rot_ref, lse_ref):
    tokens = qkv_ref.shape[0]
    heads = sink_ref.shape[0]
    key_at = heads * HD
    value_at = key_at + PAIR
    per_group = heads // 2
    cos, sin = cos_ref[...], sin_ref[...]
    allowed = allowed_ref[...] > 0.5
    left = lane_index((tokens, PAIR)) < HD
    lanes = lane_index((tokens, PAIR))

    def rope(values):
        return values * cos + swap_halves(values) * sin

    key = rope(qkv_ref[:, key_at:value_at])
    value = qkv_ref[:, value_at : value_at + PAIR]
    rot_ref[:, key_at:value_at] = key.astype(LOW)
    rot_ref[:, value_at : value_at + PAIR] = value.astype(LOW)
    keys = [twin(key, g).astype(LOW) for g in range(2)]
    values = [twin(value, g).astype(LOW) for g in range(2)]
    lse_all = jnp.zeros((tokens, PAIR), F32)
    for pair in range(heads // 2):
        cols = slice(pair * PAIR, (pair + 1) * PAIR)
        group = (2 * pair) // per_group
        query = rope(qkv_ref[:, cols])
        rot_ref[:, cols] = query.astype(LOW)
        outs = []
        for side in range(2):
            head = 2 * pair + side
            mine = left if side == 0 else jnp.logical_not(left)
            one = jnp.where(mine, query * HD ** (-0.5), 0.0).astype(LOW)
            scores = dot(one, keys[group], NT)
            scores = jnp.where(allowed, scores, MASKED)
            sink = sink_ref[head]
            top = jnp.maximum(jnp.max(scores, axis=1, keepdims=True), sink)
            weights = jnp.exp(scores - top)
            denom = jnp.sum(weights, axis=1, keepdims=True) + jnp.exp(sink - top)
            lse = top + jnp.log(denom)
            lse_all = jnp.where(lanes == head, lse, lse_all)
            prob = (weights * (1.0 / denom)).astype(LOW)
            outs.append(dot(prob, values[group]))
        out_ref[:, cols] = jnp.where(left, outs[0], outs[1]).astype(LOW)
    lse_ref[...] = lse_all


def attend_backward_kernel(
    sink_ref,
    rows_ref,
    weights_ref,
    rot_ref,
    lse_ref,
    cos_ref,
    sin_ref,
    allowed_ref,
    out_ref,
    sink_out_ref,
    sum_ref,
    grad_ref,
):
    step = pl.program_id(0)
    part = dot(rows_ref[...], weights_ref[...])

    @pl.when(step == 0)
    def _():
        sum_ref[...] = part

    @pl.when(step > 0)
    def _():
        sum_ref[...] += part

    @pl.when(step == pl.num_programs(0) - 1)
    def _():
        grad_ref[...] = sum_ref[...].astype(LOW)
        attend_back(
            sink_ref,
            rot_ref,
            grad_ref,
            lse_ref,
            cos_ref,
            sin_ref,
            allowed_ref,
            out_ref,
            sink_out_ref,
        )


def attend_back(
    sink_ref, rot_ref, grad_ref, lse_ref, cos_ref, sin_ref, allowed_ref, out_ref, sink_out_ref
):
    tokens = rot_ref.shape[0]
    heads = sink_ref.shape[0]
    key_at = heads * HD
    value_at = key_at + PAIR
    per_group = heads // 2
    scale = HD ** (-0.5)
    cos, sin = cos_ref[...], sin_ref[...]
    allowed = allowed_ref[...] > 0.5
    lanes = lane_index((tokens, PAIR))
    left = lanes < HD

    def turn_back(values):
        return values * cos - swap_halves(values) * sin

    key = rot_ref[:, key_at:value_at].astype(F32)
    value = rot_ref[:, value_at : value_at + PAIR].astype(F32)
    keys = [twin(key, g).astype(LOW) for g in range(2)]
    values = [twin(value, g).astype(LOW) for g in range(2)]
    key_sums = [jnp.zeros((tokens, PAIR), F32) for _ in range(2)]
    value_sums = [jnp.zeros((tokens, PAIR), F32) for _ in range(2)]
    sink_all = jnp.zeros((tokens, PAIR), F32)
    lse_all = lse_ref[...]
    for pair in range(heads // 2):
        cols = slice(pair * PAIR, (pair + 1) * PAIR)
        group = (2 * pair) // per_group
        query = rot_ref[:, cols].astype(F32)
        grad = grad_ref[:, cols].astype(F32)
        outs = []
        for side in range(2):
            head = 2 * pair + side
            mine = left if side == 0 else jnp.logical_not(left)
            one = jnp.where(mine, query, 0.0).astype(LOW)
            grad_one = jnp.where(mine, grad, 0.0).astype(LOW)
            lse = jnp.sum(jnp.where(lanes == head, lse_all, 0.0), axis=1, keepdims=True)
            scores = dot(one, keys[group], NT) * scale
            prob = jnp.where(allowed, jnp.exp(jnp.where(allowed, scores - lse, 0.0)), 0.0)
            grad_prob = dot(grad_one, values[group], NT)
            delta = jnp.sum(prob * grad_prob, axis=1, keepdims=True)
            grad_score = (prob * (grad_prob - delta)).astype(LOW)
            outs.append(dot(grad_score, keys[group]))
            key_sums[group] += dot(grad_score, one, TN)
            value_sums[group] += dot(prob.astype(LOW), grad_one, TN)
            sink_all = jnp.where(lanes == head, jnp.exp(sink_ref[head] - lse) * delta, sink_all)
        out_ref[:tokens, cols] = turn_back(jnp.where(left, outs[0], outs[1]) * scale).astype(LOW)

    def fold(sums):
        both = [one + pltpu.roll(one, HD, 1) for one in sums]
        return jnp.where(left, both[0], both[1])

    out_ref[:tokens, key_at:value_at] = turn_back(fold(key_sums) * scale).astype(LOW)
    out_ref[:tokens, value_at : value_at + PAIR] = fold(value_sums).astype(LOW)
    sink_out_ref[...] = -jnp.sum(sink_all, axis=0, keepdims=True)


def kernel_params():
    return pltpu.CompilerParams(vmem_limit_bytes=VMEM_BYTES)


SHORT = pl.CostEstimate(flops=1, bytes_accessed=1, transcendentals=0)
IN_VMEM = pl.BlockSpec(memory_space=pltpu.VMEM)
IN_SMEM = pl.BlockSpec(memory_space=pltpu.SMEM)


def by_row(block, columns):
    return pl.BlockSpec((block, columns), lambda i: (i, 0))


def by_column(rows, block):
    return pl.BlockSpec((rows, block), lambda i: (0, i))


def whole_block(*shape):
    return pl.BlockSpec(shape, lambda i: (0, 0))


def held_block(*shape):
    return pl.BlockSpec(shape, lambda i: (0, 0), pipeline_mode=pl.Buffered(1))


STEPS = 4


def attend_forward(sinks, rows, weights, bias, cos, sin, allowed):
    tokens, inner = rows.shape
    width = bias.shape[1]
    heads = sinks.shape[0]
    block = inner // STEPS
    return pl.pallas_call(
        attend_forward_kernel,
        grid=(STEPS,),
        out_shape=(
            jax.ShapeDtypeStruct((tokens, heads * HD), LOW),
            jax.ShapeDtypeStruct((tokens, width), LOW),
            jax.ShapeDtypeStruct((tokens, PAIR), F32),
        ),
        in_specs=[
            IN_SMEM,
            by_column(tokens, block),
            by_row(block, weights.shape[1]),
            whole_block(1, width),
            whole_block(*cos.shape),
            whole_block(*sin.shape),
            whole_block(*allowed.shape),
        ],
        out_specs=(
            whole_block(tokens, heads * HD),
            whole_block(tokens, width),
            whole_block(tokens, PAIR),
        ),
        scratch_shapes=[pltpu.VMEM((tokens, width), F32)],
        compiler_params=kernel_params(),
        cost_estimate=SHORT,
        name="attend_forward",
    )(sinks, rows, weights, bias, cos, sin, allowed)


def attend_backward(sinks, rows, weights, rotated, lse, cos, sin, allowed):
    tokens, width = rotated.shape
    inner = rows.shape[1]
    out_width = sinks.shape[0] * HD
    block = inner // STEPS
    return pl.pallas_call(
        attend_backward_kernel,
        grid=(STEPS,),
        out_shape=(
            jax.ShapeDtypeStruct((tokens, width), LOW),
            jax.ShapeDtypeStruct((1, PAIR), F32),
        ),
        in_specs=[
            IN_SMEM,
            by_column(tokens, block),
            by_row(block, out_width),
            whole_block(tokens, width),
            whole_block(*lse.shape),
            whole_block(*cos.shape),
            whole_block(*sin.shape),
            whole_block(*allowed.shape),
        ],
        out_specs=(whole_block(tokens, width), whole_block(1, PAIR)),
        scratch_shapes=[pltpu.VMEM((tokens, out_width), F32), pltpu.VMEM((tokens, out_width), LOW)],
        compiler_params=kernel_params(),
        cost_estimate=SHORT,
        name="attend_backward",
    )(sinks, rows, weights, rotated, lse, cos, sin, allowed)


def compact_kernel(shard, shard_pad, left_ref, weights_ref, *refs):
    unit_ref, upper_ref, lower_ref, gain_ref = refs if len(refs) == 4 else (None, *refs, None)
    start = weights_ref.shape[1] - left_ref.shape[1]
    product = dot(left_ref[...], weights_ref[:, start:], NT)
    half = upper_ref.shape[0]
    shards = weights_ref.shape[0] // shard_pad
    if gain_ref is not None:
        gain = jnp.sum(product * unit_ref[...].astype(F32), axis=0, keepdims=True)
    for step in range(upper_ref.shape[1] // (shards * shard)):

        @pl.when(pl.program_id(0) == step)
        def _():
            for i in range(shards):
                piece = product[:, i * shard_pad : i * shard_pad + shard].astype(LOW)
                at = (step * shards + i) * shard
                upper_ref[:, at : at + shard] = piece[:half]
                lower_ref[:, at : at + shard] = piece[half:]
                if gain_ref is not None:
                    pad_at = i * shard_pad
                    gain_ref[:, at : at + shard] = gain[:, pad_at : pad_at + shard]


def compact_product(left, tokens, weights, block_width, shard, shard_pad, name, unit=None):
    inner = left.shape[1]
    rows = weights.shape[0]
    features = rows // shard_pad * shard
    half = jax.ShapeDtypeStruct((tokens // 2, features), LOW)
    operands = [left, weights]
    in_specs = [whole_block(tokens, inner), by_row(rows // STEPS, block_width)]
    out_shape = [half, half]
    if unit is not None:
        operands.append(unit)
        in_specs.append(by_column(tokens, rows // STEPS))
        out_shape.append(jax.ShapeDtypeStruct((1, features), F32))
    return pl.pallas_call(
        functools.partial(compact_kernel, shard, shard_pad),
        grid=(STEPS,),
        out_shape=out_shape,
        in_specs=in_specs,
        out_specs=[whole_block(*one.shape) for one in out_shape],
        compiler_params=kernel_params(),
        cost_estimate=SHORT,
        name=name,
    )(*operands)


def rms_scale(values):
    return lax.rsqrt(jnp.mean(values * values, axis=1, keepdims=True) + EPSILON)


def join_halves(halves, out_ref):
    upper, upper_in, lower, lower_in = halves
    half = upper.shape[0]
    out_ref[:half, :] = upper[...].astype(F32) + upper_in[...].astype(F32)
    out_ref[half:, :] = lower[...].astype(F32) + lower_in[...].astype(F32)


def token_forward_kernel(place_ref, input_ref, *refs):
    halves, refs = refs[:4], refs[4:]
    bias_ref, gain_ref, router_ref, router_bias_ref, named_ref, slots_ref = refs[:6]
    resid_ref, gates_ref, sent_ref, own_ref = refs[6:]
    features = input_ref.shape[1]
    experts = router_ref.shape[0]
    chunk = own_ref.shape[1]
    join_halves(halves, resid_ref)
    resid = input_ref[...].astype(F32) + resid_ref[...] + bias_ref[...]
    resid_ref[...] = resid
    normed = resid * rms_scale(resid) * gain_ref[...]
    logits = lax.dot_general(
        normed, router_ref[...], NT, precision=PRECISE, preferred_element_type=F32
    )
    named = named_ref[...] > 0.5
    logits = jnp.where(named, logits + router_bias_ref[...], MASKED)
    weights = jnp.exp(logits - jnp.max(logits, axis=1, keepdims=True))
    weights = jnp.where(named, weights, 0.0)
    gates = weights / jnp.sum(weights, axis=1, keepdims=True)
    gates_ref[...] = gates
    high, low = split_low(gates)
    sent_ref[:, :features] = normed.astype(LOW)
    sent_ref[:, features : features + experts] = high
    sent_ref[:, features + experts : features + 2 * experts] = low
    spare = sent_ref.shape[1] - features - 2 * experts
    if spare:
        sent_ref[:, features + 2 * experts :] = jnp.zeros((resid.shape[0], spare), LOW)
    own = sent_ref[:, pl.ds(pl.multiple_of(place_ref[0] * chunk, 128), chunk)]
    own_ref[...] = dot(slots_ref[...], own).astype(LOW)


def token_forward(place, inputs, halves, bias, gain, router, router_bias, named, slots, width, chunk):
    tokens, features = inputs.shape
    experts = router.shape[0]
    return pl.pallas_call(
        token_forward_kernel,
        out_shape=(
            jax.ShapeDtypeStruct((tokens, features), F32),
            jax.ShapeDtypeStruct((tokens, experts), F32),
            jax.ShapeDtypeStruct((tokens, width), LOW),
            jax.ShapeDtypeStruct((slots.shape[0], chunk), LOW),
        ),
        in_specs=[IN_SMEM] + [IN_VMEM] * 11,
        out_specs=(IN_VMEM,) * 4,
        compiler_params=kernel_params(),
        cost_estimate=SHORT,
        name="token_forward",
    )(place, inputs, *halves, bias, gain, router, router_bias, named, slots)


def token_backward_kernel(shard, shard_pad, place_ref, *refs):
    near_halves, halves, refs = refs[:4], refs[4:8], refs[8:]
    gates_ref, router_ref, resid_ref, cotangent_ref, gain_ref = refs[:5]
    out_ref, spread_ref, blocks_ref, router_out_ref, vectors_ref = refs[5:10]
    near_ref, far_ref, grad_ref, router_all_ref = refs[10:]
    tokens, features = resid_ref.shape
    experts = router_ref.shape[0]
    split = near_ref.shape[1]
    rest = features - split
    join_halves(near_halves, near_ref)
    join_halves(halves, far_ref)
    gates = gates_ref[...]
    grad_gates = far_ref[:, rest : rest + experts] + far_ref[:, rest + experts : rest + 2 * experts]
    grad_logits = gates * (grad_gates - jnp.sum(gates * grad_gates, axis=1, keepdims=True))
    through = lax.dot_general(
        grad_logits, router_ref[...], NN, precision=PRECISE, preferred_element_type=F32
    )
    grad_ref[:, :split] = through[:, :split] + near_ref[...]
    grad_ref[:, split:] = through[:, split:] + far_ref[:, :rest]
    grad_two = grad_ref[...]
    resid = resid_ref[...]
    scale = rms_scale(resid)
    unit = resid * scale
    gain = gain_ref[...]
    router_part = lax.dot_general(
        grad_logits, unit * gain, TN, precision=PRECISE, preferred_element_type=F32
    )
    scaled = grad_two * gain
    mean = jnp.mean(unit * scaled, axis=1, keepdims=True)
    grad_resid = cotangent_ref[...].astype(F32) + scale * (scaled - unit * mean)
    out_ref[...] = grad_resid
    vectors_ref[...] = jnp.zeros_like(vectors_ref)
    vectors_ref[0:1, :features] = jnp.sum(grad_two * unit, axis=0, keepdims=True)
    vectors_ref[1:2, :features] = jnp.sum(grad_resid, axis=0, keepdims=True)
    vectors_ref[2:3, :experts] = jnp.sum(grad_logits, axis=0, keepdims=True)
    low = grad_resid.astype(LOW)
    for i in range(features // shard):
        at = i * shard_pad
        spread_ref[:, at : at + shard] = low[:, i * shard : (i + 1) * shard]
        spread_ref[:, at + shard : at + shard_pad] = jnp.zeros((tokens, shard_pad - shard), LOW)
    turned = spread_ref[...].T
    for i in range(features // shard):
        blocks_ref[i] = turned[i * shard_pad : (i + 1) * shard_pad]
    router_all_ref[:, :features] = router_part.astype(LOW)
    spare = router_all_ref.shape[1] - features
    router_all_ref[:, features:] = jnp.zeros((router_part.shape[0], spare), LOW)
    block = router_out_ref.shape[1]
    start = pl.multiple_of(place_ref[0] * block, 128)
    router_out_ref[...] = router_all_ref[:, pl.ds(start, block)]


def pack_kernel(router_ref, vectors_ref, gain_ref, sinks_ref, out_ref):
    experts, width = router_ref.shape
    features = gain_ref.shape[1]
    out_ref[...] = jnp.zeros_like(out_ref)
    out_ref[:experts, :] = router_ref[...]
    row = experts
    for values in (gain_ref[...], vectors_ref[0:1, :features], vectors_ref[1:2, :features]):
        for at in range(0, features, width):
            piece = values[:, at : at + width].astype(LOW)
            out_ref[row : row + 1, : piece.shape[1]] = piece
            row += 1
    lanes = sinks_ref.shape[1]
    out_ref[row : row + 1, :lanes] = sinks_ref[...].astype(LOW)
    out_ref[row + 1 : row + 2, :lanes] = vectors_ref[2:3, :lanes].astype(LOW)


def pack_small(router, vectors, gain, sinks):
    experts, width = router.shape
    rows = round_up(experts + 3 * -(-gain.shape[1] // width) + 2, 16)
    return pl.pallas_call(
        pack_kernel,
        out_shape=jax.ShapeDtypeStruct((rows, width), LOW),
        in_specs=[IN_VMEM] * 4,
        out_specs=IN_VMEM,
        compiler_params=kernel_params(),
        cost_estimate=SHORT,
        name="pack_small",
    )(router, vectors, gain, sinks)


def unpack_kernel(place_ref, *refs):
    chunk_refs, (scale_ref, rest_ref), refs = refs[:4], refs[4:6], refs[6:]
    router_ref, gain_ref, first_ref, second_ref, sinks_ref, bias_ref, all_ref, vector_ref = refs
    experts, features = router_ref.shape
    width = chunk_refs[0].shape[1]
    assemble(place_ref, chunk_refs, all_ref)
    router_ref[...] = all_ref[:experts, :features].astype(F32)
    tiles = -(-features // width)
    for tile in range(tiles):
        at = tile * width
        size = min(width, features - at)
        row = experts + tile
        parts = all_ref[row : row + 1, :].astype(F32)
        total = sum(parts[:, i * width : (i + 1) * width] for i in range(4))
        vector_ref[0:1, at : at + size] = total[:, :size]
        for i in range(2):
            row = i * tiles + tile
            vector_ref[i + 1 : i + 2, at : at + size] = rest_ref[row : row + 1, :size].astype(F32)
    gain_ref[...] = (vector_ref[0:1, :] / scale_ref[...]).reshape(features)
    first_ref[...] = vector_ref[1:2, :].reshape(features)
    second_ref[...] = vector_ref[2:3, :].reshape(features)
    row = 2 * tiles
    heads, biases = sinks_ref.shape[0], bias_ref.shape[0]
    sinks_ref[...] = rest_ref[row : row + 1, :heads].astype(F32).reshape(heads)
    bias_ref[...] = rest_ref[row + 1 : row + 2, :biases].astype(F32).reshape(biases)


def unpack_small(place, chunks, rest, gain, experts, heads):
    rows, width = chunks[0].shape
    features = gain.shape[1]
    wide = jax.ShapeDtypeStruct((features,), F32)
    return pl.pallas_call(
        unpack_kernel,
        out_shape=(
            jax.ShapeDtypeStruct((experts, features), F32),
            wide,
            wide,
            wide,
            jax.ShapeDtypeStruct((heads,), F32),
            jax.ShapeDtypeStruct((experts,), F32),
        ),
        in_specs=[IN_SMEM] + [IN_VMEM] * 6,
        out_specs=(IN_VMEM,) * 6,
        scratch_shapes=[
            pltpu.VMEM((rows, len(chunks) * width), LOW),
            pltpu.VMEM((8, features), F32),
        ],
        compiler_params=kernel_params(),
        cost_estimate=SHORT,
        name="unpack_small",
    )(place, *chunks, gain, rest)


def gathered_kernel(shard, blocks_ref, rows_ref, *refs):
    *out_refs, sum_ref = refs
    blocks = blocks_ref.shape[0]
    turned = jnp.concatenate([blocks_ref[i] for i in range(blocks)], axis=1)
    total = dot(turned, rows_ref[...])
    first = pl.program_id(0) == 0

    @pl.when(first)
    def _():
        sum_ref[...] = total

    @pl.when(jnp.logical_not(first))
    def _():
        sum_ref[...] += total

    @pl.when(pl.program_id(0) == pl.num_programs(0) - 1)
    def _():
        at = 0
        for out_ref in out_refs[: len(out_refs) // 2 if len(out_refs) > 1 else 1]:
            out_ref[...] = sum_ref[:shard, at : at + out_ref.shape[1]]
            at += out_ref.shape[1]
        at = 0
        for out_ref in out_refs[len(out_refs) // 2 if len(out_refs) > 1 else 1 :]:
            size = out_ref.shape[0]
            out_ref[...] = sum_ref[shard : shard + 1, at : at + size].reshape(size)
            at += size


def gathered_products(blocks, which, rows, widths, shard, shard_pad, biases, name):
    parts, _, tokens = blocks.shape
    total, width = rows.shape
    block = parts // STEPS
    out_shape = [jax.ShapeDtypeStruct((shard, one), F32) for one in widths]
    if biases:
        out_shape += [jax.ShapeDtypeStruct((one,), F32) for one in widths]
    return pl.pallas_call(
        functools.partial(gathered_kernel, shard),
        grid=(STEPS,),
        out_shape=out_shape,
        in_specs=[
            pl.BlockSpec((block, shard_pad, tokens), lambda i: (i, which, 0)),
            by_row(total // STEPS, width),
        ],
        out_specs=[
            pl.BlockSpec(one.shape, lambda i, rank=len(one.shape): (0,) * rank)
            for one in out_shape
        ],
        scratch_shapes=[pltpu.VMEM((shard_pad, width), F32)],
        compiler_params=kernel_params(),
        cost_estimate=SHORT,
        name=name,
    )(blocks, rows)


def token_backward(
    place, near, halves, gates, router, resid, cotangent, gain, shard, shard_pad, ring
):
    tokens, features = resid.shape
    experts = router.shape[0]
    router_block = round_up(-(-features // ring), 128)
    parts = features // shard
    return pl.pallas_call(
        functools.partial(token_backward_kernel, shard, shard_pad),
        out_shape=(
            jax.ShapeDtypeStruct((tokens, features), F32),
            jax.ShapeDtypeStruct((tokens, features // shard * shard_pad), LOW),
            jax.ShapeDtypeStruct((parts, shard_pad, tokens), LOW),
            jax.ShapeDtypeStruct((experts, router_block), LOW),
            jax.ShapeDtypeStruct((8, router_block * ring), F32),
        ),
        in_specs=[IN_SMEM] + [IN_VMEM] * 13,
        out_specs=(IN_VMEM,) * 5,
        scratch_shapes=[
            pltpu.VMEM((tokens, near[0].shape[1]), F32),
            pltpu.VMEM((tokens, halves[0].shape[1]), F32),
            pltpu.VMEM((tokens, features), F32),
            pltpu.VMEM((experts, router_block * ring), LOW),
        ],
        compiler_params=kernel_params(),
        cost_estimate=SHORT,
        name="token_backward",
    )(place, *near, *halves, gates, router, resid, cotangent, gain)


def output_kernel(place_ref, *refs):
    near_refs, (resid_ref, out_ref, near_ref) = refs[:4], refs[4:]
    assemble(place_ref, near_refs, near_ref)
    near = near_ref[:, : out_ref.shape[0]].astype(F32)
    out_ref[...] = (resid_ref[...] + near).astype(LOW).T


def output_rows(place, near, resid):
    tokens, features = resid.shape
    return pl.pallas_call(
        output_kernel,
        out_shape=jax.ShapeDtypeStruct((features, tokens), LOW),
        in_specs=[IN_SMEM] + [IN_VMEM] * 5,
        out_specs=IN_VMEM,
        scratch_shapes=[pltpu.VMEM((tokens, sum(one.shape[1] for one in near)), LOW)],
        compiler_params=kernel_params(),
        cost_estimate=SHORT,
        name="output_rows",
    )(place, *near, resid)


def mix_kernel(place_ref, gates_ref, rows_ref, out_ref):
    experts, slots = gates_ref.shape[1], place_ref.shape[1]
    own = lax.broadcasted_iota(jnp.int32, (experts, slots), 1) // (slots // experts)
    own = own == lax.broadcasted_iota(jnp.int32, (experts, slots), 0)
    spread = dot(gates_ref[...].astype(LOW), own.astype(F32).astype(LOW))
    weights = (place_ref[...].astype(F32) * spread).astype(LOW)
    out_ref[...] = dot(weights, rows_ref[...]).astype(LOW)


def mix_results(place_t, gates, rows):
    return pl.pallas_call(
        mix_kernel,
        out_shape=jax.ShapeDtypeStruct((place_t.shape[0], rows.shape[1]), LOW),
        in_specs=[IN_VMEM] * 3,
        out_specs=IN_VMEM,
        compiler_params=kernel_params(),
        cost_estimate=SHORT,
        name="mix_results",
    )(place_t, gates, rows)


def input_grad_kernel(*refs):
    halves, (resid_ref, input_ref, gain_ref, out_ref, sum_ref) = refs[:4], refs[4:]
    join_halves(halves, sum_ref)
    inputs = input_ref[...].astype(F32)
    scale = rms_scale(inputs)
    unit = inputs * scale
    scaled = sum_ref[...] * gain_ref[...]
    mean = jnp.mean(unit * scaled, axis=1, keepdims=True)
    out_ref[...] = (resid_ref[...] + scale * (scaled - unit * mean)).T


def input_grad_rows(halves, resid, inputs, gain):
    tokens, features = resid.shape
    return pl.pallas_call(
        input_grad_kernel,
        out_shape=jax.ShapeDtypeStruct((features, tokens), F32),
        in_specs=[IN_VMEM] * 7,
        out_specs=IN_VMEM,
        scratch_shapes=[pltpu.VMEM((tokens, features), F32)],
        compiler_params=kernel_params(),
        cost_estimate=SHORT,
        name="input_grad",
    )(*halves, resid, inputs, gain)


def store_halves(values, rest, experts, upper_ref, lower_ref):
    half = upper_ref.shape[0]
    main = values[:, :rest].astype(LOW)
    upper_ref[:, :rest], lower_ref[:, :rest] = main[:half], main[half:]
    high, low = split_low(values[:, rest : rest + experts] + values[:, rest + experts : rest + 2 * experts])
    for out_ref, rows in ((upper_ref, slice(0, half)), (lower_ref, slice(half, 2 * half))):
        out_ref[:, rest : rest + experts] = high[rows]
        out_ref[:, rest + experts : rest + 2 * experts] = low[rows]
        spare = out_ref.shape[1] - rest - 2 * experts
        if spare:
            out_ref[:, rest + 2 * experts :] = jnp.zeros((half, spare), LOW)


def combine_kernel(rest, experts, place_ref, rows_ref, upper_ref, lower_ref):
    store_halves(dot(place_ref[...], rows_ref[...]), rest, experts, upper_ref, lower_ref)


def combine_far(place_t, rows, rest, experts):
    half = jax.ShapeDtypeStruct((place_t.shape[0] // 2, rows.shape[1]), LOW)
    return pl.pallas_call(
        functools.partial(combine_kernel, rest, experts),
        out_shape=(half, half),
        in_specs=[IN_VMEM] * 2,
        out_specs=(IN_VMEM,) * 2,
        compiler_params=kernel_params(),
        cost_estimate=SHORT,
        name="combine_far",
    )(place_t, rows)


def combine_near_kernel(place_ref, rows_ref, upper_ref, lower_ref):
    total = dot(place_ref[...], rows_ref[...]).astype(LOW)
    half = upper_ref.shape[0]
    upper_ref[...], lower_ref[...] = total[:half], total[half:]


def combine_near(place_t, rows):
    half = jax.ShapeDtypeStruct((place_t.shape[0] // 2, rows.shape[1]), LOW)
    return pl.pallas_call(
        combine_near_kernel,
        out_shape=(half, half),
        in_specs=[IN_VMEM] * 2,
        out_specs=(IN_VMEM,) * 2,
        compiler_params=kernel_params(),
        cost_estimate=SHORT,
        name="combine_near",
    )(place_t, rows)


def middle_kernel(rest, experts, *refs):
    halves, (upper_ref, lower_ref, sum_ref) = refs[:4], refs[4:]
    join_halves(halves, sum_ref)
    store_halves(sum_ref[...], rest, experts, upper_ref, lower_ref)


def middle_far(halves, rest, experts):
    half = jax.ShapeDtypeStruct(halves[0].shape, LOW)
    return pl.pallas_call(
        functools.partial(middle_kernel, rest, experts),
        out_shape=(half, half),
        in_specs=[IN_VMEM] * 4,
        out_specs=(IN_VMEM,) * 2,
        scratch_shapes=[pltpu.VMEM((2 * half.shape[0], half.shape[1]), F32)],
        compiler_params=kernel_params(),
        cost_estimate=SHORT,
        name="middle_far",
    )(*halves)


def assemble(place_ref, near_refs, out_ref):
    ring, width = len(near_refs), near_refs[0].shape[1]
    for ahead, near_ref in enumerate(near_refs):
        start = (place_ref[0] + ahead) % ring * width
        out_ref[:, pl.ds(pl.multiple_of(start, 128), width)] = near_ref[...]


def grad_hidden_kernel(place_ref, *refs):
    chunk_refs, (down_ref, bias_ref, out_ref, all_ref, rows_ref) = refs[:-5], refs[-5:]
    hidden, features = down_ref.shape
    assemble(place_ref, chunk_refs, rows_ref)
    rows = rows_ref[:, :features]
    all_ref[...] = rows
    spare = out_ref.shape[1] - hidden
    out_ref[:, :hidden] = dot(rows, down_ref[...], NT)
    with_bias = jnp.sum(rows.astype(F32) * bias_ref[...], axis=1, keepdims=True)
    out_ref[:, hidden:] = jnp.broadcast_to(with_bias, (rows.shape[0], spare))


def grad_hidden_product(place, chunks, down, bias):
    count, chunk = chunks[0].shape
    hidden, features = down.shape
    width = round_up(hidden + 1, 128)
    block = count // 4
    return pl.pallas_call(
        grad_hidden_kernel,
        grid=(count // block,),
        out_shape=(
            jax.ShapeDtypeStruct((count, width), F32),
            jax.ShapeDtypeStruct((count, features), LOW),
        ),
        in_specs=[IN_SMEM]
        + [by_row(block, chunk)] * len(chunks)
        + [whole_block(hidden, features), whole_block(1, features)],
        out_specs=(by_row(block, width), by_row(block, features)),
        scratch_shapes=[pltpu.VMEM((block, len(chunks) * chunk), LOW)],
        compiler_params=kernel_params(),
        cost_estimate=SHORT,
        name="grad_hidden",
    )(place, *chunks, down, bias)


def result_kernel(act_ref, down_ref, bias_ref, out_ref):
    parts, rows, width = out_ref.shape
    result = (dot(act_ref[...], down_ref[...]) + bias_ref[...]).astype(LOW)
    for part in range(parts):
        columns = result[:, part * width : (part + 1) * width]
        out_ref[part, :, : columns.shape[1]] = columns
        if columns.shape[1] < width:
            out_ref[part, :, columns.shape[1] :] = jnp.zeros((rows, width - columns.shape[1]), LOW)


def expert_result(act, down, bias, parts, width):
    count, hidden = act.shape
    features = down.shape[1]
    block = count // 4
    return pl.pallas_call(
        result_kernel,
        grid=(count // block,),
        out_shape=jax.ShapeDtypeStruct((parts, count, width), LOW),
        in_specs=[by_row(block, hidden), held_block(hidden, features), whole_block(1, features)],
        out_specs=pl.BlockSpec((parts, block, width), lambda i: (0, i, 0)),
        compiler_params=kernel_params(),
        cost_estimate=SHORT,
        name="expert_result",
    )(act, down, bias)


def place_kernel(place_ref, rows_ref, out_ref):
    out_ref[...] = dot(place_ref[...], rows_ref[...]).astype(LOW)


def place_rows(place, rows):
    count, tokens = place.shape
    width = rows.shape[1]
    block = count // 4
    return pl.pallas_call(
        place_kernel,
        grid=(count // block,),
        out_shape=jax.ShapeDtypeStruct((count, width), LOW),
        in_specs=[
            pl.BlockSpec((block, tokens), lambda i: (i, 0)),
            pl.BlockSpec((tokens, width), lambda i: (0, 0)),
        ],
        out_specs=pl.BlockSpec((block, width), lambda i: (i, 0)),
        compiler_params=kernel_params(),
        cost_estimate=SHORT,
        name="place_rows",
    )(place, rows)


def expert_kernel(experts, ring, place_ref, *refs):
    near_refs, refs = refs[:ring], refs[ring:]
    far_ref, first_ref, gate_ref, up_ref, gate_bias_ref, up_bias_ref, mine_ref = refs[:7]
    grad_far_ref, act_ref, act_gated_ref, grad_gate_ref, grad_up_ref = refs[7:12]
    bias_sums_ref, rows_ref, near_ref = refs[12:]
    hidden, features = gate_ref.shape
    split = near_ref.shape[1]
    rest = features - split
    assemble(place_ref, near_refs, near_ref)
    near, far = near_ref[...], far_ref[:, :rest]
    rows_ref[:, :split], rows_ref[:, split:] = near, far
    mine = mine_ref[...]
    gate = jnp.sum(far_ref[:, rest:].astype(F32) * mine, axis=1, keepdims=True)

    def product(weights_ref):
        return dot(near, weights_ref[:, :split], NT) + dot(far, weights_ref[:, split:], NT)

    gate_lin = product(gate_ref) + gate_bias_ref[...]
    up_lin = product(up_ref) + up_bias_ref[...]
    gate_tanh = jnp.tanh(gate_lin * (1.0 / CLAMP_LIMIT))
    up_tanh = jnp.tanh(up_lin * (1.0 / CLAMP_LIMIT))
    gate_soft = CLAMP_LIMIT * gate_tanh
    up_one = CLAMP_LIMIT * up_tanh + 1.0
    sigmoid = 1.0 / (1.0 + jnp.exp(-GLU_SLOPE * gate_soft))
    swish = gate_soft * sigmoid
    act = (up_one * swish).astype(LOW)
    act_ref[...] = act
    act_gated_ref[:, :hidden] = (act.astype(F32) * gate).astype(LOW)
    spare = act_gated_ref.shape[1] - hidden
    act_gated_ref[:, hidden:] = jnp.broadcast_to(gate.astype(LOW), (act.shape[0], spare))
    first = first_ref[:, :hidden]
    with_bias = jnp.max(first_ref[:, hidden:], axis=1, keepdims=True)
    grad_weight = jnp.sum(act.astype(F32) * first, axis=1, keepdims=True) + with_bias
    grad_act = first * gate
    swish_slope = sigmoid + GLU_SLOPE * swish * (1.0 - sigmoid)
    grad_gate = (grad_act * up_one * swish_slope * (1.0 - gate_tanh * gate_tanh)).astype(LOW)
    grad_up = (grad_act * swish * (1.0 - up_tanh * up_tanh)).astype(LOW)
    grad_gate_ref[...] = grad_gate
    grad_up_ref[...] = grad_up
    grad_far = dot(grad_gate, gate_ref[:, split:]) + dot(grad_up, up_ref[:, split:])
    grad_far_ref[:, :rest] = grad_far.astype(LOW)
    high = grad_weight.astype(LOW).astype(F32)
    lanes = lane_index(mine.shape)
    spread = jnp.where(lanes < experts, high, grad_weight - high) * mine
    grad_far_ref[:, rest:] = spread.astype(LOW)
    sums = jnp.concatenate(
        [
            jnp.sum(grad_gate.astype(F32), axis=0, keepdims=True),
            jnp.sum(grad_up.astype(F32), axis=0, keepdims=True),
        ],
        axis=0,
    )
    is_first = pl.program_id(0) == 0
    bias_sums_ref[...] = jnp.where(is_first, 0.0, bias_sums_ref[...]) + sums


def expert_step(place, near, far, first, gate, up, gate_bias, up_bias, mine, experts):
    count = far.shape[0]
    hidden, features = gate.shape
    block = count // 4
    rest = features - sum(one.shape[1] for one in near)
    gated = round_up(hidden + 8, 128)
    hidden_rows = jax.ShapeDtypeStruct((count, hidden), LOW)
    return pl.pallas_call(
        functools.partial(expert_kernel, experts, len(near)),
        grid=(count // block,),
        out_shape=(
            jax.ShapeDtypeStruct(far.shape, LOW),
            hidden_rows,
            jax.ShapeDtypeStruct((count, gated), LOW),
            hidden_rows,
            hidden_rows,
            jax.ShapeDtypeStruct((2, hidden), F32),
            jax.ShapeDtypeStruct((count, features), LOW),
        ),
        in_specs=[IN_SMEM]
        + [by_row(block, one.shape[1]) for one in near]
        + [
            by_row(block, far.shape[1]),
            by_row(block, first.shape[1]),
            held_block(hidden, features),
            held_block(hidden, features),
            whole_block(1, hidden),
            whole_block(1, hidden),
            whole_block(1, mine.shape[1]),
        ],
        out_specs=(
            by_row(block, far.shape[1]),
            by_row(block, hidden),
            by_row(block, gated),
            by_row(block, hidden),
            by_row(block, hidden),
            whole_block(2, hidden),
            by_row(block, features),
        ),
        scratch_shapes=[pltpu.VMEM((block, features - rest), LOW)],
        compiler_params=kernel_params(),
        cost_estimate=pl.CostEstimate(
            flops=8 * count * features * hidden,
            bytes_accessed=8 * count * features + 4 * features * hidden + 12 * count * hidden,
            transcendentals=3 * count * hidden,
        ),
        name="expert_step",
    )(place, *near, far, first, gate, up, gate_bias, up_bias, mine)


def grad_rows_kernel(grad_gate_ref, grad_up_ref, gate_ref, up_ref, out_ref):
    out = dot(grad_gate_ref[...], gate_ref[...]) + dot(grad_up_ref[...], up_ref[...])
    out_ref[...] = out.astype(LOW)


def grad_rows_near(grad_gate, grad_up, gate, up, split):
    count, hidden = grad_gate.shape
    block = count // 4
    return pl.pallas_call(
        grad_rows_kernel,
        grid=(count // block,),
        out_shape=jax.ShapeDtypeStruct((count, split), LOW),
        in_specs=[
            by_row(block, hidden),
            by_row(block, hidden),
            held_block(hidden, split),
            held_block(hidden, split),
        ],
        out_specs=by_row(block, split),
        compiler_params=kernel_params(),
        cost_estimate=SHORT,
        name="grad_rows",
    )(grad_gate, grad_up, gate, up)


def weight_grad_kernel(left_ref, right_ref, out_ref, *refs):
    bias_ref, turned_ref = refs if len(refs) == 2 else (None, refs[0])

    @pl.when(pl.program_id(0) == 0)
    def _():
        turned_ref[...] = left_ref[...].T

    hidden = out_ref.shape[0]
    product = dot(turned_ref[...], right_ref[...])
    out_ref[...] = product[:hidden]
    if bias_ref is not None:
        bias_ref[...] = product[hidden : hidden + 8]


def weight_grad(left, right, hidden):
    count, width = left.shape
    features = right.shape[1]
    block = round_up(-(-features // STEPS), 128)
    out_shape = [jax.ShapeDtypeStruct((hidden, features), F32)]
    out_specs = [by_column(hidden, block)]
    if width > hidden:
        out_shape.append(jax.ShapeDtypeStruct((8, features), F32))
        out_specs.append(by_column(8, block))
    return pl.pallas_call(
        weight_grad_kernel,
        grid=(STEPS,),
        out_shape=out_shape,
        in_specs=[whole_block(count, width), by_column(count, block)],
        out_specs=out_specs,
        scratch_shapes=[pltpu.VMEM((width, count), LOW)],
        compiler_params=kernel_params(),
        cost_estimate=SHORT,
        name="weight_grad",
    )(left, right)


def exchange(rows, parts):
    count, width = rows.shape
    moved = lax.all_to_all(
        rows.reshape(parts, count // parts, width),
        "expert",
        split_axis=0,
        concat_axis=0,
        tiled=True,
    )
    return moved.reshape(count, width)


def low_sum(halves):
    upper, upper_in, lower, lower_in = halves
    return (
        (upper.astype(F32) + upper_in.astype(F32)).astype(LOW),
        (lower.astype(F32) + lower_in.astype(F32)).astype(LOW),
    )


def tensor_sum(upper, lower, ring, middle=low_sum):
    near = [(i, i ^ 1) for i in range(ring)]
    far = [(i, ring - 1 - i) for i in range(ring)]
    upper_in = lax.ppermute(upper, "tensor", near)
    lower_in = lax.ppermute(lower, "tensor", far)
    upper, lower = middle((upper, upper_in, lower, lower_in))
    upper_in = lax.ppermute(upper, "tensor", far)
    lower_in = lax.ppermute(lower, "tensor", near)
    return upper, upper_in, lower, lower_in


def together(*values):
    return lax.optimization_barrier(values)


def ring_steps(ring):
    return [(i, (i + 1) % ring) for i in range(ring)], [(i, (i - 1) % ring) for i in range(ring)]


def tensor_chunks(own, ring):
    up, down = ring_steps(ring)
    half = own.shape[0] // 2
    before = lax.ppermute(own, "tensor", up)
    behind = lax.ppermute(own, "tensor", down)
    far_top = lax.ppermute(before[:half], "tensor", up)
    far_bottom = lax.ppermute(behind[half:], "tensor", down)
    across = jnp.concatenate([far_top, far_bottom], axis=0)
    return own, behind, across, before


def tensor_chunks_short(own, ring):
    across = [(i, (i + 2) % ring) for i in range(ring)]
    up, down = ring_steps(ring)
    before = lax.ppermute(own, "tensor", up)
    behind = lax.ppermute(own, "tensor", down)
    return own, behind, lax.ppermute(own, "tensor", across), before


def expert_sum(values, count, beside, work):
    masks = {32: (1, 2, 6, 8, 24)}.get(count) or [1 << i for i in range(count.bit_length() - 1)]
    for step, mask in enumerate(masks):
        if step == len(masks) // 2:
            values, beside = together(values, beside)
            made = work(beside)
        if step == len(masks) - 1:
            values, made = together(values, made)
        there = lax.ppermute(values, "expert", [(i, i ^ mask) for i in range(count)])
        values = (values.astype(F32) + there.astype(F32)).astype(values.dtype)
    return values, beside, made


def on_device(
    expert_axis,
    tensor_axis,
    block_input,
    out_cotangent,
    seq_lengths,
    route_ids,
    attn_gain,
    w_query,
    w_key,
    w_value,
    b_query,
    b_key,
    b_value,
    sink_logits,
    w_output,
    b_output,
    ffn_gain,
    w_router,
    b_router,
    w_gate,
    w_up,
    b_gate,
    b_up,
    w_down,
    b_down,
):
    tokens, features = block_input.shape
    heads = sink_logits.shape[0]
    experts = w_router.shape[1]
    capacity = 2 * tokens * route_ids.shape[1] // experts
    slots = experts * capacity
    shard = w_query.shape[0]
    shard_pad = round_up(shard + 1, 16)
    width = round_up(features + 2 * experts, 128)
    chunk = max(1, round(width / 128 / (2 * tensor_axis))) * 128
    split = chunk * tensor_axis
    rest = features - split
    block_width = round_up(-(-features // tensor_axis), 128)
    mine_expert = lax.axis_index("expert")
    mine_tensor = lax.axis_index("tensor")

    out_width = w_output.shape[0]
    packed = jnp.concatenate([w_output.T, w_query, w_key, w_value], axis=1)
    packed = jnp.pad(packed, ((0, shard_pad - shard), (0, 0)))
    weights = lax.all_gather(packed, "expert", axis=0, tiled=True)

    expert_ids = jnp.arange(experts, dtype=jnp.int32)
    named = jnp.any(route_ids[:, :, None] == expert_ids[None, None, :], axis=1)
    named_t = jnp.any(route_ids.T[:, None, :] == expert_ids[None, :, None], axis=0)
    token_ids = jnp.arange(tokens, dtype=jnp.int32)
    earlier = (token_ids[:, None] < token_ids[None, :]).astype(LOW)
    rank_t = dot(named_t.astype(LOW), earlier).astype(jnp.int32)
    place = (rank_t[:, None, :] == jnp.arange(capacity, dtype=jnp.int32)[None, :, None]) & named_t[
        :, None, :
    ]
    place = place.astype(LOW).reshape(slots, tokens)
    place_t = place.T


    def own_block(rows, size, ahead=0):
        start = (mine_tensor + ahead) % tensor_axis * size
        return lax.dynamic_slice(rows, (0, start), (tokens, size))

    cotangent_wide = jnp.pad(
        out_cotangent, ((0, 0), (0, block_width * tensor_axis - features))
    )
    cotangent_own = exchange(place_rows(place, own_block(cotangent_wide, block_width)), experts)
    up, down_ring = ring_steps(tensor_axis)
    cotangent_before = lax.ppermute(cotangent_own, "tensor", up)
    cotangent_behind = lax.ppermute(cotangent_own, "tensor", down_ring)
    cotangent_across = place_rows(place, own_block(cotangent_wide, block_width, 2))

    segment, position = layout(seq_lengths[0], tokens)
    cos, sin = rope_tables(position)
    allowed = (segment[:, None] == segment[None, :]) & (token_ids[None, :] <= token_ids[:, None])
    allowed = allowed.astype(F32)

    inputs = block_input.astype(F32)
    scale_one = lax.rsqrt(jnp.mean(inputs * inputs, axis=-1, keepdims=True) + EPSILON)
    unit_one = inputs * scale_one
    normed_low = (unit_one * attn_gain).astype(LOW)
    spread_low = jnp.pad(
        normed_low.reshape(tokens, expert_axis, shard), ((0, 0), (0, 0), (0, shard_pad - shard))
    )
    one_column = (jnp.arange(shard_pad) == shard).astype(LOW)
    normed_blocks = jnp.transpose(spread_low + one_column, (1, 2, 0))
    normed_blocks = normed_blocks.reshape(expert_axis * shard_pad, tokens)

    (
        weights,
        cotangent_across,
        cotangent_own,
        cotangent_before,
        cotangent_behind,
        normed_blocks,
    ) = together(
        weights,
        cotangent_across,
        cotangent_own,
        cotangent_before,
        cotangent_behind,
        normed_blocks,
    )
    cotangent_across = exchange(cotangent_across, experts)
    bias = jnp.concatenate([b_query, b_key, b_value])[None, :]
    spread_low = spread_low.reshape(tokens, expert_axis * shard_pad)
    attn_low, rotated, lse = attend_forward(
        sink_logits, spread_low, weights, bias, cos, sin, allowed
    )
    attn_all = lax.all_gather(attn_low, "expert", axis=0, tiled=True)
    attn_part = compact_product(attn_low, tokens, weights, out_width, shard, shard_pad, "attn_output")
    attn_sum = tensor_sum(*attn_part, tensor_axis)
    ring_place = mine_tensor.astype(jnp.int32).reshape(1)
    residual, gates, sent, rows_own = token_forward(
        ring_place,
        block_input,
        attn_sum,
        b_output[None, :],
        ffn_gain[None, :],
        w_router.T,
        b_router[None, :],
        named.astype(F32),
        place,
        width,
        chunk,
    )

    gate_t, up_t, down = w_gate[0].T, w_up[0].T, w_down[0]
    hidden = down.shape[0]
    bias_once = jnp.where(mine_tensor == 0, b_down, 0.0)
    rows_own, cotangent_across = together(rows_own, cotangent_across)
    cotangent_rows = (cotangent_own, cotangent_behind, cotangent_across, cotangent_before)
    first, cotangent_all = grad_hidden_product(ring_place, cotangent_rows, down, bias_once)
    rows_own = exchange(rows_own, experts)
    rows_far = place_rows(place, sent[:, split:])
    rows_own, rows_far, first = together(rows_own, rows_far, first)
    rows_near = tensor_chunks(rows_own, tensor_axis)
    rows_far = exchange(rows_far, experts)

    lane = jnp.arange(width - features)
    mine = ((lane % experts == mine_expert) & (lane < 2 * experts)).astype(F32)[None, :]
    rows_near, rows_far, attn_all = together(rows_near, rows_far, attn_all)
    grad_far, act, act_gated, grad_gate, grad_up, bias_sums, rows_all = expert_step(
        ring_place, rows_near, rows_far, first, gate_t, up_t, b_gate, b_up, mine, experts
    )
    back_far = exchange(grad_far, experts)
    grad_near = grad_rows_near(grad_gate, grad_up, gate_t, up_t, split)
    result = expert_result(act, down, bias_once, tensor_axis, block_width)
    result_own = lax.psum_scatter(result, "tensor", scatter_dimension=0, tiled=False)
    grad_near, back_far, grad_gate, grad_up, act_gated = together(
        grad_near, back_far, grad_gate, grad_up, act_gated
    )
    back_near = exchange(grad_near, experts)
    far_halves = combine_far(place_t, back_far, rest, experts)
    w_gate_grad = weight_grad(grad_gate, rows_all, hidden)[0]

    def middle(halves):
        nonlocal w_gate_grad, grad_up, act_gated
        *halves, w_gate_grad = together(*halves, w_gate_grad)
        upper, lower = middle_far(halves, rest, experts)
        upper, lower, grad_up, act_gated = together(upper, lower, grad_up, act_gated)
        return upper, lower

    far_sum = tensor_sum(*far_halves, tensor_axis, middle)
    w_up_grad = weight_grad(grad_up, rows_all, hidden)[0]
    w_down_grad, b_down_grad = weight_grad(act_gated, cotangent_all, hidden)
    back_near, w_up_grad, w_down_grad, b_down_grad, result_own, *far_sum = together(
        back_near, w_up_grad, w_down_grad, b_down_grad, result_own, *far_sum
    )
    w_gate_grad, w_up_grad = w_gate_grad.T[None], w_up_grad.T[None]
    w_down_grad, b_down_grad = w_down_grad[None], b_down_grad[0:1]
    b_gate_grad = bias_sums[0:1]
    b_up_grad = bias_sums[1:2]

    upper, lower = combine_near(place_t, back_near)
    upper, lower, result_own = together(upper, lower, result_own)
    near_sum = tensor_sum(upper, lower, tensor_axis)
    returned = exchange(result_own, experts)
    grad_resid, resid_spread, resid_blocks, router_block, vectors = token_backward(
        ring_place,
        near_sum,
        far_sum,
        gates,
        w_router.T,
        residual,
        out_cotangent,
        ffn_gain[None, :],
        shard,
        shard_pad,
        tensor_axis,
    )
    grad_qkv, sink_part = attend_backward(
        sink_logits, resid_spread, weights, rotated, lse, cos, sin, allowed
    )
    grad_qkv, returned = together(grad_qkv, returned)
    grad_qkv_all = lax.all_gather(grad_qkv, "expert", axis=0, tiled=True)
    upper, lower, attn_gain_part = compact_product(
        grad_qkv, tokens, weights, weights.shape[1], shard, shard_pad, "grad_normed", spread_low
    )
    grad_normed = tensor_sum(upper, lower, tensor_axis)
    normed_blocks = normed_blocks.reshape(expert_axis, shard_pad, tokens)
    blocks = jnp.concatenate([normed_blocks, resid_blocks], axis=1)
    blocks = exchange(blocks.reshape(expert_axis * 2 * shard_pad, tokens), expert_axis)
    blocks = blocks.reshape(expert_axis, 2 * shard_pad, tokens)

    sinks_row = jnp.pad(sink_part[:, :heads], ((0, 0), (0, tokens - heads)))
    small = pack_small(router_block, vectors, attn_gain_part, sinks_row)

    def output_product(blocks):
        return gathered_products(
            blocks, 1, attn_all, (out_width,), shard, shard_pad, False, "output_grad"
        )[0]

    small, blocks, w_output_grad = expert_sum(small, expert_axis, blocks, output_product)
    small, returned = together(small, returned)
    shared = experts + -(-features // block_width)
    widths = (w_query.shape[1], w_key.shape[1], w_value.shape[1])
    w_output_grad = w_output_grad.T
    qkv_grads = gathered_products(
        blocks, 0, grad_qkv_all, widths, shard, shard_pad, True, "qkv_grad"
    )
    query_grad, *qkv_grads = qkv_grads
    chunks = tensor_chunks_short(small[:shared], tensor_axis)
    router_grad, gain_grad, ffn_gain_grad, output_bias_grad, sink_grad, router_bias_grad = (
        unpack_small(ring_place, chunks, small[shared:], attn_gain[None, :], experts, heads)
    )

    input_grad = input_grad_rows(grad_normed, grad_resid, block_input, attn_gain[None, :]).T
    mixed = tensor_chunks_short(mix_results(place_t, gates, returned), tensor_axis)
    block_output = output_rows(ring_place, mixed, residual).T

    return (
        block_output,
        input_grad,
        gain_grad,
        query_grad,
        qkv_grads[0],
        qkv_grads[1],
        qkv_grads[2],
        qkv_grads[3],
        qkv_grads[4],
        sink_grad,
        w_output_grad,
        output_bias_grad,
        ffn_gain_grad,
        router_grad.T,
        router_bias_grad,
        w_gate_grad,
        w_up_grad,
        b_gate_grad,
        b_up_grad,
        w_down_grad,
        b_down_grad,
    )


def solution(mesh):
    in_specs = (
        P("expert", None),
        P("expert", None),
        P("expert", None),
        P("expert", None),
        P(),
        P("expert", "tensor"),
        P("expert", "tensor"),
        P("expert", "tensor"),
        P("tensor"),
        P("tensor"),
        P("tensor"),
        P("tensor"),
        P("tensor", "expert"),
        P(),
        P(),
        P(),
        P(),
        P("expert", None, "tensor"),
        P("expert", None, "tensor"),
        P("expert", "tensor"),
        P("expert", "tensor"),
        P("expert", "tensor", None),
        P("expert", None),
    )
    out_specs = (
        P("expert", None),
        P("expert", None),
        P(),
        P("expert", "tensor"),
        P("expert", "tensor"),
        P("expert", "tensor"),
        P("tensor"),
        P("tensor"),
        P("tensor"),
        P("tensor"),
        P("tensor", "expert"),
        P(),
        P(),
        P(),
        P(),
        P("expert", None, "tensor"),
        P("expert", None, "tensor"),
        P("expert", "tensor"),
        P("expert", "tensor"),
        P("expert", "tensor", None),
        P("expert", None),
    )
    body = functools.partial(on_device, mesh.shape["expert"], mesh.shape["tensor"])
    return jax.shard_map(body, mesh=mesh, in_specs=in_specs, out_specs=out_specs, check_vma=False)
```
